32 devices in a mesh: down: 16 (over z, y, core), cross: 2 (over x).
Axes of the slice: x: 2, y: 2, z: 4, core: 2. Of those that a mesh axis runs over, the one named last changes fastest.
Arguments:
- right_side: float32 [128, 64, 256], P('down', 'cross'), may hold values from -6 to 6
- kappa: float32 [128, 64, 256], P('down', 'cross'), may hold values from 0.3 to 3
- band_mask: int32 [128, 64, 256], P('down', 'cross'), may hold values 0 or 1
- tile_route: int32 [16, 8], P('down', 'cross'), may hold values from -1 to 3, as said below
Outputs:
- pressure: float32 [128, 64, 256], P('down', 'cross')
The draws below stay inside these ranges and needn't reach their ends.
Inputs may be any that keep to these rules, and one draw needn't show every extreme that they name: `tile_route`: within the tiles of one device each value other than -1 occurs at most once; in every draw some owner receives 2 tiles from every device of its cross-slope group.
All inputs are finite; a program needn't handle non-finite values. No bound on the sum of `band_mask` on one device may be relied on, other than what follows from the above.
Results may differ from the reference program's by a relative error of at most 0.0003.
Values sent between devices are 32-bit elements; how exact they have to be, the bound alone decides.
No kernel may reach another device: no remote copies, remote signals or barrier semaphores. Data moves between devices by JAX's collectives and lax.ppermute only.
A program may use at most 64 MiB of HBM per device.

```python
import math
import jax
import jax.numpy as jnp
from jax import lax

CX = 8
CY = 32
NZ = 256
TPD = 4
SLOTS = 2
BLOCK_SWEEPS = 4
COARSE_ITERS = 12
NX = 128
NY = 64
N_DOWN = 16
N_CROSS = 2


def draw_tile_route(key, part):
    key_cloud = jax.random.fold_in(key, 11)
    key_row = jax.random.fold_in(key, 12)
    key_base = jax.random.fold_in(key, 13)
    cloud = (jax.random.randint(key_cloud, (N_DOWN, N_CROSS, TPD), 0, 8) > 0).astype(jnp.int32)
    chosen = jax.random.randint(key_row, (), 0, N_DOWN)
    row_ids = jnp.arange(N_DOWN)[:, None, None]
    cloud = jnp.where(row_ids == chosen, 1, cloud)
    base = jax.random.randint(key_base, (N_DOWN, 1, 1), 0, N_CROSS)
    base = jnp.where(row_ids == chosen, N_CROSS - 2, base)
    ranks = jnp.cumsum(cloud, axis=2) - cloud
    owner = (base + ranks // SLOTS) % N_CROSS
    value = owner * SLOTS + ranks % SLOTS
    route = jnp.where(cloud == 1, value, -1)
    return route.reshape(N_DOWN, N_CROSS * TPD).astype(jnp.int32)


def with_ends(array, own_key, least, largest):
    longest = array.shape.index(max(array.shape))
    spots = []
    for shift in (0, 1):
        where = [jax.random.randint(jax.random.fold_in(own_key, axis), (), 0, length) for axis, length in enumerate(array.shape)]
        where[longest] = (where[longest] + shift) % array.shape[longest]
        spots.append(tuple(where))
    return array.at[spots[0]].set(least).at[spots[1]].set(largest)


def levels(own_key, shape, cuts, low, top_value):
    def one(axis_at, parts):
        draws = jax.random.uniform(jax.random.fold_in(jax.random.fold_in(own_key, 6), axis_at), (parts,), jnp.float32, low / len(cuts), top_value / len(cuts))
        return jnp.repeat(jnp.exp(draws), shape[axis_at] // parts).reshape((-1,) + (1,) * (len(shape) - axis_at - 1))

    level = one(*cuts[0])
    for cut in cuts[1:]:
        level = level * one(*cut)
    return level


def bell_draw(own_key, shape, scale, reach, pieces=(), held_as=jnp.bfloat16):
    result = jax.random.normal(own_key, shape, jnp.float32) * scale
    if len(pieces) > 0:
        result = levels(own_key, shape, pieces, -0.22, 0.18) * result
    return jnp.clip(result, min=-reach, max=reach).astype(held_as)


def setup_inputs(seed: int = 0) -> dict:
    key_of = jax.random.split(jax.random.key(seed), 5)
    return {
        "right_side": bell_draw(key_of[0], (NX, NY, NZ), 1.0, 6.0, ((0, 16), (1, 2)), jnp.float32),
        "kappa": jnp.clip(jnp.exp(math.log(3.0) - 2.3025851 * jax.random.uniform(key_of[1], (NX, NY, NZ), jnp.float32) ** levels(key_of[1], (NX, NY, NZ), ((0, 16), (1, 2)), -0.2, 0.2)), 0.3, 3.0),
        "band_mask": with_ends((jax.random.randint(key_of[2], (NX, NY, NZ), 0, 3) < 1).astype(jnp.int32), jax.random.fold_in(key_of[2], 1), 0, 1),
        "tile_route": draw_tile_route(jax.random.fold_in(key_of[4], 71), 0),
    }


OMEGA = 0.8
SNOW_FACTOR = 3.0


def pad_all(field):
    return jnp.pad(field, [(0, 0)] * (field.ndim - 3) + [(1, 1)] * 3)


def center(padded):
    return padded[..., 1:-1, 1:-1, 1:-1]


def neighbours(padded):
    return [padded[..., 2:, 1:-1, 1:-1], padded[..., :-2, 1:-1, 1:-1],
            padded[..., 1:-1, 2:, 1:-1], padded[..., 1:-1, :-2, 1:-1],
            padded[..., 1:-1, 1:-1, 2:], padded[..., 1:-1, 1:-1, :-2]]


def stencil(field_pad, conduct_pad, scale):
    middle = center(field_pad)
    kmiddle = center(conduct_pad)
    total = jnp.zeros_like(middle)
    for other, kother in zip(neighbours(field_pad), neighbours(conduct_pad)):
        total = total + scale * (kmiddle + kother) * (middle - other)
    return total


def diagonal(conduct_pad, scale):
    kmiddle = center(conduct_pad)
    total = jnp.zeros_like(kmiddle)
    for kother in neighbours(conduct_pad):
        total = total + scale * (kmiddle + kother)
    return total


def block_smooth(residual, conduct):
    conduct_pad = pad_all(conduct)
    diag = diagonal(conduct_pad, 2.0)
    safe = jnp.where(diag > 0, diag, 1.0)
    fix = OMEGA * residual / safe
    for sweep in range(BLOCK_SWEEPS - 1):
        fix = fix + OMEGA * (residual - stencil(pad_all(fix), conduct_pad, 2.0)) / safe
    return fix


def coarse_solve(totals, link_down, link_cross, outflow):
    link_up = jnp.concatenate([jnp.zeros_like(link_down[:1]), link_down[:-1]], 0)
    link_back = jnp.concatenate([jnp.zeros_like(link_cross[:, :1]), link_cross[:, :-1]], 1)

    def operate(field):
        padded = jnp.pad(field, 1)
        return (outflow * field - link_down * padded[2:, 1:-1] - link_up * padded[:-2, 1:-1]
                - link_cross * padded[1:-1, 2:] - link_back * padded[1:-1, :-2])

    def sweep(step, carry):
        answer, resid, search, norm_now = carry
        image = operate(search)
        alpha = norm_now / jnp.sum(search * image)
        answer = answer + alpha * search
        resid = resid - alpha * image
        norm_next = jnp.sum(resid * resid)
        search = resid + (norm_next / norm_now) * search
        return (answer, resid, search, norm_next)

    start = (jnp.zeros_like(totals), totals, totals, jnp.sum(totals * totals))
    return lax.fori_loop(0, COARSE_ITERS, sweep, start)[0]


def reference(right_side, kappa, band_mask, tile_route):
    conduct = kappa / (1.0 + SNOW_FACTOR * band_mask.astype(jnp.float32))
    conduct_pad = pad_all(conduct)
    diag_fine = diagonal(conduct_pad, 0.5)
    pressure = OMEGA * right_side / diag_fine
    pressure = pressure + OMEGA * (right_side - stencil(pad_all(pressure), conduct_pad, 0.5)) / diag_fine
    residual = right_side - stencil(pad_all(pressure), conduct_pad, 0.5)
    rows_all, cols_all, layers = residual.shape
    half_x, half_y, half_z = CX // 2, CY // 2, layers // 2
    tile_w = half_y // TPD
    coarse_res = residual.reshape(rows_all // 2, 2, cols_all // 2, 2, half_z, 2).sum(axis=(1, 3, 5))
    coarse_con = conduct.reshape(rows_all // 2, 2, cols_all // 2, 2, half_z, 2).sum(axis=(1, 3, 5)) * 0.125
    tiles_res = coarse_res.reshape(N_DOWN, half_x, N_CROSS * TPD, tile_w, half_z).transpose(0, 2, 1, 3, 4)
    tiles_con = coarse_con.reshape(N_DOWN, half_x, N_CROSS * TPD, tile_w, half_z).transpose(0, 2, 1, 3, 4)
    cloud = (tile_route >= 0).astype(jnp.float32)
    tile_fix = block_smooth(tiles_res, tiles_con) * cloud[:, :, None, None, None]
    tile_fix = tile_fix.transpose(0, 2, 1, 3, 4).reshape(rows_all // 2, cols_all // 2, half_z)
    coarse_pad = pad_all(coarse_con)
    faces_down = 2.0 * (coarse_pad[:-1, 1:-1, 1:-1] + coarse_pad[1:, 1:-1, 1:-1])
    link_rows = faces_down[::half_x].sum(axis=2).reshape(N_DOWN + 1, N_CROSS, half_y).sum(axis=2)
    faces_cross = 2.0 * (coarse_pad[1:-1, :-1, 1:-1] + coarse_pad[1:-1, 1:, 1:-1])
    link_cols = faces_cross[:, ::half_y].sum(axis=2).reshape(N_DOWN, half_x, N_CROSS + 1).sum(axis=1)
    vertical = 2.0 * (coarse_con[:, :, 0] + coarse_con[:, :, -1])
    vertical = vertical.reshape(N_DOWN, half_x, N_CROSS, half_y).sum(axis=(1, 3))
    outflow = link_rows[:-1] + link_rows[1:] + link_cols[:, :-1] + link_cols[:, 1:] + vertical
    totals = coarse_res.reshape(N_DOWN, half_x, N_CROSS, half_y, half_z).sum(axis=(1, 3, 4))
    brick_fix = coarse_solve(totals, link_rows[1:], link_cols[:, 1:], outflow)
    spread = jnp.repeat(jnp.repeat(brick_fix, half_x, 0), half_y, 1)
    correction = tile_fix + spread[:, :, None]
    fine_fix = jnp.broadcast_to(correction[:, None, :, None, :, None],
                                (rows_all // 2, 2, cols_all // 2, 2, half_z, 2)).reshape(rows_all, cols_all, layers)
    pressure = pressure + fine_fix
    for sweep in range(2):
        pressure = pressure + OMEGA * (right_side - stencil(pad_all(pressure), conduct_pad, 0.5)) / diag_fine
    return pressure
```

```python
import functools

import jax
import jax.numpy as jnp
from jax import lax
from jax.experimental import pallas as pl
from jax.experimental.pallas import tpu as pltpu
from jax.sharding import PartitionSpec as P

BLOCK_SWEEPS = 4
COARSE_ITERS = 12
OMEGA = 0.8
KEEP = 1.0 - OMEGA
SNOW_FACTOR = 3.0

DEPTH = 4
STRIP = 8
FLOAT = jnp.float32
VMEM_BYTES = 48 * 1024 * 1024


def partners(count, odd):
    found = []
    for i in range(count):
        j = ((i + 1) ^ 1) - 1 if odd else i ^ 1
        found.append(j if 0 <= j < count else i)
    return found


def pairings(count):
    return [k for k in (False, True) if any(j != i for i, j in enumerate(partners(count, k)))]


def pairs_of(count_down, count_cross, down_kind, cross_kind):
    rows = list(range(count_down)) if down_kind is None else partners(count_down, down_kind)
    cols = list(range(count_cross)) if cross_kind is None else partners(count_cross, cross_kind)
    return [
        (i * count_cross + j, rows[i] * count_cross + cols[j])
        for i in range(count_down)
        for j in range(count_cross)
    ]


def facing(index, count, kind):
    ahead = (index % 2 == 0) != kind
    return ahead, jnp.where(ahead, index < count - 1, index > 0)


def roll(x, amount, axis):
    return pltpu.roll(x, amount % x.shape[axis], axis)


def iota(shape, axis):
    return lax.broadcasted_iota(jnp.int32, shape, axis)


def gather(field, rows, wx, wx_at, wy, wz):
    low, here, high = rows
    value = field[here]
    total = wx[wx_at] * field[high] + wx[wx_at - 1] * field[low]
    total = total + wy * roll(value, -1, 0) + roll(wy * value, 1, 0)
    return total + wz * roll(value, -1, 1) + roll(wz * value, 1, 1)


def pack_kernel(nd, nc, rhs, kappa, mask, conduct, *messages):
    rows, cols, _ = rhs.shape
    messages = iter(messages)
    down, cross = lax.axis_index("down"), lax.axis_index("cross")
    for x in range(rows):
        conduct[x] = kappa[x] / (1.0 + SNOW_FACTOR * mask[x].astype(FLOAT))
    for kind in pairings(nd):
        ahead, _ = facing(down, nd, kind)
        out = next(messages)
        out[:DEPTH] = conduct[pl.ds(jnp.where(ahead, rows - DEPTH, 0), DEPTH)]
        out[DEPTH:] = rhs[pl.ds(jnp.where(ahead, rows - DEPTH + 1, 0), DEPTH - 1)]
    for cross_kind in pairings(nc):
        right, _ = facing(cross, nc, cross_kind)
        strip = pl.ds(pl.multiple_of(jnp.where(right, cols - STRIP, 0), STRIP), STRIP)
        out = next(messages)
        out[:rows] = conduct[:, strip, :]
        out[rows:] = rhs[:, strip, :]
        for kind in pairings(nd):
            ahead, _ = facing(down, nd, kind)
            out = next(messages)
            out[: DEPTH - 1] = conduct[pl.ds(jnp.where(ahead, rows - DEPTH + 1, 0), DEPTH - 1), strip, :]
            out[DEPTH - 1 :] = rhs[pl.ds(jnp.where(ahead, rows - DEPTH + 2, 0), DEPTH - 2), strip, :]


def pair_sum(x, axis):
    even = iota(x.shape, axis) % 2 == 0
    return x + jnp.where(even, roll(x, -1, axis), roll(x, 1, axis))


def total_of(x):
    return jnp.sum(jnp.sum(x, axis=0, keepdims=True), axis=1, keepdims=True)


def fold_lanes(x):
    return sum(x[:, i : i + 128] for i in range(0, x.shape[1], 128))


def main_kernel(nd, nc, rhs, conduct, route, *refs):
    rows, cols, layers = rhs.shape
    tiles = route.shape[1]
    tile_w = cols // tiles
    n_messages = len(pairings(nd)) + len(pairings(nc)) * (1 + len(pairings(nd)))
    messages = iter(refs[:n_messages])
    src, gain, wx, wy, wz, state, chunks, q, first, pres = refs[n_messages:]
    down, cross = lax.axis_index("down"), lax.axis_index("cross")
    wide = cols + 2 * STRIP
    own = slice(STRIP, STRIP + cols)

    zero_strip = jnp.zeros((q.shape[0], STRIP, layers), FLOAT)
    for ref in (q, src):
        ref[:, :STRIP, :] = zero_strip[: ref.shape[0]]
        ref[:, STRIP + cols :, :] = zero_strip[: ref.shape[0]]
    if len(pairings(nd)) < 2:
        q[...] = jnp.zeros(q.shape, FLOAT)
        src[...] = jnp.zeros(src.shape, FLOAT)
    q[DEPTH : DEPTH + rows, own, :] = conduct[...]
    src[DEPTH - 1 : DEPTH - 1 + rows, own, :] = rhs[...]
    for kind in pairings(nd):
        ahead, valid = facing(down, nd, kind)
        got = next(messages)
        q[pl.ds(jnp.where(ahead, DEPTH + rows, 0), DEPTH), own, :] = jnp.where(valid, got[:DEPTH], 0.0)
        src[pl.ds(jnp.where(ahead, DEPTH - 1 + rows, 0), DEPTH - 1), own, :] = jnp.where(
            valid, got[DEPTH:], 0.0
        )
    for cross_kind in pairings(nc):
        right, cross_valid = facing(cross, nc, cross_kind)
        strip = pl.ds(pl.multiple_of(jnp.where(right, STRIP + cols, 0), STRIP), STRIP)
        got = next(messages)
        q[DEPTH : DEPTH + rows, strip, :] = jnp.where(cross_valid, got[:rows], 0.0)
        src[DEPTH - 1 : DEPTH - 1 + rows, strip, :] = jnp.where(cross_valid, got[rows:], 0.0)
        for kind in pairings(nd):
            ahead, valid = facing(down, nd, kind)
            valid = valid & cross_valid
            got = next(messages)
            q[pl.ds(jnp.where(ahead, DEPTH + rows, 1), DEPTH - 1), strip, :] = jnp.where(
                valid, got[: DEPTH - 1], 0.0
            )
            src[pl.ds(jnp.where(ahead, DEPTH - 1 + rows, 1), DEPTH - 2), strip, :] = jnp.where(
                valid, got[DEPTH - 1 :], 0.0
            )

    lane = iota((wide, layers), 1)
    col = iota((wide, layers), 0)
    col_ok = (col >= jnp.where(cross > 0, 0, STRIP)) & (
        col < jnp.where(cross < nc - 1, wide, STRIP + cols)
    )

    for i in range(rows + 2 * (DEPTH - 1)):
        x = i - (DEPTH - 1)
        here = q[i + 1]
        ahead = q[i + 2]
        above = jnp.where(lane == layers - 1, 0.0, roll(here, -1, 1))
        below = jnp.where(lane == 0, 0.0, roll(here, 1, 1))
        right = roll(here, -1, 0)
        doubled = 6.0 * here + (q[i] + ahead) + (right + roll(here, 1, 0)) + (above + below)
        ok = col_ok & (doubled > 0.0)
        if x < 0:
            ok = ok & (down > 0)
        if x >= rows:
            ok = ok & (down < nd - 1)
        gain_here = jnp.where(ok, (2.0 * OMEGA) / doubled, 0.0)
        gain[i] = gain_here
        first[i] = gain_here * src[i]
        if i < wx.shape[0]:
            wx[i] = 0.5 * (here + ahead)
        if -2 <= x < rows + 2:
            wy[x + 2] = 0.5 * (here + right)
            wz[x + 2] = jnp.where(lane == layers - 1, 0.0, 0.5 * (here + above))

    for i in range(rows + 4):
        spread = gather(first, (i, i + 1, i + 2), wx, i + 1, wy[i], wz[i])
        pres[i] = KEEP * first[i + 1] + gain[i + 1] * (src[i + 1] + spread)

    tile_shape = (tiles, tile_w, layers)
    res_sum = jnp.zeros((cols, layers), FLOAT)
    coarse_res, coarse_con = [], []
    for k in range(rows // 2):
        res_pair = None
        for x in (2 * k, 2 * k + 1):
            i = x + 2
            value = pres[i]
            here = q[x + DEPTH]
            spread = gather(pres, (i - 1, i, i + 1), wx, i + 1, wy[i], wz[i])
            diag = wx[i + 1] + wx[i] + wy[i] + roll(wy[i], 1, 0)
            vertical = wz[i] + roll(wz[i], 1, 1)
            vertical = vertical + jnp.where((lane == 0) | (lane == layers - 1), 0.5 * here, 0.0)
            res = (src[x + DEPTH - 1] - (diag + vertical) * value + spread)[own]
            res_pair = res if res_pair is None else res_pair + res
        res_sum = res_sum + res_pair
        con_pair = q[2 * k + DEPTH, own, :] + q[2 * k + 1 + DEPTH, own, :]
        coarse_res.append(pair_sum(pair_sum(res_pair, 1), 0).reshape(tile_shape))
        coarse_con.append((0.125 * pair_sum(pair_sum(con_pair, 1), 0)).reshape(tile_shape))

    strip_col = iota((STRIP, layers), 0)
    own_lane = iota((cols, layers), 1)

    def rows_sum(start):
        return total_of(sum(q[DEPTH + start + r, own, :] for r in range(4)))

    def cols_sum(start):
        acc = jnp.zeros((STRIP, layers), FLOAT)
        for x in range(rows):
            left = q[x + DEPTH, start - STRIP : start, :]
            right = q[x + DEPTH, start : start + STRIP, :]
            acc = acc + jnp.where(strip_col >= STRIP - 2, left, 0.0) + jnp.where(strip_col < 2, right, 0.0)
        return total_of(acc)

    plane = sum(q[x + DEPTH, own, :] for x in range(rows))
    ends = total_of(jnp.where((own_lane < 2) | (own_lane >= layers - 2), plane, 0.0))
    link_down = 0.25 * rows_sum(rows - 2)
    link_up = 0.25 * rows_sum(-2)
    link_cross = 0.25 * cols_sum(STRIP + cols)
    link_back = 0.25 * cols_sum(STRIP)
    outflow = link_down + link_up + link_cross + link_back + 0.25 * ends
    total = total_of(res_sum)
    line = iota((8, 128), 0)
    summary = jnp.where(line == 0, total, jnp.where(line == 1, link_down, jnp.where(line == 2, link_cross, outflow)))

    tile_col = iota(tile_shape, 1)
    tile_lane = iota(tile_shape, 2)
    half_rows = len(coarse_con)
    link_x = [2.0 * (coarse_con[k] + coarse_con[k + 1]) for k in range(half_rows - 1)]
    link_y, link_z, tile_gain = [], [], []
    for k in range(half_rows):
        con = coarse_con[k]
        y_high = jnp.where(tile_col < tile_w - 2, roll(con, -2, 1), 0.0)
        y_low = jnp.where(tile_col >= 2, roll(con, 2, 1), 0.0)
        z_high = jnp.where(tile_lane < layers - 2, roll(con, -2, 2), 0.0)
        z_low = jnp.where(tile_lane >= 2, roll(con, 2, 2), 0.0)
        diag = 6.0 * con + (y_high + y_low) + (z_high + z_low)
        if k > 0:
            diag = diag + coarse_con[k - 1]
        if k < half_rows - 1:
            diag = diag + coarse_con[k + 1]
        diag = 2.0 * diag
        tile_gain.append(OMEGA / jnp.where(diag > 0.0, diag, 1.0))
        link_y.append(jnp.where(tile_col < tile_w - 2, 2.0 * (con + y_high), 0.0))
        link_z.append(jnp.where(tile_lane < layers - 2, 2.0 * (con + z_high), 0.0))
    fix = [tile_gain[k] * coarse_res[k] for k in range(half_rows)]
    for _ in range(BLOCK_SWEEPS - 1):
        updated = []
        for k in range(half_rows):
            value = fix[k]
            acc = coarse_res[k] + link_y[k] * roll(value, -2, 1) + roll(link_y[k] * value, 2, 1)
            acc = acc + link_z[k] * roll(value, -2, 2) + roll(link_z[k] * value, 2, 2)
            if k > 0:
                acc = acc + link_x[k - 1] * fix[k - 1]
            if k < half_rows - 1:
                acc = acc + link_x[k] * fix[k + 1]
            updated.append(KEEP * value + tile_gain[k] * acc)
        fix = updated
    touched = [jnp.where(route[0, t] >= 0, 1.0, 0.0) for t in range(tiles)]
    fix = [jnp.stack([f[t] * touched[t] for t in range(tiles)]) for f in fix]

    for i in range(rows + 4):
        if 2 <= i < rows + 2:
            state[i, :STRIP, :] = pres[i, :STRIP, :]
            state[i, own, :] = pres[i, own, :] + fix[(i - 2) // 2].reshape(cols, layers)
            state[i, STRIP + cols :, :] = pres[i, STRIP + cols :, :]
        else:
            state[i] = pres[i]

    half = layers // 2
    body_rows = 2 * tile_w
    count = nd * nc
    zero_chunk = jnp.zeros((body_rows, 128), FLOAT)

    def fill(b, carry):
        chunks[b, :body_rows, :] = zero_chunk
        chunks[b, body_rows:, :] = summary
        return carry

    lax.fori_loop(0, count, fill, 0)
    parity_col = iota((tile_w, layers), 0) % 2
    parity_lane = iota((tile_w, layers), 1) % 2

    def put(index, packed):
        chunks[index, :tile_w, :] = packed[:, :half]
        chunks[index, tile_w:body_rows, :] = packed[:, half:]

    def pack_row(f):
        top = jnp.where(parity_lane == 0, f[0], f[1])
        bottom = jnp.where(parity_lane == 0, f[2], f[3])
        return jnp.where(parity_col == 0, top, bottom)

    pair_col = iota((tile_w, layers), 0) // 2

    def pack_edge(tile, column):
        out = jnp.broadcast_to(fix[0][tile, column : column + 1], (tile_w, layers))
        for k in range(1, half_rows):
            line = jnp.broadcast_to(fix[k][tile, column : column + 1], (tile_w, layers))
            out = jnp.where(pair_col == k, line, out)
        return out

    me = down * nc + cross
    edges = {-1: (0, 0), 1: (tiles - 1, tile_w - 1)}
    for dx in (-1, 0, 1):
        for dy in (-1, 0, 1):
            if (dx, dy) == (0, 0):
                continue
            there = jnp.bool_(True)
            if dx:
                there = there & ((down > 0) if dx < 0 else (down < nd - 1))
            if dy:
                there = there & ((cross > 0) if dy < 0 else (cross < nc - 1))

            @pl.when(there)
            def _(dx=dx, dy=dy):
                k = 0 if dx < 0 else half_rows - 1
                if dy == 0:
                    packed = pack_row(fix[k])
                elif dx == 0:
                    packed = pack_edge(*edges[dy])
                else:
                    tile, column = edges[dy]
                    packed = jnp.broadcast_to(fix[k][tile, column : column + 1], (tile_w, layers))
                put(me + dx * nc + dy, packed)


def coarse_solve(totals, outflow, link_down, link_up, link_cross):
    nc = len(totals)

    def operate(v):
        out = []
        for c in range(nc):
            image = outflow[c] * v[c] - link_down[c] * roll(v[c], -1, 0) - link_up[c] * roll(v[c], 1, 0)
            if c < nc - 1:
                image = image - link_cross[c] * v[c + 1]
            if c > 0:
                image = image - link_cross[c - 1] * v[c - 1]
            out.append(image)
        return out

    def dot(a, b):
        return jnp.sum(sum(x * y for x, y in zip(a, b)), axis=0, keepdims=True)

    answer = [jnp.zeros_like(t) for t in totals]
    resid = search = totals
    norm = dot(totals, totals)
    for step in range(COARSE_ITERS):
        image = operate(search)
        alpha = norm / dot(search, image)
        answer = [a + alpha * s for a, s in zip(answer, search)]
        if step == COARSE_ITERS - 1:
            break
        resid = [r - alpha * m for r, m in zip(resid, image)]
        norm_next = dot(resid, resid)
        beta = norm_next / norm
        search = [r + beta * s for r, s in zip(resid, search)]
        norm = norm_next
    return answer


def last_kernel(nd, nc, tiles, got, src, gain, wx, wy, wz, state, out, bricks, pres, third):
    rows, cols, layers = out.shape
    tile_w = cols // tiles
    body_rows = 2 * tile_w
    down, cross = lax.axis_index("down"), lax.axis_index("cross")
    own = slice(STRIP, STRIP + cols)

    last = iota((nd, 128), 0) == nd - 1
    totals = [got[:, c, body_rows, :] for c in range(nc)]
    link_down = [jnp.where(last, 0.0, got[:, c, body_rows + 1, :]) for c in range(nc)]
    link_up = [roll(link, 1, 0) for link in link_down]
    link_cross = [got[:, c, body_rows + 2, :] for c in range(nc)]
    outflow = [got[:, c, body_rows + 3, :] for c in range(nc)]
    answer = coarse_solve(totals, outflow, link_down, link_up, link_cross)
    for c in range(nc):
        bricks[c] = answer[c]

    lanes = iota((tile_w, layers), 1) % 2
    sublanes = iota((tile_w, layers), 0) % 2

    def neighbour(dx, dy):
        there = jnp.bool_(True)
        if dx:
            there = there & ((down > 0) if dx < 0 else (down < nd - 1))
        if dy:
            there = there & ((cross > 0) if dy < 0 else (cross < nc - 1))
        row = jnp.clip(down + dx, 0, nd - 1)
        col = jnp.clip(cross + dy, 0, nc - 1)
        line = bricks[col, pl.ds(row, 1), :]
        brick = jnp.concatenate([line] * (layers // 128), axis=1)
        packed = jnp.concatenate(
            [got[row, col, :tile_w, :], got[row, col, tile_w:body_rows, :]], axis=1
        )
        return there, brick, packed

    def unpack_row(packed):
        parts = []
        for sub in (0, 1):
            tall = jnp.where(sublanes == sub, packed, roll(packed, 1 if sub == 0 else -1, 0))
            for lan in (0, 1):
                parts.append(jnp.where(lanes == lan, tall, roll(tall, 1 if lan == 0 else -1, 1)))
        return jnp.concatenate(parts, axis=0)

    mine = jnp.concatenate([bricks[cross, pl.ds(down, 1), :]] * (layers // 128), axis=1)
    for i in range(2, rows + 2):
        pres[i, own, :] = state[i, own, :] + mine
    for dx, at in ((-1, 0), (1, rows + 2)):
        there, brick, packed = neighbour(dx, 0)
        extra = jnp.where(there, unpack_row(packed) + brick, 0.0)
        for i in (at, at + 1):
            pres[i, own, :] = state[i, own, :] + extra
    for dy, start in ((-1, 0), (1, STRIP + cols)):
        strip = slice(start, start + STRIP)
        there, brick, packed = neighbour(0, dy)
        for k in range(rows // 2):
            line = packed[2 * k : 2 * k + 1] + brick
            extra = jnp.where(there, jnp.broadcast_to(line, (STRIP, layers)), 0.0)
            for i in (2 * k + 2, 2 * k + 3):
                pres[i, strip, :] = state[i, strip, :] + extra
        for dx, at in ((-1, 0), (1, rows + 2)):
            there, brick, packed = neighbour(dx, dy)
            extra = jnp.where(there, jnp.broadcast_to(packed[0:1] + brick, (STRIP, layers)), 0.0)
            for i in (at, at + 1):
                pres[i, strip, :] = state[i, strip, :] + extra

    for i in range(rows + 2):
        spread = gather(pres, (i, i + 1, i + 2), wx, i + 2, wy[i + 1], wz[i + 1])
        third[i] = KEEP * pres[i + 1] + gain[i + 2] * (src[i + 2] + spread)
    for x in range(rows):
        spread = gather(third, (x, x + 1, x + 2), wx, x + 3, wy[x + 2], wz[x + 2])
        new = KEEP * third[x + 1] + gain[x + 3] * (src[x + 3] + spread)
        out[x] = new[own]


def whole(shape):
    return jax.ShapeDtypeStruct(shape, FLOAT)


def call(kernel, out_shape, n_in, scratch=(), smem=()):
    return pl.pallas_call(
        kernel,
        out_shape=out_shape,
        in_specs=[
            pl.BlockSpec(memory_space=pltpu.SMEM if i in smem else pltpu.VMEM) for i in range(n_in)
        ],
        out_specs=jax.tree.map(lambda _: pl.BlockSpec(memory_space=pltpu.VMEM), out_shape),
        scratch_shapes=list(scratch),
        compiler_params=pltpu.CompilerParams(vmem_limit_bytes=VMEM_BYTES),
    )


def body(nd, nc, right_side, kappa, band_mask, tile_route):
    rows, cols, layers = right_side.shape
    tiles = tile_route.shape[1]
    axes = ("down", "cross")
    wide = cols + 2 * STRIP

    shapes, perms = [], []
    for kind in pairings(nd):
        shapes.append((2 * DEPTH - 1, cols, layers))
        perms.append(pairs_of(nd, nc, kind, None))
    for cross_kind in pairings(nc):
        shapes.append((2 * rows, STRIP, layers))
        perms.append(pairs_of(nd, nc, None, cross_kind))
        for kind in pairings(nd):
            shapes.append((2 * DEPTH - 3, STRIP, layers))
            perms.append(pairs_of(nd, nc, kind, cross_kind))
    conduct, *messages = call(
        functools.partial(pack_kernel, nd, nc),
        [whole((rows, cols, layers))] + [whole(s) for s in shapes],
        3,
    )(right_side, kappa, band_mask)
    received = [lax.ppermute(m, axes, p) for m, p in zip(messages, perms)]

    body_rows = 2 * (cols // tiles)
    heights = (rows + 6, rows + 6, rows + 5, rows + 4, rows + 4, rows + 4)
    *kept, chunks = call(
        functools.partial(main_kernel, nd, nc),
        [whole((h, wide, layers)) for h in heights] + [whole((nd * nc, body_rows + 8, 128))],
        3 + len(received),
        scratch=[
            pltpu.VMEM((h, wide, layers), FLOAT) for h in (rows + 8, rows + 6, rows + 4)
        ],
        smem=(2,),
    )(right_side, conduct, tile_route, *received)
    arrived = lax.all_to_all(chunks, axes, 0, 0, tiled=True).reshape(nd, nc, body_rows + 8, 128)
    return call(
        functools.partial(last_kernel, nd, nc, tiles),
        whole((rows, cols, layers)),
        1 + len(kept),
        scratch=[
            pltpu.VMEM((nc, nd, 128), FLOAT),
            pltpu.VMEM((rows + 4, wide, layers), FLOAT),
            pltpu.VMEM((rows + 2, wide, layers), FLOAT),
        ],
    )(arrived, *kept)


def solution(mesh):
    return jax.shard_map(
        functools.partial(body, mesh.shape["down"], mesh.shape["cross"]),
        mesh=mesh,
        in_specs=(
            P("down", "cross", None),
            P("down", "cross", None),
            P("down", "cross", None),
            P("down", "cross"),
        ),
        out_specs=P("down", "cross", None),
        check_vma=False,
    )
```

```python
import functools

import jax
import jax.numpy as jnp
from jax import lax
from jax.experimental import pallas as pl
from jax.experimental.pallas import tpu as pltpu
from jax.sharding import PartitionSpec as P

BLOCK_SWEEPS = 4
COARSE_ITERS = 12
OMEGA = 0.8
KEEP = 1.0 - OMEGA
SNOW_FACTOR = 3.0

DEPTH = 4
CORNER = 2 * DEPTH - 3
STRIP = 8
LANES = 128
HALF = 8
CHUNK = HALF + 1
FLOAT = jnp.float32
VMEM_BYTES = 48 * 1024 * 1024


def partners(count, odd):
    found = []
    for i in range(count):
        j = ((i + 1) ^ 1) - 1 if odd else i ^ 1
        found.append(j if 0 <= j < count else i)
    return found


def pairings(count):
    return [k for k in (False, True) if any(j != i for i, j in enumerate(partners(count, k)))]


def pairs_of(count_down, count_cross, down_kind, cross_kind):
    rows = list(range(count_down)) if down_kind is None else partners(count_down, down_kind)
    cols = list(range(count_cross)) if cross_kind is None else partners(count_cross, cross_kind)
    return [
        (i * count_cross + j, rows[i] * count_cross + cols[j])
        for i in range(count_down)
        for j in range(count_cross)
    ]


def facing(index, count, kind):
    ahead = (index % 2 == 0) != kind
    return ahead, jnp.where(ahead, index < count - 1, index > 0)


def beside(index, count, step):
    return (index + step >= 0) & (index + step < count)


def roll(x, amount, axis):
    return pltpu.roll(x, amount % x.shape[axis], axis)


def iota(shape, axis):
    return lax.broadcasted_iota(jnp.int32, shape, axis)


def gather(field, here, wx, wx_at, wy, wz):
    value = field[here]
    total = wx[wx_at] * field[here + 1] + wx[wx_at - 1] * field[here - 1]
    total = total + wy * roll(value, -1, 0) + roll(wy * value, 1, 0)
    return total + wz * roll(value, -1, 1) + roll(wz * value, 1, 1)


def edge_rows(ahead, rows, depth):
    return pl.ds(jnp.where(ahead, rows - depth, 0), depth)


def edge_strip(right, cols):
    return pl.ds(pl.multiple_of(jnp.where(right, cols - STRIP, 0), STRIP), STRIP)


def pack_kernel(nd, nc, rhs_hbm, kappa_hbm, mask_hbm, conduct, *refs):
    *messages, rhs, kappa, mask, sems = refs
    rows, cols, _ = rhs.shape
    messages = iter(messages)
    down, cross = lax.axis_index("down"), lax.axis_index("cross")
    copies = [
        pltpu.make_async_copy(src, dst, sems.at[i])
        for i, (src, dst) in enumerate(((kappa_hbm, kappa), (mask_hbm, mask), (rhs_hbm, rhs)))
    ]
    for copy in copies:
        copy.start()
    copies[0].wait()
    copies[1].wait()
    for x in range(rows):
        conduct[x] = kappa[x] / (1.0 + SNOW_FACTOR * mask[x].astype(FLOAT))
    copies[2].wait()
    for kind in pairings(nd):
        ahead, _ = facing(down, nd, kind)
        out = next(messages)
        out[:DEPTH] = conduct[edge_rows(ahead, rows, DEPTH)]
        out[DEPTH:] = rhs[edge_rows(ahead, rows, DEPTH - 1)]
        if kind:
            for cross_kind in pairings(nc):
                right, _ = facing(cross, nc, cross_kind)
                strip = edge_strip(right, cols)
                out = next(messages)
                out[: DEPTH - 1] = conduct[edge_rows(ahead, rows, DEPTH - 1), strip, :]
                out[DEPTH - 1 :] = rhs[edge_rows(ahead, rows, DEPTH - 2), strip, :]
    for cross_kind in pairings(nc):
        right, _ = facing(cross, nc, cross_kind)
        strip = edge_strip(right, cols)
        out = next(messages)
        out[:rows] = conduct[:, strip, :]
        out[rows:] = rhs[:, strip, :]


def strip_kernel(nd, nc, even, *refs):
    cols = even.shape[1]
    count = len(pairings(nc))
    ahead, _ = facing(lax.axis_index("down"), nd, False)
    for cross_kind, own, out in zip(pairings(nc), refs[:count], refs[count:]):
        right, _ = facing(lax.axis_index("cross"), nc, cross_kind)
        strip = edge_strip(right, cols)
        rows = own.shape[0] // 2
        out[: 2 * rows] = own[...]
        out[2 * rows : 2 * rows + DEPTH - 1] = even[pl.ds(jnp.where(ahead, 0, 1), DEPTH - 1), strip, :]
        out[2 * rows + DEPTH - 1 :] = even[
            pl.ds(jnp.where(ahead, DEPTH, DEPTH + 1), DEPTH - 2), strip, :
        ]


def fold(x):
    x = sum(x[:, i : i + LANES] for i in range(0, x.shape[1], LANES))
    return jnp.sum(x, axis=0, keepdims=True)


def swap_pairs(x, axis):
    return jnp.where(iota(x.shape, axis) % 2 == 0, roll(x, -1, axis), roll(x, 1, axis))


def pack_pairs(a, b, axis):
    even = iota(a.shape, axis) % 2 == 0
    return jnp.where(even, a, b) + swap_pairs(jnp.where(even, b, a), axis)


def unpack_pairs(x, axis):
    even = iota(x.shape, axis) % 2 == 0
    return jnp.where(even, x, roll(x, 1, axis)), jnp.where(even, roll(x, -1, axis), x)


def main_kernel(nd, nc, rhs, conduct, route, *refs):
    rows, cols, layers = rhs.shape
    tiles = route.shape[1]
    tile_w = cols // tiles
    n_down, n_cross = len(pairings(nd)), len(pairings(nc))
    n_messages = n_down + n_cross * n_down
    vertical = refs[:n_down]
    corners = refs[n_down : n_down + n_cross * (n_down - 1)]
    strips = refs[n_down + n_cross * (n_down - 1) : n_messages]
    src, gain, wx, wy, wz, state, swapped, chunks, q, first, pres, diag = refs[n_messages:]
    down, cross = lax.axis_index("down"), lax.axis_index("cross")
    wide = cols + STRIP
    own, halo = slice(0, cols), slice(cols, wide)

    if n_down < 2:
        q[...] = jnp.zeros(q.shape, FLOAT)
        src[...] = jnp.zeros(src.shape, FLOAT)
    else:
        for ref in (q, src):
            for i in (0, ref.shape[0] - 1):
                ref[i, halo, :] = jnp.zeros((STRIP, layers), FLOAT)
    q[DEPTH : DEPTH + rows, own, :] = conduct[...]
    src[DEPTH - 1 : DEPTH - 1 + rows, own, :] = rhs[...]
    halo_col = iota((STRIP, layers), 0)
    sides = []
    for cross_kind in pairings(nc):
        right, valid = facing(cross, nc, cross_kind)
        start = jnp.where(right, 0, STRIP // 2)
        stop = jnp.where(valid, start + STRIP // 2, 0)
        sides.append((halo_col >= start) & (halo_col < stop))

    def merged(parts, valid=None):
        total = jnp.zeros((STRIP, layers), FLOAT)
        for side, part in zip(sides, parts):
            total = jnp.where(side if valid is None else side & valid, part, total)
        return total

    for x in range(rows):
        q[DEPTH + x, halo, :] = merged([s[x] for s in strips])
        src[DEPTH - 1 + x, halo, :] = merged([s[rows + x] for s in strips])
    for at, kind in enumerate(pairings(nd)):
        ahead, valid = facing(down, nd, kind)
        got = vertical[at]
        q_at = jnp.where(ahead, DEPTH + rows, 0)
        src_at = jnp.where(ahead, DEPTH - 1 + rows, 0)
        q[pl.ds(q_at, DEPTH), own, :] = jnp.where(valid, got[:DEPTH], 0.0)
        src[pl.ds(src_at, DEPTH - 1), own, :] = jnp.where(valid, got[DEPTH:], 0.0)
        nearer = jnp.where(ahead, 0, 1)
        parts, start = (corners, 0) if kind else (strips, 2 * rows)
        for i in range(DEPTH - 1):
            q[q_at + nearer + i, halo, :] = merged([p[start + i] for p in parts], valid)
        for i in range(DEPTH - 2):
            src[src_at + nearer + i, halo, :] = merged([p[start + DEPTH - 1 + i] for p in parts], valid)

    lane = iota((wide, layers), 1)
    col = iota((wide, layers), 0)
    last_lane = lane == layers - 1
    middle_col = cols + STRIP // 2
    col_ok = (col < jnp.where(cross < nc - 1, middle_col, cols)) | (
        col >= jnp.where(cross > 0, middle_col, wide)
    )

    for i in range(rows + 2 * (DEPTH - 1)):
        x = i - (DEPTH - 1)
        here = q[i + 1]
        ahead = q[i + 2]
        above = jnp.where(last_lane, 0.0, roll(here, -1, 1))
        below = jnp.where(lane == 0, 0.0, roll(here, 1, 1))
        right = roll(here, -1, 0)
        doubled = 6.0 * here + (q[i] + ahead) + (right + roll(here, 1, 0)) + (above + below)
        ok = col_ok & (doubled > 0.0)
        if x < 0:
            ok = ok & (down > 0)
        if x >= rows:
            ok = ok & (down < nd - 1)
        gain_here = jnp.where(ok, (2.0 * OMEGA) / doubled, 0.0)
        gain[i] = gain_here
        first[i] = gain_here * src[i]
        if 0 <= x < rows:
            diag[x] = 0.5 * doubled
        if i < wx.shape[0]:
            wx[i] = 0.5 * (here + ahead)
        if -2 <= x < rows + 2:
            wy[x + 2] = 0.5 * (here + right)
            wz[x + 2] = jnp.where(last_lane, 0.0, 0.5 * (here + above))

    for i in range(rows + 4):
        spread = gather(first, i + 1, wx, i + 1, wy[i], wz[i])
        pres[i] = KEEP * first[i + 1] + gain[i + 1] * (src[i + 1] + spread)

    res_rows, con_rows = [], []
    for k in range(rows // 2):
        pair = None
        for x in (2 * k, 2 * k + 1):
            i = x + 2
            spread = gather(pres, i, wx, i + 1, wy[i], wz[i])
            res = (src[x + DEPTH - 1] - diag[x] * pres[i] + spread)[own]
            pair = res if pair is None else pair + res
        res_rows.append(pair)
        con_rows.append(0.125 * (q[2 * k + DEPTH, own, :] + q[2 * k + 1 + DEPTH, own, :]))

    strip_col = iota((STRIP, layers), 0)
    plane = sum(q[x + DEPTH, own, :] for x in range(rows))
    beyond = sum(q[x + DEPTH, halo, :] for x in range(rows))
    own_lane = iota((cols, layers), 1)
    low, high = strip_col < 2, strip_col >= STRIP - 2
    ends = fold(jnp.where((own_lane < 2) | (own_lane >= layers - 2), plane, 0.0))
    link_back = fold(jnp.where(low, plane[:STRIP], 0.0) + jnp.where(high, beyond, 0.0))
    link_cross = fold(jnp.where(high, plane[cols - STRIP :], 0.0) + jnp.where(low, beyond, 0.0))
    link_up = fold(sum(q[DEPTH + x, own, :] for x in range(-2, 2)))
    link_down = fold(sum(q[DEPTH + x, own, :] for x in range(rows - 2, rows + 2)))
    outflow = link_down + link_up + link_cross + link_back + ends
    sums = jnp.concatenate([fold(sum(res_rows)), 0.25 * link_down, 0.25 * link_cross, 0.25 * outflow])
    sums = jnp.sum(sums, axis=1, keepdims=True)
    line = iota((1, LANES), 1)
    summary = jnp.where(
        line == 0, sums[0:1], jnp.where(line == 1, sums[1:2], jnp.where(line == 2, sums[2:3], sums[3:4]))
    )

    packs = rows // 4
    couples = tiles // 2
    shape = (couples, tile_w, layers)

    def coarse(lists):
        by_row = []
        for x in lists:
            t = x.reshape(couples, 2, tile_w, layers)
            by_row.append(pack_pairs(t[:, 0], t[:, 1], 2))
        return [pack_pairs(by_row[k], by_row[k + packs], 1) for k in range(packs)]

    res, con = coarse(res_rows), coarse(con_rows)
    tile_col, tile_lane = iota(shape, 1), iota(shape, 2)
    even_col = tile_col % 2 == 0
    y_end, y_start = tile_col >= tile_w - 2, tile_col < 2
    z_end, z_start = tile_lane >= layers - 2, tile_lane < 2
    link_x = [2.0 * (con[k] + con[k + 1]) for k in range(packs - 1)]
    middle = 2.0 * (con[packs - 1] + roll(con[0], -1, 1))
    middle_low = jnp.where(even_col, middle, 0.0)
    middle_high = jnp.where(even_col, 0.0, roll(middle, 1, 1))
    link_y, link_z, tile_gain = [], [], []
    for k in range(packs):
        c = con[k]
        y_high = jnp.where(y_end, 0.0, roll(c, -2, 1))
        z_high = jnp.where(z_end, 0.0, roll(c, -2, 2))
        y_low = jnp.where(y_start, 0.0, roll(c, 2, 1))
        z_low = jnp.where(z_start, 0.0, roll(c, 2, 2))
        total = 6.0 * c + (y_high + y_low) + (z_high + z_low)
        if k > 0:
            total = total + con[k - 1]
        else:
            total = total + jnp.where(even_col, 0.0, roll(con[packs - 1], 1, 1))
        if k < packs - 1:
            total = total + con[k + 1]
        else:
            total = total + jnp.where(even_col, roll(con[0], -1, 1), 0.0)
        total = 2.0 * total
        tile_gain.append(OMEGA / jnp.where(total > 0.0, total, 1.0))
        link_y.append(jnp.where(y_end, 0.0, 2.0 * (c + y_high)))
        link_z.append(jnp.where(z_end, 0.0, 2.0 * (c + z_high)))
    fix = [tile_gain[k] * res[k] for k in range(packs)]
    for _ in range(BLOCK_SWEEPS - 1):
        updated = []
        for k in range(packs):
            value = fix[k]
            acc = res[k] + link_y[k] * roll(value, -2, 1) + roll(link_y[k] * value, 2, 1)
            acc = acc + link_z[k] * roll(value, -2, 2) + roll(link_z[k] * value, 2, 2)
            if k > 0:
                acc = acc + link_x[k - 1] * fix[k - 1]
            else:
                acc = acc + middle_high * roll(fix[packs - 1], 1, 1)
            if k < packs - 1:
                acc = acc + link_x[k] * fix[k + 1]
            else:
                acc = acc + middle_low * roll(fix[0], -1, 1)
            updated.append(KEEP * value + tile_gain[k] * acc)
        fix = updated
    flat_lane = iota((tile_w, layers), 1) % 2 == 0
    touched = jnp.stack(
        [
            jnp.where(flat_lane, route[0, 2 * t], route[0, 2 * t + 1]) >= 0
            for t in range(couples)
        ]
    )
    fix = [jnp.where(touched, f, 0.0) for f in fix]

    fine = [None] * (rows // 2)
    for k in range(packs):
        for j, part in enumerate(unpack_pairs(fix[k], 1)):
            both = unpack_pairs(part, 2)
            fine[k + j * packs] = jnp.stack(both, axis=1).reshape(cols, layers)

    for i in range(rows + 4):
        if 2 <= i < rows + 2:
            state[i, own, :] = pres[i, own, :] + fine[(i - 2) // 2]
            state[i, halo, :] = pres[i, halo, :]
        else:
            state[i] = pres[i]

    pair_col = iota((tile_w, layers), 0)
    rim_shape = (tile_w, layers)

    def rim(row):
        f = fine[row].reshape(couples, 2, tile_w, layers)
        by_lane = [jnp.where(flat_lane, f[t, 0], f[t, 1]) for t in range(couples)]
        out = by_lane[0]
        for t in range(1, couples):
            out = jnp.where(pair_col % couples == t, by_lane[t], out)
        return out[:, :LANES], out[:, LANES:]

    rims = [rim(0), rim(rows // 2 - 1)]
    even_ahead, _ = facing(down, nd, False)
    even_rim = [jnp.where(even_ahead, b, a) for a, b in zip(*rims)]
    odd_rim = [jnp.where(even_ahead, a, b) for a, b in zip(*rims)]
    swapped[:HALF] = even_rim[0]
    swapped[HALF : 2 * HALF] = even_rim[1]
    swapped[2 * HALF :] = odd_rim[1]

    blank = jnp.zeros((HALF, LANES), FLOAT)

    def fill(b, carry):
        at = b * CHUNK
        chunks[pl.ds(at, HALF), :] = blank
        chunks[pl.ds(at + HALF, 1), :] = summary
        return carry

    lax.fori_loop(0, nd * nc, fill, 0)
    me = down * nc + cross
    if n_down > 1:
        step = jnp.where(even_ahead, -1, 1)

        @pl.when(beside(down, nd, step))
        def _():
            chunks[pl.ds((me + step * nc) * CHUNK, HALF), :] = odd_rim[0]

    for dy in (-1, 1):
        column = 0 if dy < 0 else cols - 1

        @pl.when(beside(cross, nc, dy))
        def _(dy=dy, column=column):
            lines = []
            for k in range(rows // 2):
                f = fine[k][column : column + 1]
                lines += [f[:, :LANES], f[:, LANES:]]
            at = (me + dy) * CHUNK
            for i, f in enumerate(lines):
                chunks[pl.ds(at + i, 1), :] = f
            for dx in (-1, 1):

                @pl.when(beside(down, nd, dx))
                def _(dx=dx):
                    at = (me + dy + dx * nc) * CHUNK
                    pair = lines[:2] if dx < 0 else lines[-2:]
                    chunks[pl.ds(at, 1), :] = pair[0]
                    chunks[pl.ds(at + 1, 1), :] = pair[1]


def relay_kernel(nd, nc, chunks_in, swapped, chunks):
    chunks[...] = chunks_in[...]
    down, cross = lax.axis_index("down"), lax.axis_index("cross")
    step = jnp.where(down % 2 == 0, 2, -2)

    @pl.when(beside(down, nd, step))
    def _():
        at = ((down + step) * nc + cross) * CHUNK
        chunks[pl.ds(at, HALF), :] = swapped[2 * HALF :]


def coarse_solve(totals, outflow, link_down, link_up, link_cross):
    nc = len(totals)

    def operate(v):
        out = []
        for c in range(nc):
            image = outflow[c] * v[c] - link_down[c] * roll(v[c], -1, 0) - link_up[c] * roll(v[c], 1, 0)
            if c < nc - 1:
                image = image - link_cross[c] * v[c + 1]
            if c > 0:
                image = image - link_cross[c - 1] * v[c - 1]
            out.append(image)
        return out

    def dot(a, b):
        return jnp.sum(sum(x * y for x, y in zip(a, b)), axis=0, keepdims=True)

    answer = [jnp.zeros_like(t) for t in totals]
    resid = search = totals
    norm = dot(totals, totals)
    for step in range(COARSE_ITERS):
        image = operate(search)
        alpha = norm / dot(search, image)
        answer = [a + alpha * s for a, s in zip(answer, search)]
        if step == COARSE_ITERS - 1:
            break
        resid = [r - alpha * m for r, m in zip(resid, image)]
        norm_next = dot(resid, resid)
        beta = norm_next / norm
        search = [r + beta * s for r, s in zip(resid, search)]
        norm = norm_next
    return answer


def last_kernel(nd, nc, tiles, got, swapped, src, gain, wx, wy, wz, state, out, bricks, pres, third):
    rows, cols, layers = out.shape
    tile_w = cols // tiles
    couples = tiles // 2
    down, cross = lax.axis_index("down"), lax.axis_index("cross")
    own, halo = slice(0, cols), slice(cols, cols + STRIP)

    tables = [got[pl.ds(c * CHUNK + HALF, nd, stride=nc * CHUNK), :] for c in range(nc)]

    def spread_lane(table, at):
        return jnp.broadcast_to(table[:, at : at + 1], (nd, LANES))

    last = iota((nd, LANES), 0) == nd - 1
    totals = [spread_lane(t, 0) for t in tables]
    link_down = [jnp.where(last, 0.0, spread_lane(t, 1)) for t in tables]
    link_up = [roll(link, 1, 0) for link in link_down]
    link_cross = [spread_lane(t, 2) for t in tables]
    outflow = [spread_lane(t, 3) for t in tables]
    answer = coarse_solve(totals, outflow, link_down, link_up, link_cross)
    for c in range(nc):
        bricks[c] = answer[c]

    def brick(dx, dy):
        line = bricks[jnp.clip(cross + dy, 0, nc - 1), pl.ds(jnp.clip(down + dx, 0, nd - 1), 1), :]
        return jnp.concatenate([line] * (layers // LANES), axis=1)

    def lines(dx, dy, start, count):
        row, col = jnp.clip(down + dx, 0, nd - 1), jnp.clip(cross + dy, 0, nc - 1)
        return got[pl.ds((row * nc + col) * CHUNK + start, count), :]

    def unpack(packed):
        sub = iota((tile_w, layers), 0) % couples
        parts = []
        for t in range(couples):
            tall = jnp.where(sub == t, packed, 0.0)
            for shift in range(1, couples):
                tall = tall + jnp.where(
                    sub == (t + shift) % couples, roll(packed, shift if t + shift < couples else shift - couples, 0), 0.0
                )
            parts += unpack_pairs(tall, 1)
        return jnp.concatenate(parts, axis=0)

    mine = brick(0, 0)
    for i in range(2, rows + 2):
        pres[i, own, :] = state[i, own, :] + mine
    even_ahead = down % 2 == 0
    even_rim = jnp.concatenate([swapped[:HALF], swapped[HALF : 2 * HALF]], axis=1)
    odd_step = jnp.where(even_ahead, -1, 1)
    odd_rim = jnp.concatenate([lines(odd_step, 0, 0, HALF), lines(2 * odd_step, 0, 0, HALF)], axis=1)
    for dx, at in ((-1, 0), (1, rows + 2)):
        rim = jnp.where(even_ahead == (dx > 0), even_rim, odd_rim)
        extra = jnp.where(beside(down, nd, dx), unpack(rim) + brick(dx, 0), 0.0)
        for i in (at, at + 1):
            pres[i, own, :] = state[i, own, :] + extra

    right = iota((STRIP, layers), 0) < STRIP // 2
    there = (iota((STRIP, layers), 0) < jnp.where(cross < nc - 1, STRIP // 2, 0)) | (
        iota((STRIP, layers), 0) >= jnp.where(cross > 0, STRIP // 2, STRIP)
    )
    b_right, b_left = brick(0, 1), brick(0, -1)
    e_right, e_left = lines(0, 1, 0, HALF), lines(0, -1, 0, HALF)

    def line_pair(block, k):
        return jnp.concatenate([block[2 * k : 2 * k + 1], block[2 * k + 1 : 2 * k + 2]], axis=1)

    for k in range(rows // 2):
        extra = jnp.where(right, line_pair(e_right, k) + b_right, line_pair(e_left, k) + b_left)
        extra = jnp.where(there, extra, 0.0)
        for i in (2 * k + 2, 2 * k + 3):
            pres[i, halo, :] = state[i, halo, :] + extra
    for dx, at in ((-1, 0), (1, rows + 2)):
        extra = jnp.where(
            right,
            line_pair(lines(dx, 1, 0, 2), 0) + brick(dx, 1),
            line_pair(lines(dx, -1, 0, 2), 0) + brick(dx, -1),
        )
        extra = jnp.where(there & beside(down, nd, dx), extra, 0.0)
        for i in (at, at + 1):
            pres[i, halo, :] = state[i, halo, :] + extra

    for i in range(rows + 2):
        spread = gather(pres, i + 1, wx, i + 2, wy[i + 1], wz[i + 1])
        third[i] = KEEP * pres[i + 1] + gain[i + 2] * (src[i + 2] + spread)
    for x in range(rows):
        spread = gather(third, x + 1, wx, x + 3, wy[x + 2], wz[x + 2])
        new = KEEP * third[x + 1] + gain[x + 3] * (src[x + 3] + spread)
        out[x] = new[own]


def whole(*shape):
    return jax.ShapeDtypeStruct(shape, FLOAT)


def call(kernel, out_shape, spaces, scratch=(), vmem_bytes=VMEM_BYTES):
    return pl.pallas_call(
        kernel,
        out_shape=out_shape,
        in_specs=[pl.BlockSpec(memory_space=s) for s in spaces],
        out_specs=jax.tree.map(lambda _: pl.BlockSpec(memory_space=pltpu.VMEM), out_shape),
        scratch_shapes=list(scratch),
        compiler_params=pltpu.CompilerParams(vmem_limit_bytes=vmem_bytes),
    )


def body(nd, nc, right_side, kappa, band_mask, tile_route):
    rows, cols, layers = right_side.shape
    tiles = tile_route.shape[1]
    axes = ("down", "cross")
    wide = cols + STRIP
    block = whole(rows, cols, layers)
    vmem, smem = pltpu.VMEM, pltpu.SMEM

    shapes, perms = [], []
    for kind in pairings(nd):
        shapes.append(whole(2 * DEPTH - 1, cols, layers))
        perms.append(pairs_of(nd, nc, kind, None))
        if kind:
            for cross_kind in pairings(nc):
                shapes.append(whole(CORNER, STRIP, layers))
                perms.append(pairs_of(nd, nc, kind, cross_kind))
    strip = [whole(2 * rows, STRIP, layers) for _ in pairings(nc)]
    conduct, *messages = call(
        functools.partial(pack_kernel, nd, nc),
        [block] + shapes + strip,
        [pltpu.HBM] * 3,
        scratch=[
            pltpu.VMEM((rows, cols, layers), FLOAT),
            pltpu.VMEM((rows, cols, layers), FLOAT),
            pltpu.VMEM((rows, cols, layers), band_mask.dtype),
            pltpu.SemaphoreType.DMA((3,)),
        ],
        vmem_bytes=53 * 1024 * 1024,
    )(right_side, kappa, band_mask)
    received = [lax.ppermute(m, axes, p) for m, p in zip(messages, perms)]
    if pairings(nc):
        strips = call(
            functools.partial(strip_kernel, nd, nc),
            [whole(2 * rows + CORNER, STRIP, layers) for _ in pairings(nc)],
            [vmem] * (1 + len(strip)),
        )(received[0], *messages[len(perms) :])
        received += [
            lax.ppermute(m, axes, pairs_of(nd, nc, None, cross_kind))
            for m, cross_kind in zip(strips, pairings(nc))
        ]

    heights = (rows + 6, rows + 6, rows + 5, rows + 4, rows + 4, rows + 4)
    *kept, swapped, chunks = call(
        functools.partial(main_kernel, nd, nc),
        [whole(h, wide, layers) for h in heights]
        + [whole(3 * HALF, LANES), whole(nd * nc * CHUNK, LANES)],
        [vmem, vmem, smem] + [vmem] * len(received),
        scratch=[
            pltpu.VMEM((h, wide, layers), FLOAT) for h in (rows + 8, rows + 6, rows + 4, rows)
        ],
    )(right_side, conduct, tile_route, *received)
    swapped = lax.ppermute(swapped, axes, pairs_of(nd, nc, False, None))
    chunks = call(
        functools.partial(relay_kernel, nd, nc),
        whole(nd * nc * CHUNK, LANES),
        [vmem, vmem],
    )(chunks, swapped)
    chunks = chunks.reshape(nd * nc, CHUNK, 1, LANES)
    arrived = lax.all_to_all(chunks, axes, 0, 0, tiled=True).reshape(nd * nc * CHUNK, LANES)
    return call(
        functools.partial(last_kernel, nd, nc, tiles),
        block,
        [vmem] * (2 + len(kept)),
        scratch=[
            pltpu.VMEM((nc, nd, LANES), FLOAT),
            pltpu.VMEM((rows + 4, wide, layers), FLOAT),
            pltpu.VMEM((rows + 2, wide, layers), FLOAT),
        ],
    )(arrived, swapped, *kept)


def solution(mesh):
    return jax.shard_map(
        functools.partial(body, mesh.shape["down"], mesh.shape["cross"]),
        mesh=mesh,
        in_specs=(
            P("down", "cross", None),
            P("down", "cross", None),
            P("down", "cross", None),
            P("down", "cross"),
        ),
        out_specs=P("down", "cross", None),
        check_vma=False,
    )
```

```python
import functools

import jax
import jax.numpy as jnp
from jax import lax
from jax.experimental import pallas as pl
from jax.experimental.pallas import tpu as pltpu
from jax.sharding import PartitionSpec as P

BLOCK_SWEEPS = 4
COARSE_ITERS = 12
OMEGA = 0.8
KEEP = 1.0 - OMEGA
SNOW_FACTOR = 3.0

DEPTH = 4
CORNER = DEPTH - 1
STRIP = 8
LANES = 128
HALF = 8
CHUNK = HALF + 1
FLOAT = jnp.float32
VMEM_BYTES = 48 * 1024 * 1024


def partners(count, odd):
    found = []
    for i in range(count):
        j = ((i + 1) ^ 1) - 1 if odd else i ^ 1
        found.append(j if 0 <= j < count else i)
    return found


def pairings(count):
    return [k for k in (False, True) if any(j != i for i, j in enumerate(partners(count, k)))]


def pairs_of(count_down, count_cross, down_kind, cross_kind):
    rows = list(range(count_down)) if down_kind is None else partners(count_down, down_kind)
    cols = list(range(count_cross)) if cross_kind is None else partners(count_cross, cross_kind)
    return [
        (i * count_cross + j, rows[i] * count_cross + cols[j])
        for i in range(count_down)
        for j in range(count_cross)
    ]


def facing(index, count, kind):
    ahead = (index % 2 == 0) != kind
    return ahead, jnp.where(ahead, index < count - 1, index > 0)


def beside(index, count, step):
    return (index + step >= 0) & (index + step < count)


def roll(x, amount, axis):
    return pltpu.roll(x, amount % x.shape[axis], axis)


def iota(shape, axis):
    return lax.broadcasted_iota(jnp.int32, shape, axis)


def gather(value, low, high, wx_low, wx_high, wy, wz):
    total = wx_high * high + wx_low * low
    total = total + wy * roll(value, -1, 0) + roll(wy * value, 1, 0)
    return total + wz * roll(value, -1, 1) + roll(wz * value, 1, 1)


class Rows:
    def __init__(self, *parts):
        self.parts = parts

    def place(self, x):
        for ref, first, count in self.parts:
            if first <= x < first + count:
                return ref, x - first
        raise IndexError(x)

    def __getitem__(self, x):
        ref, i = self.place(x)
        return ref[i]

    def __setitem__(self, x, value):
        ref, i = self.place(x)
        ref[i] = value


def smooth(field, gain, src, wx, wy, wz, x):
    spread = gather(field[x], field[x - 1], field[x + 1], wx[x - 1], wx[x], wy[x], wz[x])
    return KEEP * field[x] + gain[x] * (src[x] + spread)


def counted(x, rows):
    return jnp.where(lax.axis_index("down") % 2 == 0, x, rows - 1 - x)


def edge_strip(right, cols):
    return pl.ds(pl.multiple_of(jnp.where(right, cols - STRIP, 0), STRIP), STRIP)


def pack_rows(out, start, tiles, right):
    for i in range(0, len(tiles), 2):
        a, b = tiles[i], tiles[min(i + 1, len(tiles) - 1)]
        upper = iota(a.shape, 0) < STRIP // 2
        a, b = jnp.where(right, roll(a, STRIP // 2, 0), a), jnp.where(right, b, roll(b, STRIP // 2, 0))
        out[start + i // 2] = jnp.where(upper, a, b)


def unpack_row(message, start, i, right):
    tile = message[start + i // 2]
    return jnp.where(right == (i % 2 == 0), tile, roll(tile, STRIP // 2, 0))


def pack_kernel(nd, nc, rhs_hbm, kappa_hbm, mask_hbm, conduct, *refs):
    *messages, rhs, kappa, mask, sems = refs
    rows, cols, _ = rhs.shape
    messages = iter(messages)
    cross = lax.axis_index("cross")
    copies = [
        pltpu.make_async_copy(src, dst, sems.at[i])
        for i, (src, dst) in enumerate(((kappa_hbm, kappa), (mask_hbm, mask), (rhs_hbm, rhs)))
    ]
    for copy in copies:
        copy.start()
    copies[0].wait()
    copies[1].wait()
    for x in range(rows):
        at = counted(x, rows)
        conduct[x] = kappa[at] / (1.0 + SNOW_FACTOR * mask[at].astype(FLOAT))
    copies[2].wait()
    for kind in pairings(nd):
        near = [i if kind else rows - 1 - i for i in range(DEPTH)]
        out = next(messages)
        for i, x in enumerate(near):
            out[i] = conduct[x]
        for i, x in enumerate(near[:-1]):
            out[DEPTH + i] = rhs[counted(x, rows)]
        if kind:
            for cross_kind in pairings(nc):
                right, _ = facing(cross, nc, cross_kind)
                strip = edge_strip(right, cols)
                tiles = [conduct[x, strip, :] for x in near[: DEPTH - 1]]
                tiles += [rhs[counted(x, rows), strip, :] for x in near[: DEPTH - 2]]
                pack_rows(next(messages), 0, tiles, right)
    for cross_kind in pairings(nc):
        right, _ = facing(cross, nc, cross_kind)
        strip = edge_strip(right, cols)
        tiles = [conduct[x, strip, :] for x in range(rows)]
        tiles += [rhs[counted(x, rows), strip, :] for x in range(rows)]
        pack_rows(next(messages), 0, tiles, right)


def strip_kernel(nd, nc, even, *refs):
    cols = even.shape[1]
    count = len(pairings(nc))
    for cross_kind, own, out in zip(pairings(nc), refs[:count], refs[count:]):
        right, _ = facing(lax.axis_index("cross"), nc, cross_kind)
        strip = edge_strip(right, cols)
        rows = own.shape[0]
        out[:rows] = own[...]
        tiles = [even[i, strip, :] for i in range(DEPTH - 1)]
        tiles += [even[DEPTH + i, strip, :] for i in range(DEPTH - 2)]
        pack_rows(out, rows, tiles, right)


def fold(x):
    x = sum(x[:, i : i + LANES] for i in range(0, x.shape[1], LANES))
    return jnp.sum(x, axis=0, keepdims=True)


def swap_pairs(x, axis):
    return jnp.where(iota(x.shape, axis) % 2 == 0, roll(x, -1, axis), roll(x, 1, axis))


def pack_pairs(a, b, axis):
    even = iota(a.shape, axis) % 2 == 0
    return jnp.where(even, a, b) + swap_pairs(jnp.where(even, b, a), axis)


def unpack_pairs(x, axis):
    even = iota(x.shape, axis) % 2 == 0
    return jnp.where(even, x, roll(x, 1, axis)), jnp.where(even, roll(x, -1, axis), x)


class Frame:
    def __init__(self, nd, nc, cols, layers):
        self.cols, self.layers, self.wide = cols, layers, cols + STRIP
        self.own, self.halo = slice(0, cols), slice(cols, cols + STRIP)
        cross = lax.axis_index("cross")
        half = STRIP // 2
        self.lane = iota((self.wide, layers), 1)
        self.last_lane = self.lane == layers - 1
        col = iota((self.wide, layers), 0)
        self.col_ok = (col < jnp.where(cross < nc - 1, cols + half, cols)) | (
            col >= jnp.where(cross > 0, cols + half, self.wide)
        )
        halo_col = iota((STRIP, layers), 0)
        self.sides, self.rights = [], []
        for cross_kind in pairings(nc):
            right, valid = facing(cross, nc, cross_kind)
            start = jnp.where(right, 0, half)
            stop = jnp.where(valid, start + half, 0)
            self.sides.append((halo_col >= start) & (halo_col < stop))
            self.rights.append(right)

    def merged(self, messages, start, i):
        total = jnp.zeros((STRIP, self.layers), FLOAT)
        for side, right, message in zip(self.sides, self.rights, messages):
            total = jnp.where(side, unpack_row(message, start, i, right), total)
        return total

    def row(self, own, halo):
        return jnp.concatenate([own, halo], axis=0)

    def weights(self, q, gain, src, first, diag, wx, wy, wz, x, valid=None):
        here = q[x]
        above = jnp.where(self.last_lane, 0.0, roll(here, -1, 1))
        below = jnp.where(self.lane == 0, 0.0, roll(here, 1, 1))
        right = roll(here, -1, 0)
        doubled = 6.0 * here + (q[x - 1] + q[x + 1]) + (right + roll(here, 1, 0)) + (above + below)
        ok = self.col_ok & (doubled > 0.0)
        if valid is not None:
            ok = ok & valid
        gain_here = jnp.where(ok, (2.0 * OMEGA) / doubled, 0.0)
        gain[x] = gain_here
        first[x] = gain_here * src[x]
        if diag is not None:
            diag[x] = 0.5 * doubled
        if wx is not None:
            wx[x] = 0.5 * (here + q[x + 1])
        if wy is not None:
            self.plane_weights(wy, wz, x, here, right, above)

    def plane_weights(self, wy, wz, x, here, right, above):
        wy[x] = 0.5 * (here + right)
        wz[x] = jnp.where(self.last_lane, 0.0, 0.5 * (here + above))


def residual(frame, src, diag, pres, wx, wy, wz, x):
    spread = gather(pres[x], pres[x - 1], pres[x + 1], wx[x - 1], wx[x], wy[x], wz[x])
    return (src[x] - diag[x] * pres[x] + spread)[frame.own]


def spans(rows):
    far = rows + DEPTH
    early = dict(
        q=(0, far), src=(0, far - 1), gain=(1, far - 1), first=(1, far - 1), diag=(1, rows),
        wx=(0, far - 2), wy=(0, rows + 2), wz=(0, rows + 2), pres=(2, rows + 2),
    )
    late = dict(
        q=(-DEPTH, 0), src=(1 - DEPTH, 0), gain=(1 - DEPTH, 1), first=(1 - DEPTH, 1), diag=(0, 1),
        wx=(1 - DEPTH, 0), wy=(-2, 0), wz=(-2, 0), pres=(-2, 2),
    )
    return early, late


EARLY = ("q", "src", "gain", "first", "diag", "wx", "wy", "wz", "pres")
LATE_KEPT = ("src", "gain", "wx", "wy", "wz", "pres")
LATE_SCRATCH = ("q", "first", "diag")


def span_shape(span, wide, layers):
    return (span[1] - span[0], wide, layers)


def joined(rows, name, early_ref, late_ref):
    early, late = (d[name] for d in spans(rows))
    return Rows((early_ref, early[0], early[1] - early[0]), (late_ref, late[0], late[1] - late[0]))


def coarse_rows(pair, couples, tile_w):
    t = pair.reshape(couples, 2, tile_w, pair.shape[1])
    return pack_pairs(t[:, 0], t[:, 1], 2)


def early_kernel(nd, nc, tiles, rhs, conduct, route, even, *refs):
    rows, cols, layers = conduct.shape
    tile_w = cols // tiles
    couples = tiles // 2
    n_cross = len(pairings(nc))
    strips = refs[:n_cross]
    *arrays, res_coarse, res_row, coef, sums, touched = refs[n_cross:]
    early, _ = spans(rows)
    at = {n: Rows((r, early[n][0], r.shape[0])) for n, r in zip(EARLY, arrays)}
    q, src, gain, first, diag, wx, wy, wz, pres = (at[n] for n in EARLY)
    frame = Frame(nd, nc, cols, layers)
    own, halo = frame.own, frame.halo

    for x in range(rows):
        q[x] = frame.row(conduct[x], frame.merged(strips, 0, x))
        src[x] = frame.row(rhs[counted(x, rows)], frame.merged(strips, 0, rows + x))
    _, valid = facing(lax.axis_index("down"), nd, False)
    blank = jnp.zeros((STRIP, layers), FLOAT)
    for i in range(DEPTH):
        corner = frame.merged(strips, rows, i) if i < DEPTH - 1 else blank
        q[rows + i] = jnp.where(valid, frame.row(even[i], corner), 0.0)
    for i in range(DEPTH - 1):
        corner = frame.merged(strips, rows, DEPTH - 1 + i) if i < DEPTH - 2 else blank
        src[rows + i] = jnp.where(valid, frame.row(even[DEPTH + i], corner), 0.0)

    here = q[0]
    above = jnp.where(frame.last_lane, 0.0, roll(here, -1, 1))
    frame.plane_weights(wy, wz, 0, here, roll(here, -1, 0), above)
    wx[0] = 0.5 * (here + q[1])
    for x in range(*early["gain"]):
        frame.weights(
            q, gain, src, first,
            diag if x < rows else None,
            wx if x < early["wx"][1] else None,
            wy if x < early["wy"][1] else None,
            wz, x, valid if x >= rows else None,
        )
    for x in range(*early["pres"]):
        pres[x] = smooth(first, gain, src, wx, wy, wz, x)

    res = {x: residual(frame, src, diag, pres, wx, wy, wz, x) for x in range(3, rows)}
    res_row[...] = res[3]
    for k in range(2, rows // 2):
        res_coarse[k - 2] = coarse_rows(res[2 * k] + res[2 * k + 1], couples, tile_w)

    even_lane = iota((tile_w, layers), 1) % 2 == 0
    for t in range(couples):
        numbers = [jnp.broadcast_to(route[0:1, i : i + 1], (tile_w, layers)) for i in (2 * t, 2 * t + 1)]
        touched[t] = jnp.where(jnp.where(even_lane, *numbers) >= 0, 1.0, 0.0)

    strip_col = iota((STRIP, layers), 0)
    plane = sum(q[x][own] for x in range(rows))
    beyond = sum(q[x][halo] for x in range(rows))
    own_lane = iota((cols, layers), 1)
    low, high = strip_col < 2, strip_col >= STRIP - 2
    sums[0:1] = fold(sum(res.values()))
    sums[1:2] = fold(sum(q[x][own] for x in range(rows - 2, rows + 2)))
    sums[2:3] = fold(jnp.where(high, plane[cols - STRIP :], 0.0) + jnp.where(low, beyond, 0.0))
    sums[3:4] = fold(jnp.where(low, plane[:STRIP], 0.0) + jnp.where(high, beyond, 0.0))
    sums[4:5] = fold(jnp.where((own_lane < 2) | (own_lane >= layers - 2), plane, 0.0))

    packs = rows // 4
    by_row = [
        coarse_rows(0.125 * (q[2 * k][own] + q[2 * k + 1][own]), couples, tile_w)
        for k in range(rows // 2)
    ]
    con = [pack_pairs(by_row[k], by_row[k + packs], 1) for k in range(packs)]
    shape = (couples, tile_w, layers)
    tile_col, tile_lane = iota(shape, 1), iota(shape, 2)
    even_col = tile_col % 2 == 0
    y_end, y_start = tile_col >= tile_w - 2, tile_col < 2
    z_end, z_start = tile_lane >= layers - 2, tile_lane < 2
    for k in range(packs - 1):
        coef[3 * packs + 2 + k] = 2.0 * (con[k] + con[k + 1])
    middle = 2.0 * (con[packs - 1] + roll(con[0], -1, 1))
    coef[3 * packs] = jnp.where(even_col, middle, 0.0)
    coef[3 * packs + 1] = jnp.where(even_col, 0.0, roll(middle, 1, 1))
    for k in range(packs):
        c = con[k]
        y_high = jnp.where(y_end, 0.0, roll(c, -2, 1))
        z_high = jnp.where(z_end, 0.0, roll(c, -2, 2))
        y_low = jnp.where(y_start, 0.0, roll(c, 2, 1))
        z_low = jnp.where(z_start, 0.0, roll(c, 2, 2))
        total = 6.0 * c + (y_high + y_low) + (z_high + z_low)
        if k > 0:
            total = total + con[k - 1]
        else:
            total = total + jnp.where(even_col, 0.0, roll(con[packs - 1], 1, 1))
        if k < packs - 1:
            total = total + con[k + 1]
        else:
            total = total + jnp.where(even_col, roll(con[0], -1, 1), 0.0)
        total = 2.0 * total
        coef[k] = OMEGA / jnp.where(total > 0.0, total, 1.0)
        coef[packs + k] = jnp.where(y_end, 0.0, 2.0 * (c + y_high))
        coef[2 * packs + k] = jnp.where(z_end, 0.0, 2.0 * (c + z_high))


def late_kernel(nd, nc, tiles, rows, odd, *refs):
    n_cross = len(pairings(nc)) if len(pairings(nd)) > 1 else 0
    corners = refs[:n_cross]
    n_in = n_cross + len(EARLY) + 5
    early_refs = dict(zip(EARLY, refs[n_cross:]))
    res_coarse, res_row, coef, sums, touched = refs[n_in - 5 : n_in]
    names = LATE_KEPT + ("swapped", "fix", "summary") + LATE_SCRATCH
    late_refs = dict(zip(names, refs[n_in:]))
    swapped, fix_out, summary = (late_refs[n] for n in ("swapped", "fix", "summary"))
    wide, layers = early_refs["q"].shape[1:]
    cols = wide - STRIP
    tile_w = cols // tiles
    couples = tiles // 2
    down = lax.axis_index("down")
    even = down % 2 == 0
    q, src, gain, first, diag, wx, wy, wz, pres = (
        joined(rows, n, early_refs[n], late_refs[n]) for n in EARLY
    )
    frame = Frame(nd, nc, cols, layers)
    _, late = spans(rows)

    valid = beside(down, nd, jnp.where(even, -1, 1))
    blank = jnp.zeros((STRIP, layers), FLOAT)
    for i in range(DEPTH):
        corner = frame.merged(corners, 0, i) if i < DEPTH - 1 else blank
        q[-1 - i] = jnp.where(valid, frame.row(odd[i], corner), 0.0)
    for i in range(DEPTH - 1):
        corner = frame.merged(corners, 0, DEPTH - 1 + i) if i < DEPTH - 2 else blank
        src[-1 - i] = jnp.where(valid, frame.row(odd[DEPTH + i], corner), 0.0)
    for x in range(*late["gain"]):
        frame.weights(
            q, gain, src, first,
            diag if x == 0 else None,
            wx if x < 0 else None,
            wy if -2 <= x < 0 else None,
            wz, x, valid if x < 0 else None,
        )
    for x in range(*late["pres"]):
        pres[x] = smooth(first, gain, src, wx, wy, wz, x)
    res = [residual(frame, src, diag, pres, wx, wy, wz, x) for x in range(3)]
    res.append(res_row[...])

    res_total = sums[0:1] + fold(res[0] + res[1] + res[2])
    link_odd = fold(sum(q[x][frame.own] for x in range(-2, 2)))
    link_even, link_cross, link_back, ends = (sums[i : i + 1] for i in range(1, 5))
    outflow = link_even + link_odd + link_cross + link_back + ends
    link_down = jnp.where(even, link_even, link_odd)
    lines = jnp.concatenate([res_total, 0.25 * link_down, 0.25 * link_cross, 0.25 * outflow])
    lines = jnp.sum(lines, axis=1, keepdims=True)
    line = iota((1, LANES), 1)
    summary[...] = jnp.where(
        line == 0, lines[0:1], jnp.where(line == 1, lines[1:2], jnp.where(line == 2, lines[2:3], lines[3:4]))
    )

    packs = rows // 4
    by_row = [coarse_rows(res[2 * k] + res[2 * k + 1], couples, tile_w) for k in range(2)]
    by_row += [res_coarse[k] for k in range(rows // 2 - 2)]
    r = [pack_pairs(by_row[k], by_row[k + packs], 1) for k in range(packs)]
    middle_low, middle_high = coef[3 * packs], coef[3 * packs + 1]
    fix = [coef[k] * r[k] for k in range(packs)]
    for _ in range(BLOCK_SWEEPS - 1):
        updated = []
        for k in range(packs):
            value, link_y, link_z = fix[k], coef[packs + k], coef[2 * packs + k]
            acc = r[k] + link_y * roll(value, -2, 1) + roll(link_y * value, 2, 1)
            acc = acc + link_z * roll(value, -2, 2) + roll(link_z * value, 2, 2)
            if k > 0:
                acc = acc + coef[3 * packs + 1 + k] * fix[k - 1]
            else:
                acc = acc + middle_high * roll(fix[packs - 1], 1, 1)
            if k < packs - 1:
                acc = acc + coef[3 * packs + 2 + k] * fix[k + 1]
            else:
                acc = acc + middle_low * roll(fix[0], -1, 1)
            updated.append(KEEP * value + coef[k] * acc)
        fix = updated
    fix = [jnp.where(touched[...] > 0.0, f, 0.0) for f in fix]
    for k in range(packs):
        fix_out[k] = fix[k]

    def rim(k, j):
        part = unpack_pairs(fix[k], 1)[j]
        sub = iota((tile_w, layers), 0) % couples
        packed = part[0]
        for t in range(1, couples):
            packed = jnp.where(sub == t, part[t], packed)
        return packed[:, :LANES], packed[:, LANES:]

    even_rim, odd_rim = rim(packs - 1, 1), rim(0, 0)
    swapped[:HALF] = even_rim[0]
    swapped[HALF : 2 * HALF] = even_rim[1]
    swapped[2 * HALF : 3 * HALF] = odd_rim[1]
    swapped[3 * HALF :] = odd_rim[0]


def spread_kernel(nd, nc, tiles, fix, swapped, summary, pres_early, pres_late, state, chunks):
    packs, couples, tile_w, layers = fix.shape
    rows = 4 * packs
    cols = tiles * tile_w
    own, halo = slice(0, cols), slice(cols, cols + STRIP)
    down, cross = lax.axis_index("down"), lax.axis_index("cross")
    pres = joined(rows, "pres", pres_early, pres_late)

    fine = [None] * (rows // 2)
    for k in range(packs):
        for j, part in enumerate(unpack_pairs(fix[k], 1)):
            both = unpack_pairs(part, 2)
            fine[k + j * packs] = jnp.stack(both, axis=1).reshape(cols, layers)

    for x in range(-2, rows + 2):
        value = pres[x]
        if 0 <= x < rows:
            state[x + 2, own, :] = value[own] + fine[x // 2]
            state[x + 2, halo, :] = value[halo]
        else:
            state[x + 2] = value

    blank = jnp.zeros((HALF, LANES), FLOAT)
    sums = summary[...]

    def fill(b, carry):
        at = b * CHUNK
        chunks[pl.ds(at, HALF), :] = blank
        chunks[pl.ds(at + HALF, 1), :] = sums
        return carry

    lax.fori_loop(0, nd * nc, fill, 0)
    me = down * nc + cross
    odd_step = jnp.where(down % 2 == 0, -1, 1)

    @pl.when(beside(down, nd, odd_step))
    def _():
        chunks[pl.ds((me + odd_step * nc) * CHUNK, HALF), :] = swapped[3 * HALF :]

    for dy in (-1, 1):
        column = 0 if dy < 0 else cols - 1

        @pl.when(beside(cross, nc, dy))
        def _(dy=dy, column=column):
            lines = []
            for k in range(rows // 2):
                f = fine[k][column : column + 1]
                lines += [f[:, :LANES], f[:, LANES:]]
            at = (me + dy) * CHUNK
            for i, f in enumerate(lines):
                chunks[pl.ds(at + i, 1), :] = f
            for side in (0, 1):
                dx = -odd_step if side else odd_step

                @pl.when(beside(down, nd, dx))
                def _(side=side, dx=dx):
                    at = (me + dy + dx * nc) * CHUNK
                    pair = lines[-2:] if side else lines[:2]
                    chunks[pl.ds(at, 1), :] = pair[0]
                    chunks[pl.ds(at + 1, 1), :] = pair[1]


def relay_kernel(nd, nc, chunks_in, swapped, chunks):
    chunks[...] = chunks_in[...]
    down, cross = lax.axis_index("down"), lax.axis_index("cross")
    step = jnp.where(down % 2 == 0, 2, -2)

    @pl.when(beside(down, nd, step))
    def _():
        at = ((down + step) * nc + cross) * CHUNK
        chunks[pl.ds(at, HALF), :] = swapped[2 * HALF : 3 * HALF]


def coarse_solve(totals, outflow, link_down, link_up, link_cross):
    nc = len(totals)

    def operate(v):
        out = []
        for c in range(nc):
            image = outflow[c] * v[c] - link_down[c] * roll(v[c], -1, 0) - link_up[c] * roll(v[c], 1, 0)
            if c < nc - 1:
                image = image - link_cross[c] * v[c + 1]
            if c > 0:
                image = image - link_cross[c - 1] * v[c - 1]
            out.append(image)
        return out

    def dot(a, b):
        return jnp.sum(sum(x * y for x, y in zip(a, b)), axis=0, keepdims=True)

    answer = [jnp.zeros_like(t) for t in totals]
    resid = search = totals
    norm = dot(totals, totals)
    for step in range(COARSE_ITERS):
        image = operate(search)
        alpha = norm / dot(search, image)
        answer = [a + alpha * s for a, s in zip(answer, search)]
        if step == COARSE_ITERS - 1:
            break
        resid = [r - alpha * m for r, m in zip(resid, image)]
        norm_next = dot(resid, resid)
        beta = norm_next / norm
        search = [r + beta * s for r, s in zip(resid, search)]
        norm = norm_next
    return answer


KEPT = ("src", "gain", "wx", "wy", "wz")


def last_kernel(nd, nc, tiles, got, swapped, state, *refs):
    early = dict(zip(KEPT, refs))
    late = dict(zip(KEPT, refs[len(KEPT) :]))
    out, bricks, pres_ref, third_ref = refs[2 * len(KEPT) :]
    rows, cols, layers = out.shape
    src, gain, wx, wy, wz = (joined(rows, n, early[n], late[n]) for n in KEPT)
    tile_w = cols // tiles
    couples = tiles // 2
    down, cross = lax.axis_index("down"), lax.axis_index("cross")
    own, halo = slice(0, cols), slice(cols, cols + STRIP)

    tables = [got[pl.ds(c * CHUNK + HALF, nd, stride=nc * CHUNK), :] for c in range(nc)]

    def spread_lane(table, at):
        return jnp.broadcast_to(table[:, at : at + 1], (nd, LANES))

    last = iota((nd, LANES), 0) == nd - 1
    totals = [spread_lane(t, 0) for t in tables]
    link_down = [jnp.where(last, 0.0, spread_lane(t, 1)) for t in tables]
    link_up = [roll(link, 1, 0) for link in link_down]
    link_cross = [spread_lane(t, 2) for t in tables]
    outflow = [spread_lane(t, 3) for t in tables]
    answer = coarse_solve(totals, outflow, link_down, link_up, link_cross)
    for c in range(nc):
        bricks[c] = answer[c]

    def brick(dx, dy):
        line = bricks[jnp.clip(cross + dy, 0, nc - 1), pl.ds(jnp.clip(down + dx, 0, nd - 1), 1), :]
        return jnp.concatenate([line] * (layers // LANES), axis=1)

    def lines(dx, dy, count):
        row, col = jnp.clip(down + dx, 0, nd - 1), jnp.clip(cross + dy, 0, nc - 1)
        return got[pl.ds((row * nc + col) * CHUNK, count), :]

    def line_pair(block, k):
        return jnp.concatenate([block[2 * k : 2 * k + 1], block[2 * k + 1 : 2 * k + 2]], axis=1)

    def unpack(packed):
        sub = iota((tile_w, layers), 0) % couples
        parts = []
        for t in range(couples):
            tall = jnp.where(sub == t, packed, 0.0)
            for s in range(couples):
                if s != t:
                    tall = tall + jnp.where(sub == s, roll(packed, s - t, 0), 0.0)
            parts += unpack_pairs(tall, 1)
        return jnp.concatenate(parts, axis=0)

    odd_step = jnp.where(down % 2 == 0, -1, 1)
    even_rim = jnp.concatenate([swapped[:HALF], swapped[HALF : 2 * HALF]], axis=1)
    odd_rim = jnp.concatenate([lines(odd_step, 0, HALF), lines(2 * odd_step, 0, HALF)], axis=1)
    right = iota((STRIP, layers), 0) < STRIP // 2
    there = (iota((STRIP, layers), 0) < jnp.where(cross < nc - 1, STRIP // 2, 0)) | (
        iota((STRIP, layers), 0) >= jnp.where(cross > 0, STRIP // 2, STRIP)
    )

    pres = Rows((pres_ref, -2, rows + 4))
    third = Rows((third_ref, -1, rows + 2))
    mine = brick(0, 0)
    side_bricks = brick(0, 1), brick(0, -1)
    side_lines = lines(0, 1, HALF), lines(0, -1, HALF)
    for k in range(rows // 2):
        extra = jnp.where(right, *(line_pair(f, k) + b for f, b in zip(side_lines, side_bricks)))
        extra = jnp.where(there, extra, 0.0)
        for x in (2 * k, 2 * k + 1):
            pres_ref[x + 2, own, :] = state[x + 2, own, :] + mine
            pres_ref[x + 2, halo, :] = state[x + 2, halo, :] + extra
    for step, rim, at in ((odd_step, odd_rim, 0), (-odd_step, even_rim, rows + 2)):
        valid = beside(down, nd, step)
        row = jnp.where(valid, unpack(rim) + brick(step, 0), 0.0)
        corner = jnp.where(
            right, *(line_pair(lines(step, dy, 2), 0) + brick(step, dy) for dy in (1, -1))
        )
        corner = jnp.where(there & valid, corner, 0.0)
        for i in (at, at + 1):
            pres_ref[i, own, :] = state[i, own, :] + row
            pres_ref[i, halo, :] = state[i, halo, :] + corner

    for x in range(-1, rows + 1):
        third[x] = smooth(pres, gain, src, wx, wy, wz, x)
    for x in range(rows):
        out[counted(x, rows)] = smooth(third, gain, src, wx, wy, wz, x)[own]


def whole(*shape):
    return jax.ShapeDtypeStruct(shape, FLOAT)


def call(kernel, out_shape, spaces, scratch=(), vmem_bytes=VMEM_BYTES):
    return pl.pallas_call(
        kernel,
        out_shape=out_shape,
        in_specs=[pl.BlockSpec(memory_space=s) for s in spaces],
        out_specs=jax.tree.map(lambda _: pl.BlockSpec(memory_space=pltpu.VMEM), out_shape),
        scratch_shapes=list(scratch),
        compiler_params=pltpu.CompilerParams(vmem_limit_bytes=vmem_bytes),
    )


def body(nd, nc, right_side, kappa, band_mask, tile_route):
    rows, cols, layers = right_side.shape
    tiles = tile_route.shape[1]
    axes = ("down", "cross")
    wide = cols + STRIP
    block = whole(rows, cols, layers)
    vmem = pltpu.VMEM
    early, late = spans(rows)

    shapes, perms = [], []
    for kind in pairings(nd):
        shapes.append(whole(2 * DEPTH - 1, cols, layers))
        perms.append(pairs_of(nd, nc, kind, None))
        if kind:
            for cross_kind in pairings(nc):
                shapes.append(whole(CORNER, STRIP, layers))
                perms.append(pairs_of(nd, nc, kind, cross_kind))
    strips = [whole(rows, STRIP, layers) for _ in pairings(nc)]
    packs, couples, tile_w = rows // 4, tiles // 2, cols // tiles
    tile_shape = (couples, tile_w, layers)
    conduct, *messages = call(
        functools.partial(pack_kernel, nd, nc),
        [block] + shapes + strips,
        [pltpu.HBM] * 3,
        scratch=[
            pltpu.VMEM((rows, cols, layers), FLOAT),
            pltpu.VMEM((rows, cols, layers), FLOAT),
            pltpu.VMEM((rows, cols, layers), band_mask.dtype),
            pltpu.SemaphoreType.DMA((3,)),
        ],
        vmem_bytes=53 * 1024 * 1024,
    )(right_side, kappa, band_mask)

    received = [lax.ppermute(m, axes, p) for m, p in zip(messages, perms)]
    even, odd = received[0], received[1:]
    if strips:
        strips = call(
            functools.partial(strip_kernel, nd, nc),
            [whole(rows + CORNER, STRIP, layers) for _ in strips],
            [vmem] * (1 + len(strips)),
        )(even, *messages[len(perms) :])
        strips = [
            lax.ppermute(m, axes, pairs_of(nd, nc, None, cross_kind))
            for m, cross_kind in zip(strips, pairings(nc))
        ]
    if not odd:
        odd = [jnp.zeros((2 * DEPTH - 1, cols, layers), FLOAT)]

    first_part = call(
        functools.partial(early_kernel, nd, nc, tiles),
        [whole(*span_shape(early[n], wide, layers)) for n in EARLY]
        + [
            whole(rows // 2 - 2, *tile_shape),
            whole(cols, layers),
            whole(4 * packs + 1, *tile_shape),
            whole(5, LANES),
            whole(*tile_shape),
        ],
        [vmem] * (4 + len(strips)),
    )(right_side, conduct, tile_route, even, *strips)
    *late_arrays, swapped, fix, summary = call(
        functools.partial(late_kernel, nd, nc, tiles, rows),
        [whole(*span_shape(late[n], wide, layers)) for n in LATE_KEPT]
        + [whole(4 * HALF, LANES), whole(packs, *tile_shape), whole(1, LANES)],
        [vmem] * (len(odd) + len(first_part)),
        scratch=[pltpu.VMEM(span_shape(late[n], wide, layers), FLOAT) for n in LATE_SCRATCH],
    )(*odd, *first_part)
    early_arrays = dict(zip(EARLY, first_part))
    late_arrays = dict(zip(LATE_KEPT, late_arrays))

    partner = lax.ppermute(swapped, axes, pairs_of(nd, nc, False, None))
    state, chunks = call(
        functools.partial(spread_kernel, nd, nc, tiles),
        [whole(rows + 4, wide, layers), whole(nd * nc * CHUNK, LANES)],
        [vmem] * 5,
    )(fix, swapped, summary, early_arrays["pres"], late_arrays["pres"])
    chunks = call(
        functools.partial(relay_kernel, nd, nc),
        whole(nd * nc * CHUNK, LANES),
        [vmem, vmem],
    )(chunks, partner)
    chunks = chunks.reshape(nd * nc, CHUNK, 1, LANES)
    arrived = lax.all_to_all(chunks, axes, 0, 0, tiled=True).reshape(nd * nc * CHUNK, LANES)
    return call(
        functools.partial(last_kernel, nd, nc, tiles),
        block,
        [vmem] * (3 + 2 * len(KEPT)),
        scratch=[
            pltpu.VMEM((nc, nd, LANES), FLOAT),
            pltpu.VMEM((rows + 4, wide, layers), FLOAT),
            pltpu.VMEM((rows + 2, wide, layers), FLOAT),
        ],
    )(arrived, partner, state, *(early_arrays[n] for n in KEPT), *(late_arrays[n] for n in KEPT))


def solution(mesh):
    return jax.shard_map(
        functools.partial(body, mesh.shape["down"], mesh.shape["cross"]),
        mesh=mesh,
        in_specs=(
            P("down", "cross", None),
            P("down", "cross", None),
            P("down", "cross", None),
            P("down", "cross"),
        ),
        out_specs=P("down", "cross", None),
        check_vma=False,
    )
```

```python
import functools

import jax
import jax.numpy as jnp
from jax import lax
from jax.experimental import pallas as pl
from jax.experimental.pallas import tpu as pltpu
from jax.sharding import PartitionSpec as P

BLOCK_SWEEPS = 4
COARSE_ITERS = 12
OMEGA = 0.8
KEEP = 1.0 - OMEGA
SNOW_FACTOR = 3.0

DEPTH = 4
CORNER = DEPTH - 1
STRIP = 8
LANES = 128
LINES = 4
CHUNK = LINES + 1
FLOAT = jnp.float32
VMEM_BYTES = 24 * 1024 * 1024


def partners(count, odd):
    found = []
    for i in range(count):
        j = ((i + 1) ^ 1) - 1 if odd else i ^ 1
        found.append(j if 0 <= j < count else i)
    return found


def pairings(count):
    return [k for k in (False, True) if any(j != i for i, j in enumerate(partners(count, k)))]


def pairs_of(count_down, count_cross, down_kind, cross_kind):
    rows = list(range(count_down)) if down_kind is None else partners(count_down, down_kind)
    cols = list(range(count_cross)) if cross_kind is None else partners(count_cross, cross_kind)
    return [
        (i * count_cross + j, rows[i] * count_cross + cols[j])
        for i in range(count_down)
        for j in range(count_cross)
    ]


def facing(index, count, kind):
    ahead = (index % 2 == 0) != kind
    return ahead, jnp.where(ahead, index < count - 1, index > 0)


def beside(index, count, step):
    return (index + step >= 0) & (index + step < count)


def roll(x, amount, axis):
    return pltpu.roll(x, amount % x.shape[axis], axis)


def iota(shape, axis):
    return lax.broadcasted_iota(jnp.int32, shape, axis)


def gather(value, low, high, wx_low, wx_high, wy, wz):
    total = wx_high * high + wx_low * low
    total = total + wy * roll(value, -1, 0) + roll(wy * value, 1, 0)
    return total + wz * roll(value, -1, 1) + roll(wz * value, 1, 1)


class Rows:
    def __init__(self, *parts):
        self.parts = parts

    def place(self, x):
        for ref, first, count in self.parts:
            if first <= x < first + count:
                return ref, x - first
        raise IndexError(x)

    def __getitem__(self, x):
        ref, i = self.place(x)
        return ref[i]

    def __setitem__(self, x, value):
        ref, i = self.place(x)
        ref[i] = value


def smooth(field, gain, src, wx, wy, wz, x):
    spread = gather(field[x], field[x - 1], field[x + 1], wx[x - 1], wx[x], wy[x], wz[x])
    return KEEP * field[x] + gain[x] * (src[x] + spread)


def counted(x, rows):
    return jnp.where(lax.axis_index("down") % 2 == 0, x, rows - 1 - x)


def edge_strip(right, cols):
    return pl.ds(pl.multiple_of(jnp.where(right, cols - STRIP, 0), STRIP), STRIP)


def pack_rows(out, start, tiles, right):
    for i in range(0, len(tiles), 2):
        a, b = tiles[i], tiles[min(i + 1, len(tiles) - 1)]
        upper = iota(a.shape, 0) < STRIP // 2
        a, b = jnp.where(right, roll(a, STRIP // 2, 0), a), jnp.where(right, b, roll(b, STRIP // 2, 0))
        out[start + i // 2] = jnp.where(upper, a, b)


def unpack_row(message, start, i, right):
    tile = message[start + i // 2]
    return jnp.where(right == (i % 2 == 0), tile, roll(tile, STRIP // 2, 0))


def pack_kernel(nd, nc, rhs_hbm, kappa_hbm, mask_hbm, conduct, more, *refs):
    *messages, rhs, kappa, mask, sems = refs
    rows, cols, _ = rhs.shape
    messages = iter(messages)
    cross = lax.axis_index("cross")
    copies = [
        pltpu.make_async_copy(src, dst, sems.at[i])
        for i, (src, dst) in enumerate(((kappa_hbm, kappa), (mask_hbm, mask), (rhs_hbm, rhs)))
    ]
    for copy in copies:
        copy.start()
    copies[0].wait()
    copies[1].wait()
    for x in range(rows):
        at = counted(x, rows)
        conduct[x] = kappa[at] / (1.0 + SNOW_FACTOR * mask[at].astype(FLOAT))
    copies[2].wait()
    more[0], more[1] = conduct[DEPTH - 1], rhs[counted(DEPTH - 2, rows)]
    for kind in pairings(nd):
        near = [i if kind else rows - 1 - i for i in range(DEPTH)]
        depth = DEPTH - 1 if kind else DEPTH
        out = next(messages)
        for i, x in enumerate(near[:depth]):
            out[i] = conduct[x]
        for i, x in enumerate(near[: depth - 1]):
            out[depth + i] = rhs[counted(x, rows)]
        if kind:
            for cross_kind in pairings(nc):
                right, _ = facing(cross, nc, cross_kind)
                strip = edge_strip(right, cols)
                tiles = [conduct[x, strip, :] for x in near[: DEPTH - 1]]
                tiles += [rhs[counted(x, rows), strip, :] for x in near[: DEPTH - 2]]
                pack_rows(next(messages), 0, tiles, right)
    for cross_kind in pairings(nc):
        right, _ = facing(cross, nc, cross_kind)
        strip = edge_strip(right, cols)
        tiles = [conduct[x, strip, :] for x in range(rows)]
        tiles += [rhs[counted(x, rows), strip, :] for x in range(rows)]
        pack_rows(next(messages), 0, tiles, right)


def strip_kernel(nd, nc, even, *refs):
    cols = even.shape[1]
    count = len(pairings(nc))
    for cross_kind, own, out in zip(pairings(nc), refs[:count], refs[count:]):
        right, _ = facing(lax.axis_index("cross"), nc, cross_kind)
        strip = edge_strip(right, cols)
        rows = own.shape[0]
        out[:rows] = own[...]
        tiles = [even[i, strip, :] for i in range(DEPTH - 1)]
        tiles += [even[DEPTH + i, strip, :] for i in range(DEPTH - 2)]
        pack_rows(out, rows, tiles, right)


def fold(x):
    x = sum(x[:, i : i + LANES] for i in range(0, x.shape[1], LANES))
    return jnp.sum(x, axis=0, keepdims=True)


def swap_pairs(x, axis):
    return jnp.where(iota(x.shape, axis) % 2 == 0, roll(x, -1, axis), roll(x, 1, axis))


def pack_pairs(a, b, axis):
    even = iota(a.shape, axis) % 2 == 0
    return jnp.where(even, a, b) + swap_pairs(jnp.where(even, b, a), axis)


def unpack_pairs(x, axis):
    even = iota(x.shape, axis) % 2 == 0
    return jnp.where(even, x, roll(x, 1, axis)), jnp.where(even, roll(x, -1, axis), x)


class Frame:
    def __init__(self, nd, nc, cols, layers):
        self.cols, self.layers, self.wide = cols, layers, cols + STRIP
        self.own, self.halo = slice(0, cols), slice(cols, cols + STRIP)
        cross = lax.axis_index("cross")
        half = STRIP // 2
        self.lane = iota((self.wide, layers), 1)
        self.last_lane = self.lane == layers - 1
        col = iota((self.wide, layers), 0)
        self.col_ok = (col < jnp.where(cross < nc - 1, cols + half, cols)) | (
            col >= jnp.where(cross > 0, cols + half, self.wide)
        )
        halo_col = iota((STRIP, layers), 0)
        self.sides, self.rights = [], []
        for cross_kind in pairings(nc):
            right, valid = facing(cross, nc, cross_kind)
            start = jnp.where(right, 0, half)
            stop = jnp.where(valid, start + half, 0)
            self.sides.append((halo_col >= start) & (halo_col < stop))
            self.rights.append(right)

    def merged(self, messages, start, i):
        total = jnp.zeros((STRIP, self.layers), FLOAT)
        for side, right, message in zip(self.sides, self.rights, messages):
            total = jnp.where(side, unpack_row(message, start, i, right), total)
        return total

    def row(self, own, halo):
        return jnp.concatenate([own, halo], axis=0)

    def diagonal(self, low, here, high, valid=None):
        above = jnp.where(self.last_lane, 0.0, roll(here, -1, 1))
        below = jnp.where(self.lane == 0, 0.0, roll(here, 1, 1))
        right = roll(here, -1, 0)
        doubled = 6.0 * here + (low + high) + (right + roll(here, 1, 0)) + (above + below)
        ok = self.col_ok & (doubled > 0.0)
        if valid is not None:
            ok = ok & valid
        return doubled, jnp.where(ok, (2.0 * OMEGA) / doubled, 0.0), right, above

    def weights(self, q, gain, src, first, diag, wx, wy, wz, x, valid=None):
        here = q[x]
        doubled, gain_here, right, above = self.diagonal(q[x - 1], here, q[x + 1], valid)
        gain[x] = gain_here
        first[x] = gain_here * src[x]
        if diag is not None:
            diag[x] = 0.5 * doubled
        if wx is not None:
            wx[x] = 0.5 * (here + q[x + 1])
        if wy is not None:
            self.plane_weights(wy, wz, x, here, right, above)

    def plane_weights(self, wy, wz, x, here, right, above):
        wy[x] = 0.5 * (here + right)
        wz[x] = jnp.where(self.last_lane, 0.0, 0.5 * (here + above))


def residual(frame, src, diag, pres, wx, wy, wz, x):
    spread = gather(pres[x], pres[x - 1], pres[x + 1], wx[x - 1], wx[x], wy[x], wz[x])
    return (src[x] - diag[x] * pres[x] + spread)[frame.own]


def spans(rows):
    far = rows + DEPTH
    early = dict(
        q=(0, far), src=(0, far - 1), gain=(1, far - 1), first=(1, far - 1), diag=(1, rows),
        wx=(0, far - 2), wy=(0, rows + 2), wz=(0, rows + 2), pres=(2, rows + 2),
    )
    late = dict(
        q=(1 - DEPTH, 0), src=(2 - DEPTH, 0), gain=(2 - DEPTH, 1), first=(2 - DEPTH, 1), diag=(0, 1),
        wx=(2 - DEPTH, 0), wy=(-1, 0), wz=(-1, 0), pres=(-1, 2),
    )
    return early, late


EARLY = ("q", "src", "gain", "first", "diag", "wx", "wy", "wz", "pres")
LATE_KEPT = ("src", "gain", "wx", "wy", "wz", "pres", "q", "first")
LATE_SCRATCH = ("diag",)


def span_shape(span, wide, layers):
    return (span[1] - span[0], wide, layers)


def joined(rows, name, early_ref, late_ref):
    early, late = (d[name] for d in spans(rows))
    return Rows((early_ref, early[0], early[1] - early[0]), (late_ref, late[0], late[1] - late[0]))


def coarse_rows(pair, couples, tile_w):
    t = pair.reshape(couples, 2, tile_w, pair.shape[1])
    return pack_pairs(t[:, 0], t[:, 1], 2)


def early_kernel(nd, nc, tiles, rhs, conduct, route, even, *refs):
    rows, cols, layers = conduct.shape
    tile_w = cols // tiles
    couples = tiles // 2
    n_cross = len(pairings(nc))
    strips = refs[:n_cross]
    *arrays, res_coarse, res_row, coef, sums, touched = refs[n_cross:]
    early, _ = spans(rows)
    at = {n: Rows((r, early[n][0], r.shape[0])) for n, r in zip(EARLY, arrays)}
    q, src, gain, first, diag, wx, wy, wz, pres = (at[n] for n in EARLY)
    frame = Frame(nd, nc, cols, layers)
    own, halo = frame.own, frame.halo

    for x in range(rows):
        q[x] = frame.row(conduct[x], frame.merged(strips, 0, x))
        src[x] = frame.row(rhs[counted(x, rows)], frame.merged(strips, 0, rows + x))
    _, valid = facing(lax.axis_index("down"), nd, False)
    blank = jnp.zeros((STRIP, layers), FLOAT)
    for i in range(DEPTH):
        corner = frame.merged(strips, rows, i) if i < DEPTH - 1 else blank
        q[rows + i] = jnp.where(valid, frame.row(even[i], corner), 0.0)
    for i in range(DEPTH - 1):
        corner = frame.merged(strips, rows, DEPTH - 1 + i) if i < DEPTH - 2 else blank
        src[rows + i] = jnp.where(valid, frame.row(even[DEPTH + i], corner), 0.0)

    here = q[0]
    above = jnp.where(frame.last_lane, 0.0, roll(here, -1, 1))
    frame.plane_weights(wy, wz, 0, here, roll(here, -1, 0), above)
    wx[0] = 0.5 * (here + q[1])
    for x in range(*early["gain"]):
        frame.weights(
            q, gain, src, first,
            diag if x < rows else None,
            wx if x < early["wx"][1] else None,
            wy if x < early["wy"][1] else None,
            wz, x, valid if x >= rows else None,
        )
    for x in range(*early["pres"]):
        pres[x] = smooth(first, gain, src, wx, wy, wz, x)

    res = {x: residual(frame, src, diag, pres, wx, wy, wz, x) for x in range(3, rows)}
    res_row[...] = res[3]
    for k in range(2, rows // 2):
        res_coarse[k - 2] = coarse_rows(res[2 * k] + res[2 * k + 1], couples, tile_w)

    even_lane = iota((tile_w, layers), 1) % 2 == 0
    for t in range(couples):
        numbers = [jnp.broadcast_to(route[0:1, i : i + 1], (tile_w, layers)) for i in (2 * t, 2 * t + 1)]
        touched[t] = jnp.where(jnp.where(even_lane, *numbers) >= 0, 1.0, 0.0)

    strip_col = iota((STRIP, layers), 0)
    plane = sum(q[x][own] for x in range(rows))
    beyond = sum(q[x][halo] for x in range(rows))
    own_lane = iota((cols, layers), 1)
    low, high = strip_col < 2, strip_col >= STRIP - 2
    sums[0:1] = fold(sum(res.values()))
    sums[1:2] = fold(sum(q[x][own] for x in range(rows - 2, rows + 2)))
    sums[2:3] = fold(jnp.where(high, plane[cols - STRIP :], 0.0) + jnp.where(low, beyond, 0.0))
    sums[3:4] = fold(jnp.where(low, plane[:STRIP], 0.0) + jnp.where(high, beyond, 0.0))
    sums[4:5] = fold(jnp.where((own_lane < 2) | (own_lane >= layers - 2), plane, 0.0))

    packs = rows // 4
    by_row = [
        coarse_rows(0.125 * (q[2 * k][own] + q[2 * k + 1][own]), couples, tile_w)
        for k in range(rows // 2)
    ]
    con = [pack_pairs(by_row[k], by_row[k + packs], 1) for k in range(packs)]
    shape = (couples, tile_w, layers)
    tile_col, tile_lane = iota(shape, 1), iota(shape, 2)
    even_col = tile_col % 2 == 0
    y_end, y_start = tile_col >= tile_w - 2, tile_col < 2
    z_end, z_start = tile_lane >= layers - 2, tile_lane < 2
    for k in range(packs - 1):
        coef[3 * packs + 2 + k] = 2.0 * (con[k] + con[k + 1])
    middle = 2.0 * (con[packs - 1] + roll(con[0], -1, 1))
    coef[3 * packs] = jnp.where(even_col, middle, 0.0)
    coef[3 * packs + 1] = jnp.where(even_col, 0.0, roll(middle, 1, 1))
    for k in range(packs):
        c = con[k]
        y_high = jnp.where(y_end, 0.0, roll(c, -2, 1))
        z_high = jnp.where(z_end, 0.0, roll(c, -2, 2))
        y_low = jnp.where(y_start, 0.0, roll(c, 2, 1))
        z_low = jnp.where(z_start, 0.0, roll(c, 2, 2))
        total = 6.0 * c + (y_high + y_low) + (z_high + z_low)
        if k > 0:
            total = total + con[k - 1]
        else:
            total = total + jnp.where(even_col, 0.0, roll(con[packs - 1], 1, 1))
        if k < packs - 1:
            total = total + con[k + 1]
        else:
            total = total + jnp.where(even_col, roll(con[0], -1, 1), 0.0)
        total = 2.0 * total
        coef[k] = OMEGA / jnp.where(total > 0.0, total, 1.0)
        coef[packs + k] = jnp.where(y_end, 0.0, 2.0 * (c + y_high))
        coef[2 * packs + k] = jnp.where(z_end, 0.0, 2.0 * (c + z_high))


def late_kernel(nd, nc, tiles, rows, more, odd, *refs):
    n_cross = len(pairings(nc)) if len(pairings(nd)) > 1 else 0
    corners = refs[:n_cross]
    n_in = n_cross + len(EARLY) + 5
    early_refs = dict(zip(EARLY, refs[n_cross:]))
    res_coarse, res_row, coef, sums, touched = refs[n_in - 5 : n_in]
    names = LATE_KEPT + ("fix", "near", "far", "chunks") + LATE_SCRATCH
    late_refs = dict(zip(names, refs[n_in:]))
    fix_out, near_out, far_out, chunks = (late_refs[n] for n in ("fix", "near", "far", "chunks"))
    wide, layers = early_refs["q"].shape[1:]
    cols = wide - STRIP
    tile_w = cols // tiles
    couples = tiles // 2
    down = lax.axis_index("down")
    even = down % 2 == 0
    q, src, gain, first, diag, wx, wy, wz, pres = (
        joined(rows, n, early_refs[n], late_refs[n]) for n in EARLY
    )
    frame = Frame(nd, nc, cols, layers)
    _, late = spans(rows)

    valid = beside(down, nd, jnp.where(even, -1, 1))
    for i in range(DEPTH - 1):
        q[-1 - i] = jnp.where(valid, frame.row(odd[i], frame.merged(corners, 0, i)), 0.0)
    for i in range(DEPTH - 2):
        corner = frame.merged(corners, 0, DEPTH - 1 + i)
        src[-1 - i] = jnp.where(valid, frame.row(odd[DEPTH - 1 + i], corner), 0.0)
    for x in range(*late["gain"]):
        frame.weights(
            q, gain, src, first,
            diag if x == 0 else None,
            wx if x < 0 else None,
            wy if x == -1 else None,
            wz, x, valid if x < 0 else None,
        )
    for x in range(*late["pres"]):
        pres[x] = smooth(first, gain, src, wx, wy, wz, x)
    res = [residual(frame, src, diag, pres, wx, wy, wz, x) for x in range(3)]
    res.append(res_row[...])

    res_total = sums[0:1] + fold(res[0] + res[1] + res[2])
    link_odd = fold(sum(q[x][frame.own] for x in range(-2, 2)))
    link_even, link_cross, link_back, ends = (sums[i : i + 1] for i in range(1, 5))
    outflow = link_even + link_odd + link_cross + link_back + ends
    link_down = jnp.where(even, link_even, link_odd)
    lines = jnp.concatenate([res_total, 0.25 * link_down, 0.25 * link_cross, 0.25 * outflow])
    lines = jnp.sum(lines, axis=1, keepdims=True)
    line = iota((1, LANES), 1)
    summary = jnp.where(
        line == 0, lines[0:1], jnp.where(line == 1, lines[1:2], jnp.where(line == 2, lines[2:3], lines[3:4]))
    )

    packs = rows // 4
    by_row = [coarse_rows(res[2 * k] + res[2 * k + 1], couples, tile_w) for k in range(2)]
    by_row += [res_coarse[k] for k in range(rows // 2 - 2)]
    r = [pack_pairs(by_row[k], by_row[k + packs], 1) for k in range(packs)]
    middle_low, middle_high = coef[3 * packs], coef[3 * packs + 1]
    fix = [coef[k] * r[k] for k in range(packs)]
    for _ in range(BLOCK_SWEEPS - 1):
        updated = []
        for k in range(packs):
            value, link_y, link_z = fix[k], coef[packs + k], coef[2 * packs + k]
            acc = r[k] + link_y * roll(value, -2, 1) + roll(link_y * value, 2, 1)
            acc = acc + link_z * roll(value, -2, 2) + roll(link_z * value, 2, 2)
            if k > 0:
                acc = acc + coef[3 * packs + 1 + k] * fix[k - 1]
            else:
                acc = acc + middle_high * roll(fix[packs - 1], 1, 1)
            if k < packs - 1:
                acc = acc + coef[3 * packs + 2 + k] * fix[k + 1]
            else:
                acc = acc + middle_low * roll(fix[0], -1, 1)
            updated.append(KEEP * value + coef[k] * acc)
        fix = updated
    fix = [jnp.where(touched[...] > 0.0, f, 0.0) for f in fix]
    for k in range(packs):
        fix_out[k] = fix[k]

    parts = [unpack_pairs(fix[k % packs], 1)[k // packs] for k in range(rows // 2)]
    sub = iota((tile_w, layers), 0) % couples

    def rim(row):
        packed = parts[row][0]
        for t in range(1, couples):
            packed = jnp.where(sub == t, parts[row][t], packed)
        return packed

    near_out[...] = rim(rows // 2 - 1)
    far_out[2 * cols :] = rim(0)
    far_out[:cols], far_out[cols : 2 * cols] = more[0], more[1]

    chunks[pl.ds(LINES, nd * nc, stride=CHUNK), :] = jnp.broadcast_to(summary, (nd * nc, LANES))
    cross = lax.axis_index("cross")
    me = down * nc + cross
    odd_step = jnp.where(even, -1, 1)
    for dy in (-1, 1):
        at_couple, at_col = (0, 0) if dy < 0 else (couples - 1, tile_w - 1)
        edge = jnp.concatenate([p[at_couple][at_col : at_col + 1] for p in parts])
        edge = unpack_pairs(edge, 1)[0 if dy < 0 else 1]
        even_lane = iota((1, layers), 1) % 2 == 0
        pairs = [jnp.where(even_lane, edge[k : k + 1], edge[k + 1 : k + 2]) for k in range(0, rows // 2, 2)]

        def put(step, lines):
            at = (me + dy + step * nc) * CHUNK
            for i, line in enumerate(lines):
                chunks[pl.ds(at + 2 * i, 1), :] = line[:, :LANES]
                chunks[pl.ds(at + 2 * i + 1, 1), :] = line[:, LANES:]

        @pl.when(beside(cross, nc, dy))
        def _(put=put, edge=edge, pairs=pairs):
            put(0, pairs)
            for k, step in ((0, odd_step), (rows // 2 - 1, -odd_step)):

                @pl.when(beside(down, nd, step))
                def _(k=k, step=step):
                    put(step, [edge[k : k + 1]])


def coarse_solve(totals, outflow, link_down, link_up, link_cross):
    nc = len(totals)

    def operate(v):
        out = []
        for c in range(nc):
            image = outflow[c] * v[c] - link_down[c] * roll(v[c], -1, 0) - link_up[c] * roll(v[c], 1, 0)
            if c < nc - 1:
                image = image - link_cross[c] * v[c + 1]
            if c > 0:
                image = image - link_cross[c - 1] * v[c - 1]
            out.append(image)
        return out

    def dot(a, b):
        return jnp.sum(sum(x * y for x, y in zip(a, b)), axis=0, keepdims=True)

    answer = [jnp.zeros_like(t) for t in totals]
    resid = search = totals
    norm = dot(totals, totals)
    for step in range(COARSE_ITERS):
        image = operate(search)
        alpha = norm / dot(search, image)
        answer = [a + alpha * s for a, s in zip(answer, search)]
        if step == COARSE_ITERS - 1:
            break
        resid = [r - alpha * m for r, m in zip(resid, image)]
        norm_next = dot(resid, resid)
        beta = norm_next / norm
        search = [r + beta * s for r, s in zip(resid, search)]
        norm = norm_next
    return answer


KEPT = ("src", "gain", "wx", "wy", "wz")


def around(nd, nc, step, dy):
    row = jnp.clip(lax.axis_index("down") + step, 0, nd - 1)
    return row, jnp.clip(lax.axis_index("cross") + dy, 0, nc - 1)


def second_row(nd, nc, frame, more, q_ref, first_ref, src, gain, wx):
    valid = beside(lax.axis_index("down"), nd, jnp.where(lax.axis_index("down") % 2 == 0, -1, 1))
    q, first = Rows((q_ref, 1 - DEPTH, DEPTH - 1)), Rows((first_ref, 2 - DEPTH, DEPTH - 1))
    blank = jnp.zeros((STRIP, frame.layers), FLOAT)
    q_far = jnp.where(valid, frame.row(more[0], blank), 0.0)
    src_far = jnp.where(valid, frame.row(more[1], blank), 0.0)
    _, gain_far, _, _ = frame.diagonal(q_far, q[-3], q[-2], valid)
    here = q[-2]
    above = jnp.where(frame.last_lane, 0.0, roll(here, -1, 1))
    wy, wz = 0.5 * (here + roll(here, -1, 0)), jnp.where(frame.last_lane, 0.0, 0.5 * (here + above))
    spread = gather(first[-2], gain_far * src_far, first[-1], 0.5 * (q[-3] + here), wx[-2], wy, wz)
    return KEEP * first[-2] + gain[-2] * (src[-2] + spread)


def middle_kernel(nd, nc, tiles, got, fix, pres_early, pres_late, *refs):
    early = dict(zip(KEPT, refs))
    late = dict(zip(KEPT, refs[len(KEPT) :]))
    pres_ref, third_ref, out, bricks = refs[2 * len(KEPT) :]
    packs, couples, tile_w, layers = fix.shape
    rows, cols = 4 * packs, tiles * tile_w
    src, gain, wx, wy, wz = (joined(rows, n, early[n], late[n]) for n in KEPT)
    start = joined(rows, "pres", pres_early, pres_late)
    down, cross = lax.axis_index("down"), lax.axis_index("cross")
    own, halo = slice(0, cols), slice(cols, cols + STRIP)

    tables = [got[pl.ds(c * CHUNK + LINES, nd, stride=nc * CHUNK), :] for c in range(nc)]

    def spread_lane(table, at):
        return jnp.broadcast_to(table[:, at : at + 1], (nd, LANES))

    last = iota((nd, LANES), 0) == nd - 1
    totals = [spread_lane(t, 0) for t in tables]
    link_down = [jnp.where(last, 0.0, spread_lane(t, 1)) for t in tables]
    link_up = [roll(link, 1, 0) for link in link_down]
    link_cross = [spread_lane(t, 2) for t in tables]
    outflow = [spread_lane(t, 3) for t in tables]
    answer = coarse_solve(totals, outflow, link_down, link_up, link_cross)
    for c in range(nc):
        bricks[c] = answer[c]

    def brick(step, dy):
        row, col = around(nd, nc, step, dy)
        return jnp.concatenate([bricks[col, pl.ds(row, 1), :]] * (layers // LANES), axis=1)

    def lines(step, dy, count):
        row, col = around(nd, nc, step, dy)
        at = (row * nc + col) * CHUNK
        return [
            jnp.concatenate([got[pl.ds(at + i, 1), :], got[pl.ds(at + i + 1, 1), :]], axis=1)
            for i in range(0, count, 2)
        ]

    fine = [None] * (rows // 2)
    for k in range(packs):
        for j, part in enumerate(unpack_pairs(fix[k], 1)):
            both = unpack_pairs(part, 2)
            fine[k + j * packs] = jnp.stack(both, axis=1).reshape(cols, layers)

    half = STRIP // 2
    halo_col = iota((STRIP, layers), 0)
    right = halo_col < half
    there = (halo_col < jnp.where(cross < nc - 1, half, 0)) | (
        halo_col >= jnp.where(cross > 0, half, STRIP)
    )
    pres = Rows((pres_ref, -2, rows + 4))
    third = Rows((third_ref, 1, rows - 2))
    mine = brick(0, 0)
    side_bricks = brick(0, 1), brick(0, -1)
    side_lines = [
        [line for pair in lines(0, dy, LINES) for line in unpack_pairs(pair, 1)] for dy in (1, -1)
    ]
    for k in range(rows // 2):
        extra = jnp.where(right, *(f[k] + b for f, b in zip(side_lines, side_bricks)))
        extra = jnp.where(there, extra, 0.0)
        for x in (2 * k, 2 * k + 1):
            value = start[x]
            pres_ref[x + 2, own, :] = value[own] + (fine[k] + mine)
            pres_ref[x + 2, halo, :] = value[halo] + extra
    odd_step = jnp.where(down % 2 == 0, -1, 1)
    for step, xs in ((odd_step, (-2, -1)), (-odd_step, (rows, rows + 1))):
        valid = beside(down, nd, step)
        row = jnp.where(valid, brick(step, 0), 0.0)
        corner = jnp.where(
            right, *(lines(step, dy, 2)[0] + brick(step, dy) for dy in (1, -1))
        )
        corner = jnp.where(there & valid, corner, 0.0)
        for x in xs:
            value = start[x] if x > -2 else jnp.zeros((cols + STRIP, layers), FLOAT)
            pres_ref[x + 2, own, :] = value[own] + row
            pres_ref[x + 2, halo, :] = value[halo] + corner

    for x in range(1, rows - 1):
        third[x] = smooth(pres, gain, src, wx, wy, wz, x)
    for x in range(2, rows - 2):
        out[counted(x, rows) - 2] = smooth(third, gain, src, wx, wy, wz, x)[own]


def last_kernel(nd, nc, tiles, near, far, q_late, first_late, pres_mid, third_mid, out_mid, *refs):
    early = dict(zip(KEPT, refs))
    late = dict(zip(KEPT, refs[len(KEPT) :]))
    out, pres_edge, third_edge, out_edge, sems = refs[2 * len(KEPT) :]
    rows, cols, layers = out.shape
    src, gain, wx, wy, wz = (joined(rows, n, early[n], late[n]) for n in KEPT)
    tile_w = cols // tiles
    couples = tiles // 2
    down = lax.axis_index("down")
    own, halo = slice(0, cols), slice(cols, cols + STRIP)
    copy_mid = pltpu.make_async_copy(out_mid, out.at[pl.ds(2, rows - 4)], sems.at[0])
    copy_mid.start()

    def unpack(packed):
        sub = iota((tile_w, layers), 0) % couples
        parts = []
        for t in range(couples):
            tall = jnp.where(sub == t, packed, 0.0)
            for s in range(couples):
                if s != t:
                    tall = tall + jnp.where(sub == s, roll(packed, s - t, 0), 0.0)
            parts += unpack_pairs(tall, 1)
        return jnp.concatenate(parts, axis=0)

    odd_step = jnp.where(down % 2 == 0, -1, 1)
    more = far[:cols], far[cols : 2 * cols]
    even_rim, odd_rim = near[...], far[2 * cols :]
    pres = Rows((pres_edge, -2, 2), (pres_mid.at[pl.ds(2, rows)], 0, rows), (pres_edge.at[pl.ds(2, 2)], rows, 2))
    third = Rows((third_edge, -1, 2), (third_mid, 1, rows - 2), (third_edge.at[pl.ds(2, 2)], rows - 1, 2))
    for step, rim, at, mid in ((odd_step, odd_rim, 0, 0), (-odd_step, even_rim, 2, rows + 2)):
        extra = jnp.where(beside(down, nd, step), unpack(rim), 0.0)
        for i in (0, 1):
            pres_edge[at + i, own, :] = pres_mid[mid + i, own, :] + extra
            pres_edge[at + i, halo, :] = pres_mid[mid + i, halo, :]
    frame = Frame(nd, nc, cols, layers)
    second = second_row(nd, nc, frame, more, q_late, first_late, src, gain, wx)
    pres_edge[0] = pres_edge[0] + second
    for x in (-1, 0, rows - 1, rows):
        third[x] = smooth(pres, gain, src, wx, wy, wz, x)
    copies = [copy_mid]
    for side, xs in enumerate(((0, 1), (rows - 2, rows - 1))):
        for x in xs:
            at = counted(x, rows)
            at = jnp.where(at < 2, at, at - (rows - 4))
            out_edge[at] = smooth(third, gain, src, wx, wy, wz, x)[own]
    for side, at in enumerate((0, rows - 2)):
        copy = pltpu.make_async_copy(out_edge.at[pl.ds(2 * side, 2)], out.at[pl.ds(at, 2)], sems.at[1 + side])
        copy.start()
        copies.append(copy)
    for copy in copies:
        copy.wait()


def whole(*shape):
    return jax.ShapeDtypeStruct(shape, FLOAT)


def call(kernel, out_shape, spaces, scratch=(), vmem_bytes=VMEM_BYTES, out_space=pltpu.VMEM):
    return pl.pallas_call(
        kernel,
        out_shape=out_shape,
        in_specs=[pl.BlockSpec(memory_space=s) for s in spaces],
        out_specs=jax.tree.map(lambda _: pl.BlockSpec(memory_space=out_space), out_shape),
        scratch_shapes=list(scratch),
        compiler_params=pltpu.CompilerParams(vmem_limit_bytes=vmem_bytes),
    )


def body(nd, nc, right_side, kappa, band_mask, tile_route):
    rows, cols, layers = right_side.shape
    tiles = tile_route.shape[1]
    axes = ("down", "cross")
    wide = cols + STRIP
    block = whole(rows, cols, layers)
    vmem = pltpu.VMEM
    early, late = spans(rows)

    shapes, perms = [], []
    for kind in pairings(nd):
        shapes.append(whole(2 * DEPTH - (3 if kind else 1), cols, layers))
        perms.append(pairs_of(nd, nc, kind, None))
        if kind:
            for cross_kind in pairings(nc):
                shapes.append(whole(CORNER, STRIP, layers))
                perms.append(pairs_of(nd, nc, kind, cross_kind))
    strips = [whole(rows, STRIP, layers) for _ in pairings(nc)]
    packs, couples, tile_w = rows // 4, tiles // 2, cols // tiles
    tile_shape = (couples, tile_w, layers)
    conduct, more, *messages = call(
        functools.partial(pack_kernel, nd, nc),
        [block, whole(2, cols, layers)] + shapes + strips,
        [pltpu.HBM] * 3,
        scratch=[
            pltpu.VMEM((rows, cols, layers), FLOAT),
            pltpu.VMEM((rows, cols, layers), FLOAT),
            pltpu.VMEM((rows, cols, layers), band_mask.dtype),
            pltpu.SemaphoreType.DMA((3,)),
        ],
        vmem_bytes=53 * 1024 * 1024,
    )(right_side, kappa, band_mask)

    received = [lax.ppermute(m, axes, p) for m, p in zip(messages, perms)]
    even, odd = received[0], received[1:]
    if strips:
        strips = call(
            functools.partial(strip_kernel, nd, nc),
            [whole(rows + CORNER, STRIP, layers) for _ in strips],
            [vmem] * (1 + len(strips)),
        )(even, *messages[len(perms) :])
        strips = [
            lax.ppermute(m, axes, pairs_of(nd, nc, None, cross_kind))
            for m, cross_kind in zip(strips, pairings(nc))
        ]
    if not odd:
        odd = [jnp.zeros((2 * DEPTH - 3, cols, layers), FLOAT)]

    first_part = call(
        functools.partial(early_kernel, nd, nc, tiles),
        [whole(*span_shape(early[n], wide, layers)) for n in EARLY]
        + [
            whole(rows // 2 - 2, *tile_shape),
            whole(cols, layers),
            whole(4 * packs + 1, *tile_shape),
            whole(5, LANES),
            whole(*tile_shape),
        ],
        [vmem] * (4 + len(strips)),
    )(right_side, conduct, tile_route, even, *strips)
    *late_arrays, fix, near, far, chunks = call(
        functools.partial(late_kernel, nd, nc, tiles, rows),
        [whole(*span_shape(late[n], wide, layers)) for n in LATE_KEPT]
        + [
            whole(packs, *tile_shape),
            whole(tile_w, layers),
            whole(2 * cols + tile_w, layers),
            whole(nd * nc * CHUNK, LANES),
        ],
        [vmem] * (1 + len(odd) + len(first_part)),
        scratch=[pltpu.VMEM(span_shape(late[n], wide, layers), FLOAT) for n in LATE_SCRATCH],
    )(more, *odd, *first_part)
    early_arrays = dict(zip(EARLY, first_part))
    late_arrays = dict(zip(LATE_KEPT, late_arrays))
    kept = [d[n] for d in (early_arrays, late_arrays) for n in KEPT]

    chunks = chunks.reshape(nd * nc, CHUNK, 1, LANES)
    arrived = lax.all_to_all(chunks, axes, 0, 0, tiled=True).reshape(nd * nc * CHUNK, LANES)
    far = lax.ppermute(far, axes, pairs_of(nd, nc, True, None))
    near = lax.ppermute(near, axes, pairs_of(nd, nc, False, None))
    middle = call(
        functools.partial(middle_kernel, nd, nc, tiles),
        [
            whole(rows + 4, wide, layers),
            whole(rows - 2, wide, layers),
            whole(rows - 4, cols, layers),
        ],
        [vmem] * (4 + len(kept)),
        scratch=[pltpu.VMEM((nc, nd, LANES), FLOAT)],
    )(arrived, fix, early_arrays["pres"], late_arrays["pres"], *kept)
    return call(
        functools.partial(last_kernel, nd, nc, tiles),
        block,
        [vmem] * (7 + len(kept)),
        scratch=[
            pltpu.VMEM((4, wide, layers), FLOAT),
            pltpu.VMEM((4, wide, layers), FLOAT),
            pltpu.VMEM((4, cols, layers), FLOAT),
            pltpu.SemaphoreType.DMA((3,)),
        ],
        out_space=pltpu.HBM,
    )(near, far, late_arrays["q"], late_arrays["first"], *middle, *kept)


def solution(mesh):
    return jax.shard_map(
        functools.partial(body, mesh.shape["down"], mesh.shape["cross"]),
        mesh=mesh,
        in_specs=(
            P("down", "cross", None),
            P("down", "cross", None),
            P("down", "cross", None),
            P("down", "cross"),
        ),
        out_specs=P("down", "cross", None),
        check_vma=False,
    )
```

```python
import functools

import jax
import jax.numpy as jnp
from jax import lax
from jax.experimental import pallas as pl
from jax.experimental.pallas import tpu as pltpu
from jax.sharding import PartitionSpec as P

BLOCK_SWEEPS = 4
COARSE_ITERS = 12
OMEGA = 0.8
KEEP = 1.0 - OMEGA
SNOW_FACTOR = 3.0

DEPTH = 3
CORNER = DEPTH
STRIP = 8
LANES = 128
CHUNK = 2
FLOAT = jnp.float32
VMEM_BYTES = 24 * 1024 * 1024


def partners(count, odd):
    found = []
    for i in range(count):
        j = ((i + 1) ^ 1) - 1 if odd else i ^ 1
        found.append(j if 0 <= j < count else i)
    return found


def pairings(count):
    return [k for k in (False, True) if any(j != i for i, j in enumerate(partners(count, k)))]


def pairs_of(count_down, count_cross, down_kind, cross_kind):
    rows = list(range(count_down)) if down_kind is None else partners(count_down, down_kind)
    cols = list(range(count_cross)) if cross_kind is None else partners(count_cross, cross_kind)
    return [
        (i * count_cross + j, rows[i] * count_cross + cols[j])
        for i in range(count_down)
        for j in range(count_cross)
    ]


def facing(index, count, kind):
    ahead = (index % 2 == 0) != kind
    return ahead, jnp.where(ahead, index < count - 1, index > 0)


def beside(index, count, step):
    return (index + step >= 0) & (index + step < count)


def roll(x, amount, axis):
    return pltpu.roll(x, amount % x.shape[axis], axis)


def iota(shape, axis):
    return lax.broadcasted_iota(jnp.int32, shape, axis)


def gather(value, low, high, wx_low, wx_high, wy, wz):
    total = wx_high * high + wx_low * low
    total = total + wy * roll(value, -1, 0) + roll(wy * value, 1, 0)
    return total + wz * roll(value, -1, 1) + roll(wz * value, 1, 1)


class Rows:
    def __init__(self, *parts):
        self.parts = parts

    def place(self, x):
        for ref, first, count in self.parts:
            if first <= x < first + count:
                return ref, x - first
        raise IndexError(x)

    def __getitem__(self, x):
        ref, i = self.place(x)
        return ref[i]

    def __setitem__(self, x, value):
        ref, i = self.place(x)
        ref[i] = value


def smooth(field, gain, src, wx, wy, wz, x):
    spread = gather(field[x], field[x - 1], field[x + 1], wx[x - 1], wx[x], wy[x], wz[x])
    return KEEP * field[x] + gain[x] * (src[x] + spread)


def counted(x, rows):
    return jnp.where(lax.axis_index("down") % 2 == 0, x, rows - 1 - x)


def edge_strip(right, cols):
    return pl.ds(pl.multiple_of(jnp.where(right, cols - STRIP, 0), STRIP), STRIP)


def pack_rows(out, start, tiles, right):
    for i in range(0, len(tiles), 2):
        a, b = tiles[i], tiles[min(i + 1, len(tiles) - 1)]
        upper = iota(a.shape, 0) < STRIP // 2
        a, b = jnp.where(right, roll(a, STRIP // 2, 0), a), jnp.where(right, b, roll(b, STRIP // 2, 0))
        out[start + i // 2] = jnp.where(upper, a, b)


def unpack_row(message, start, i, right):
    tile = message[start + i // 2]
    return jnp.where(right == (i % 2 == 0), tile, roll(tile, STRIP // 2, 0))


def pack_kernel(nd, nc, rhs_hbm, kappa_hbm, mask_hbm, conduct, *refs):
    *messages, rhs, kappa, mask, sems = refs
    rows, cols, _ = rhs.shape
    messages = iter(messages)
    cross = lax.axis_index("cross")
    copies = [
        pltpu.make_async_copy(src, dst, sems.at[i])
        for i, (src, dst) in enumerate(((kappa_hbm, kappa), (mask_hbm, mask), (rhs_hbm, rhs)))
    ]
    for copy in copies:
        copy.start()
    copies[0].wait()
    copies[1].wait()
    for x in range(rows):
        at = counted(x, rows)
        conduct[x] = kappa[at] / (1.0 + SNOW_FACTOR * mask[at].astype(FLOAT))
    copies[2].wait()
    for kind in pairings(nd):
        near = [i if kind else rows - 1 - i for i in range(DEPTH)]
        out = next(messages)
        for i, x in enumerate(near):
            out[i] = conduct[x]
        for i, x in enumerate(near[:-1]):
            out[DEPTH + i] = rhs[counted(x, rows)]
        if kind:
            for cross_kind in pairings(nc):
                right, _ = facing(cross, nc, cross_kind)
                strip = edge_strip(right, cols)
                tiles = [conduct[x, strip, :] for x in near]
                tiles += [rhs[counted(x, rows), strip, :] for x in near[:-1]]
                pack_rows(next(messages), 0, tiles, right)
    for cross_kind in pairings(nc):
        right, _ = facing(cross, nc, cross_kind)
        strip = edge_strip(right, cols)
        tiles = [conduct[x, strip, :] for x in range(rows)]
        tiles += [rhs[counted(x, rows), strip, :] for x in range(rows)]
        pack_rows(next(messages), 0, tiles, right)


def strip_kernel(nd, nc, even, *refs):
    cols = even.shape[1]
    count = len(pairings(nc))
    for cross_kind, own, out in zip(pairings(nc), refs[:count], refs[count:]):
        right, _ = facing(lax.axis_index("cross"), nc, cross_kind)
        strip = edge_strip(right, cols)
        rows = own.shape[0]
        out[:rows] = own[...]
        tiles = [even[i, strip, :] for i in range(2 * DEPTH - 1)]
        pack_rows(out, rows, tiles, right)


def fold(x):
    x = sum(x[:, i : i + LANES] for i in range(0, x.shape[1], LANES))
    return jnp.sum(x, axis=0, keepdims=True)


def swap_pairs(x, axis):
    return jnp.where(iota(x.shape, axis) % 2 == 0, roll(x, -1, axis), roll(x, 1, axis))


def pack_pairs(a, b, axis):
    even = iota(a.shape, axis) % 2 == 0
    return jnp.where(even, a, b) + swap_pairs(jnp.where(even, b, a), axis)


def unpack_pairs(x, axis):
    even = iota(x.shape, axis) % 2 == 0
    return jnp.where(even, x, roll(x, 1, axis)), jnp.where(even, roll(x, -1, axis), x)


class Frame:
    def __init__(self, nd, nc, cols, layers):
        self.cols, self.layers, self.wide = cols, layers, cols + STRIP
        self.own, self.halo = slice(0, cols), slice(cols, cols + STRIP)
        cross = lax.axis_index("cross")
        half = STRIP // 2
        self.lane = iota((self.wide, layers), 1)
        self.last_lane = self.lane == layers - 1
        col = iota((self.wide, layers), 0)
        self.col_ok = (col < jnp.where(cross < nc - 1, cols + half, cols)) | (
            col >= jnp.where(cross > 0, cols + half, self.wide)
        )
        halo_col = iota((STRIP, layers), 0)
        self.sides, self.rights = [], []
        for cross_kind in pairings(nc):
            right, valid = facing(cross, nc, cross_kind)
            start = jnp.where(right, 0, half)
            stop = jnp.where(valid, start + half, 0)
            self.sides.append((halo_col >= start) & (halo_col < stop))
            self.rights.append(right)

    def merged(self, messages, start, i):
        total = jnp.zeros((STRIP, self.layers), FLOAT)
        for side, right, message in zip(self.sides, self.rights, messages):
            total = jnp.where(side, unpack_row(message, start, i, right), total)
        return total

    def row(self, own, halo):
        return jnp.concatenate([own, halo], axis=0)

    def diagonal(self, low, here, high, valid=None):
        above = jnp.where(self.last_lane, 0.0, roll(here, -1, 1))
        below = jnp.where(self.lane == 0, 0.0, roll(here, 1, 1))
        right = roll(here, -1, 0)
        doubled = 6.0 * here + (low + high) + (right + roll(here, 1, 0)) + (above + below)
        ok = self.col_ok & (doubled > 0.0)
        if valid is not None:
            ok = ok & valid
        return doubled, jnp.where(ok, (2.0 * OMEGA) / doubled, 0.0), right, above

    def weights(self, q, gain, src, first, diag, wx, wy, wz, x, valid=None):
        here = q[x]
        doubled, gain_here, right, above = self.diagonal(q[x - 1], here, q[x + 1], valid)
        gain[x] = gain_here
        first[x] = gain_here * src[x]
        if diag is not None:
            diag[x] = 0.5 * doubled
        if wx is not None:
            wx[x] = 0.5 * (here + q[x + 1])
        if wy is not None:
            self.plane_weights(wy, wz, x, here, right, above)

    def plane_weights(self, wy, wz, x, here, right, above):
        wy[x] = 0.5 * (here + right)
        wz[x] = jnp.where(self.last_lane, 0.0, 0.5 * (here + above))


def residual(frame, src, diag, pres, wx, wy, wz, x):
    spread = gather(pres[x], pres[x - 1], pres[x + 1], wx[x - 1], wx[x], wy[x], wz[x])
    return (src[x] - diag[x] * pres[x] + spread)[frame.own]


def spans(rows):
    early = dict(
        q=(0, rows + DEPTH), src=(0, rows + DEPTH - 1), gain=(1, rows + DEPTH - 1),
        first=(1, rows + DEPTH - 1), diag=(1, rows), wx=(0, rows + 1), wy=(0, rows + 1),
        wz=(0, rows + 1), pres=(2, rows + 1),
    )
    late = dict(
        q=(-DEPTH, 0), src=(1 - DEPTH, 0), gain=(1 - DEPTH, 1), first=(1 - DEPTH, 1), diag=(0, 1),
        wx=(1 - DEPTH, 0), wy=(-1, 0), wz=(-1, 0), pres=(-1, 2),
    )
    return early, late


EARLY = ("q", "src", "gain", "first", "diag", "wx", "wy", "wz", "pres")
LATE_KEPT = ("src", "gain", "wx", "wy", "wz", "pres")
LATE_SCRATCH = ("q", "first", "diag")


def span_shape(span, wide, layers):
    return (span[1] - span[0], wide, layers)


def joined(rows, name, early_ref, late_ref):
    early, late = (d[name] for d in spans(rows))
    return Rows((early_ref, early[0], early[1] - early[0]), (late_ref, late[0], late[1] - late[0]))


def coarse_rows(pair, couples, tile_w):
    t = pair.reshape(couples, 2, tile_w, pair.shape[1])
    return pack_pairs(t[:, 0], t[:, 1], 2)


def early_kernel(nd, nc, tiles, rhs, conduct, route, even, *refs):
    rows, cols, layers = conduct.shape
    tile_w = cols // tiles
    couples = tiles // 2
    n_cross = len(pairings(nc))
    strips = refs[:n_cross]
    *arrays, res_coarse, res_row, coef, sums, touched = refs[n_cross:]
    early, _ = spans(rows)
    at = {n: Rows((r, early[n][0], r.shape[0])) for n, r in zip(EARLY, arrays)}
    q, src, gain, first, diag, wx, wy, wz, pres = (at[n] for n in EARLY)
    frame = Frame(nd, nc, cols, layers)
    own, halo = frame.own, frame.halo

    for x in range(rows):
        q[x] = frame.row(conduct[x], frame.merged(strips, 0, x))
        src[x] = frame.row(rhs[counted(x, rows)], frame.merged(strips, 0, rows + x))
    _, valid = facing(lax.axis_index("down"), nd, False)
    for i in range(DEPTH):
        q[rows + i] = jnp.where(valid, frame.row(even[i], frame.merged(strips, rows, i)), 0.0)
    for i in range(DEPTH - 1):
        corner = frame.merged(strips, rows, DEPTH + i)
        src[rows + i] = jnp.where(valid, frame.row(even[DEPTH + i], corner), 0.0)

    here = q[0]
    above = jnp.where(frame.last_lane, 0.0, roll(here, -1, 1))
    frame.plane_weights(wy, wz, 0, here, roll(here, -1, 0), above)
    wx[0] = 0.5 * (here + q[1])
    for x in range(*early["gain"]):
        frame.weights(
            q, gain, src, first,
            diag if x < rows else None,
            wx if x < early["wx"][1] else None,
            wy if x < early["wy"][1] else None,
            wz, x, valid if x >= rows else None,
        )
    for x in range(*early["pres"]):
        pres[x] = smooth(first, gain, src, wx, wy, wz, x)

    res = {x: residual(frame, src, diag, pres, wx, wy, wz, x) for x in range(3, rows)}
    res_row[...] = res[3]
    for k in range(2, rows // 2):
        res_coarse[k - 2] = coarse_rows(res[2 * k] + res[2 * k + 1], couples, tile_w)

    even_lane = iota((tile_w, layers), 1) % 2 == 0
    for t in range(couples):
        numbers = [jnp.broadcast_to(route[0:1, i : i + 1], (tile_w, layers)) for i in (2 * t, 2 * t + 1)]
        touched[t] = jnp.where(jnp.where(even_lane, *numbers) >= 0, 1.0, 0.0)

    strip_col = iota((STRIP, layers), 0)
    plane = sum(q[x][own] for x in range(rows))
    beyond = sum(q[x][halo] for x in range(rows))
    own_lane = iota((cols, layers), 1)
    low, high = strip_col < 2, strip_col >= STRIP - 2
    sums[0:1] = fold(sum(res.values()))
    sums[1:2] = fold(sum(q[x][own] for x in range(rows - 2, rows + 2)))
    sums[2:3] = fold(jnp.where(high, plane[cols - STRIP :], 0.0) + jnp.where(low, beyond, 0.0))
    sums[3:4] = fold(jnp.where(low, plane[:STRIP], 0.0) + jnp.where(high, beyond, 0.0))
    sums[4:5] = fold(jnp.where((own_lane < 2) | (own_lane >= layers - 2), plane, 0.0))

    packs = rows // 4
    by_row = [
        coarse_rows(0.125 * (q[2 * k][own] + q[2 * k + 1][own]), couples, tile_w)
        for k in range(rows // 2)
    ]
    con = [pack_pairs(by_row[k], by_row[k + packs], 1) for k in range(packs)]
    shape = (couples, tile_w, layers)
    tile_col, tile_lane = iota(shape, 1), iota(shape, 2)
    even_col = tile_col % 2 == 0
    y_end, y_start = tile_col >= tile_w - 2, tile_col < 2
    z_end, z_start = tile_lane >= layers - 2, tile_lane < 2
    for k in range(packs - 1):
        coef[3 * packs + 2 + k] = 2.0 * (con[k] + con[k + 1])
    middle = 2.0 * (con[packs - 1] + roll(con[0], -1, 1))
    coef[3 * packs] = jnp.where(even_col, middle, 0.0)
    coef[3 * packs + 1] = jnp.where(even_col, 0.0, roll(middle, 1, 1))
    for k in range(packs):
        c = con[k]
        y_high = jnp.where(y_end, 0.0, roll(c, -2, 1))
        z_high = jnp.where(z_end, 0.0, roll(c, -2, 2))
        y_low = jnp.where(y_start, 0.0, roll(c, 2, 1))
        z_low = jnp.where(z_start, 0.0, roll(c, 2, 2))
        total = 6.0 * c + (y_high + y_low) + (z_high + z_low)
        if k > 0:
            total = total + con[k - 1]
        else:
            total = total + jnp.where(even_col, 0.0, roll(con[packs - 1], 1, 1))
        if k < packs - 1:
            total = total + con[k + 1]
        else:
            total = total + jnp.where(even_col, roll(con[0], -1, 1), 0.0)
        total = 2.0 * total
        coef[k] = OMEGA / jnp.where(total > 0.0, total, 1.0)
        coef[packs + k] = jnp.where(y_end, 0.0, 2.0 * (c + y_high))
        coef[2 * packs + k] = jnp.where(z_end, 0.0, 2.0 * (c + z_high))


def late_kernel(nd, nc, tiles, rows, odd, *refs):
    n_cross = len(pairings(nc)) if len(pairings(nd)) > 1 else 0
    corners = refs[:n_cross]
    n_in = n_cross + len(EARLY) + 5
    early_refs = dict(zip(EARLY, refs[n_cross:]))
    res_coarse, res_row, coef, sums, touched = refs[n_in - 5 : n_in]
    names = LATE_KEPT + ("fix", "near", "far", "chunks_hbm") + LATE_SCRATCH + ("chunks", "sem")
    n_side = len(pairings(nc))
    sides = refs[n_in : n_in + n_side]
    late_refs = dict(zip(names, refs[n_in + n_side :]))
    fix_out, near_out, far_out = (late_refs[n] for n in ("fix", "near", "far"))
    chunks_hbm, chunks, sem = (late_refs[n] for n in ("chunks_hbm", "chunks", "sem"))
    wide, layers = early_refs["q"].shape[1:]
    cols = wide - STRIP
    tile_w = cols // tiles
    couples = tiles // 2
    down = lax.axis_index("down")
    even = down % 2 == 0
    q, src, gain, first, diag, wx, wy, wz, pres = (
        joined(rows, n, early_refs[n], late_refs[n]) for n in EARLY
    )
    frame = Frame(nd, nc, cols, layers)
    _, late = spans(rows)

    valid = beside(down, nd, jnp.where(even, -1, 1))
    for i in range(DEPTH):
        q[-1 - i] = jnp.where(valid, frame.row(odd[i], frame.merged(corners, 0, i)), 0.0)
    for i in range(DEPTH - 1):
        corner = frame.merged(corners, 0, DEPTH + i)
        src[-1 - i] = jnp.where(valid, frame.row(odd[DEPTH + i], corner), 0.0)
    for x in range(*late["gain"]):
        frame.weights(
            q, gain, src, first,
            diag if x == 0 else None,
            wx if x < 0 else None,
            wy if x == -1 else None,
            wz, x, valid if x < 0 else None,
        )
    for x in range(*late["pres"]):
        pres[x] = smooth(first, gain, src, wx, wy, wz, x)
    res = [residual(frame, src, diag, pres, wx, wy, wz, x) for x in range(3)]
    res.append(res_row[...])

    res_total = sums[0:1] + fold(res[0] + res[1] + res[2])
    link_odd = fold(sum(q[x][frame.own] for x in range(-2, 2)))
    link_even, link_cross, link_back, ends = (sums[i : i + 1] for i in range(1, 5))
    outflow = link_even + link_odd + link_cross + link_back + ends
    link_down = jnp.where(even, link_even, link_odd)
    lines = jnp.concatenate([res_total, 0.25 * link_down, 0.25 * link_cross, 0.25 * outflow])
    lines = jnp.sum(lines, axis=1, keepdims=True)
    line = iota((1, layers), 1)
    summary = jnp.zeros((1, layers), FLOAT)
    for i in range(4):
        summary = jnp.where(line == 2 * i + 1, lines[i : i + 1], summary)

    packs = rows // 4
    by_row = [coarse_rows(res[2 * k] + res[2 * k + 1], couples, tile_w) for k in range(2)]
    by_row += [res_coarse[k] for k in range(rows // 2 - 2)]
    r = [pack_pairs(by_row[k], by_row[k + packs], 1) for k in range(packs)]
    middle_low, middle_high = coef[3 * packs], coef[3 * packs + 1]
    fix = [coef[k] * r[k] for k in range(packs)]
    for _ in range(BLOCK_SWEEPS - 1):
        updated = []
        for k in range(packs):
            value, link_y, link_z = fix[k], coef[packs + k], coef[2 * packs + k]
            acc = r[k] + link_y * roll(value, -2, 1) + roll(link_y * value, 2, 1)
            acc = acc + link_z * roll(value, -2, 2) + roll(link_z * value, 2, 2)
            if k > 0:
                acc = acc + coef[3 * packs + 1 + k] * fix[k - 1]
            else:
                acc = acc + middle_high * roll(fix[packs - 1], 1, 1)
            if k < packs - 1:
                acc = acc + coef[3 * packs + 2 + k] * fix[k + 1]
            else:
                acc = acc + middle_low * roll(fix[0], -1, 1)
            updated.append(KEEP * value + coef[k] * acc)
        fix = updated
    fix = [jnp.where(touched[...] > 0.0, f, 0.0) for f in fix]
    for k in range(packs):
        fix_out[k] = fix[k]

    parts = [unpack_pairs(fix[k % packs], 1)[k // packs] for k in range(rows // 2)]
    count = nd * nc
    for i in range(CHUNK):
        part = summary[:, i * LANES : (i + 1) * LANES]
        chunks[pl.ds(i, count, stride=CHUNK), :] = jnp.broadcast_to(part, (count, LANES))
    cross = lax.axis_index("cross")
    odd_step = jnp.where(even, -1, 1)
    edges = {}
    for dy in (-1, 1):
        at_couple, at_col = (0, 0) if dy < 0 else (couples - 1, tile_w - 1)
        edge = jnp.concatenate([p[at_couple][at_col : at_col + 1] for p in parts])
        edges[dy] = edge = unpack_pairs(edge, 1)[0 if dy < 0 else 1]
        for k, step in ((0, odd_step), (rows // 2 - 1, -odd_step)):

            @pl.when(beside(cross, nc, dy) & beside(down, nd, step))
            def _(k=k, step=step, dy=dy, edge=edge):
                both = jnp.where(line % 2 == 0, edge[k : k + 1], summary)
                at = ((cross + dy) * nd + down + step) * CHUNK
                for i in range(CHUNK):
                    chunks[pl.ds(at + i, 1), :] = both[:, i * LANES : (i + 1) * LANES]

    copy = pltpu.make_async_copy(chunks, chunks_hbm, sem)
    copy.start()

    sub = iota((tile_w, layers), 0) % couples
    for out, k, x in ((far_out, 0, 1), (near_out, rows // 2 - 1, rows - 2)):
        packed = parts[k][0]
        for t in range(1, couples):
            packed = jnp.where(sub == t, parts[k][t], packed)
        out[cols:] = packed
        fine = jnp.stack(unpack_pairs(parts[k], 2), axis=1).reshape(cols, layers)
        out[:cols] = pres[x][frame.own] + fine
    for cross_kind, out in zip(pairings(nc), sides):
        right, _ = facing(cross, nc, cross_kind)
        out[: rows // 2] = jnp.where(right, edges[1], edges[-1])
    copy.wait()


def coarse_solve(totals, outflow, link_down, link_up, link_cross):
    nc = len(totals)

    def operate(v):
        out = []
        for c in range(nc):
            image = outflow[c] * v[c] - link_down[c] * roll(v[c], -1, 0) - link_up[c] * roll(v[c], 1, 0)
            if c < nc - 1:
                image = image - link_cross[c] * v[c + 1]
            if c > 0:
                image = image - link_cross[c - 1] * v[c - 1]
            out.append(image)
        return out

    def dot(a, b):
        return jnp.sum(sum(x * y for x, y in zip(a, b)), axis=0, keepdims=True)

    answer = [jnp.zeros_like(t) for t in totals]
    resid = search = totals
    norm = dot(totals, totals)
    for step in range(COARSE_ITERS):
        image = operate(search)
        alpha = norm / dot(search, image)
        answer = [a + alpha * s for a, s in zip(answer, search)]
        if step == COARSE_ITERS - 1:
            break
        resid = [r - alpha * m for r, m in zip(resid, image)]
        norm_next = dot(resid, resid)
        beta = norm_next / norm
        search = [r + beta * s for r, s in zip(resid, search)]
        norm = norm_next
    return answer


KEPT = ("src", "gain", "wx", "wy", "wz")


def around(nd, nc, step, dy):
    row = jnp.clip(lax.axis_index("down") + step, 0, nd - 1)
    return row, jnp.clip(lax.axis_index("cross") + dy, 0, nc - 1)


def fine_row(packed, couples):
    sub = iota(packed.shape, 0) % couples
    parts = []
    for t in range(couples):
        tall = jnp.where(sub == t, packed, 0.0)
        for s in range(couples):
            if s != t:
                tall = tall + jnp.where(sub == s, roll(packed, s - t, 0), 0.0)
        parts += unpack_pairs(tall, 1)
    return jnp.concatenate(parts, axis=0)


def base_kernel(nd, nc, tiles, near, fix, pres_early, pres_late, *refs):
    *sides, base = refs
    packs, couples, tile_w, layers = fix.shape
    rows, cols = 4 * packs, tiles * tile_w
    start = joined(rows, "pres", pres_early, pres_late)
    down = lax.axis_index("down")
    own, halo = slice(0, cols), slice(cols, cols + STRIP)
    frame = Frame(nd, nc, cols, layers)
    for k in range(packs):
        for j, part in enumerate(unpack_pairs(fix[k], 1)):
            both = unpack_pairs(part, 2)
            fine = jnp.stack(both, axis=1).reshape(cols, layers)
            row = k + j * packs
            edge = jnp.zeros((STRIP, layers), FLOAT)
            for place, side in zip(frame.sides, sides):
                edge = jnp.where(place, side[row : row + 1], edge)
            for x in (2 * row, 2 * row + 1):
                base[x + 2, own, :] = start[x][own] + fine
                base[x + 2, halo, :] = start[x][halo] + edge
    there = beside(down, nd, jnp.where(down % 2 == 0, 1, -1))
    rim = jnp.where(there, fine_row(near[cols:], couples), 0.0)
    base[rows + 2, own, :] = start[rows][own] + rim
    base[rows + 2, halo, :] = start[rows][halo]
    base[rows + 3, own, :] = jnp.where(there, near[:cols], 0.0)
    base[rows + 3, halo, :] = jnp.zeros((STRIP, layers), FLOAT)
    base[1] = start[-1]
    base[0] = jnp.zeros((cols + STRIP, layers), FLOAT)


def last_kernel(nd, nc, tiles, got, far, base, *refs):
    early = dict(zip(KEPT, refs))
    late = dict(zip(KEPT, refs[len(KEPT) :]))
    out, pres_ref, third_ref, new, bricks, sems = refs[2 * len(KEPT) :]
    rows, cols, layers = out.shape
    src, gain, wx, wy, wz = (joined(rows, n, early[n], late[n]) for n in KEPT)
    down, cross = lax.axis_index("down"), lax.axis_index("cross")
    own, halo = slice(0, cols), slice(cols, cols + STRIP)
    even = down % 2 == 0

    tables = [got[pl.ds(c * nd * CHUNK, nd, stride=CHUNK), :] for c in range(nc)]

    def spread_lane(table, at):
        return jnp.broadcast_to(table[:, 2 * at + 1 : 2 * at + 2], (nd, LANES))

    last = iota((nd, LANES), 0) == nd - 1
    totals = [spread_lane(t, 0) for t in tables]
    link_down = [jnp.where(last, 0.0, spread_lane(t, 1)) for t in tables]
    link_up = [roll(link, 1, 0) for link in link_down]
    link_cross = [spread_lane(t, 2) for t in tables]
    outflow = [spread_lane(t, 3) for t in tables]
    answer = coarse_solve(totals, outflow, link_down, link_up, link_cross)
    for c in range(nc):
        bricks[c] = answer[c]

    def brick(step, dy):
        row, col = around(nd, nc, step, dy)
        return jnp.concatenate([bricks[col, pl.ds(row, 1), :]] * (layers // LANES), axis=1)

    def corner_of(step, dy):
        row, col = around(nd, nc, step, dy)
        at = (col * nd + row) * CHUNK
        both = jnp.concatenate([got[pl.ds(at + i, 1), :] for i in range(CHUNK)], axis=1)
        return unpack_pairs(both, 1)[0] + brick(step, dy)

    half = STRIP // 2
    halo_col = iota((STRIP, layers), 0)
    right = halo_col < half
    there = (halo_col < jnp.where(cross < nc - 1, half, 0)) | (
        halo_col >= jnp.where(cross > 0, half, STRIP)
    )
    pres = Rows((pres_ref, -2, rows + 4))
    third = Rows((third_ref, -1, rows + 2))
    odd_step = jnp.where(even, -1, 1)
    mine = brick(0, 0)
    side = jnp.where(there, jnp.where(right, brick(0, 1), brick(0, -1)), 0.0)
    valid = beside(down, nd, odd_step)
    odd_rows = (fine_row(far[cols:], tiles // 2), far[:cols])
    odd_rows = [jnp.where(valid, f, 0.0) for f in odd_rows]
    for step, xs in ((-odd_step, (rows, rows + 1)), (odd_step, (-1, -2))):
        valid = beside(down, nd, step)
        row = jnp.where(valid, brick(step, 0), 0.0)
        corner = jnp.where(right, corner_of(step, 1), corner_of(step, -1))
        corner = jnp.where(there & valid, corner, 0.0)
        for i, x in enumerate(xs):
            value = base[x + 2, own, :] + row
            pres_ref[x + 2, own, :] = value + odd_rows[i] if x < 0 else value
            pres_ref[x + 2, halo, :] = base[x + 2, halo, :] + (0.0 if i else corner)
    for x in reversed(range(rows)):
        pres_ref[x + 2, own, :] = base[x + 2, own, :] + mine
        pres_ref[x + 2, halo, :] = base[x + 2, halo, :] + side

    copies = []
    for x in reversed(range(-1, rows + 1)):
        third[x] = smooth(pres, gain, src, wx, wy, wz, x)
        if x + 1 < rows:
            y = x + 1
            new[counted(y, rows)] = smooth(third, gain, src, wx, wy, wz, y)[own]
            if y in (rows // 2, 0):
                at = jnp.where(even, y, rows // 2 - y)
                span = pl.ds(at, rows // 2)
                copies.append(pltpu.make_async_copy(new.at[span], out.at[span], sems.at[len(copies)]))
                copies[-1].start()
    for copy in copies:
        copy.wait()


def whole(*shape):
    return jax.ShapeDtypeStruct(shape, FLOAT)


def call(kernel, out_shape, spaces, scratch=(), vmem_bytes=VMEM_BYTES, out_spaces=None):
    return pl.pallas_call(
        kernel,
        out_shape=out_shape,
        in_specs=[pl.BlockSpec(memory_space=s) for s in spaces],
        out_specs=jax.tree.map(
            lambda _, s: pl.BlockSpec(memory_space=s),
            out_shape,
            out_spaces or jax.tree.map(lambda _: pltpu.VMEM, out_shape),
        ),
        scratch_shapes=list(scratch),
        compiler_params=pltpu.CompilerParams(vmem_limit_bytes=vmem_bytes),
    )


def body(nd, nc, right_side, kappa, band_mask, tile_route):
    rows, cols, layers = right_side.shape
    tiles = tile_route.shape[1]
    axes = ("down", "cross")
    wide = cols + STRIP
    block = whole(rows, cols, layers)
    vmem = pltpu.VMEM
    early, late = spans(rows)

    shapes, perms = [], []
    for kind in pairings(nd):
        shapes.append(whole(2 * DEPTH - 1, cols, layers))
        perms.append(pairs_of(nd, nc, kind, None))
        if kind:
            for cross_kind in pairings(nc):
                shapes.append(whole(CORNER, STRIP, layers))
                perms.append(pairs_of(nd, nc, kind, cross_kind))
    strips = [whole(rows, STRIP, layers) for _ in pairings(nc)]
    packs, couples, tile_w = rows // 4, tiles // 2, cols // tiles
    tile_shape = (couples, tile_w, layers)
    conduct, *messages = call(
        functools.partial(pack_kernel, nd, nc),
        [block] + shapes + strips,
        [pltpu.HBM] * 3,
        scratch=[
            pltpu.VMEM((rows, cols, layers), FLOAT),
            pltpu.VMEM((rows, cols, layers), FLOAT),
            pltpu.VMEM((rows, cols, layers), band_mask.dtype),
            pltpu.SemaphoreType.DMA((3,)),
        ],
        vmem_bytes=54400 * 1024,
    )(right_side, kappa, band_mask)

    received = [lax.ppermute(m, axes, p) for m, p in zip(messages, perms)]
    even, odd = received[0], received[1:]
    if strips:
        strips = call(
            functools.partial(strip_kernel, nd, nc),
            [whole(rows + CORNER, STRIP, layers) for _ in strips],
            [vmem] * (1 + len(strips)),
        )(even, *messages[len(perms) :])
        strips = [
            lax.ppermute(m, axes, pairs_of(nd, nc, None, cross_kind))
            for m, cross_kind in zip(strips, pairings(nc))
        ]
    if not odd:
        odd = [jnp.zeros((2 * DEPTH - 1, cols, layers), FLOAT)]

    first_part = call(
        functools.partial(early_kernel, nd, nc, tiles),
        [whole(*span_shape(early[n], wide, layers)) for n in EARLY]
        + [
            whole(rows // 2 - 2, *tile_shape),
            whole(cols, layers),
            whole(4 * packs + 1, *tile_shape),
            whole(5, LANES),
            whole(*tile_shape),
        ],
        [vmem] * (4 + len(strips)),
    )(right_side, conduct, tile_route, even, *strips)
    late_arrays = call(
        functools.partial(late_kernel, nd, nc, tiles, rows),
        [whole(STRIP, layers) for _ in pairings(nc)]
        + [whole(*span_shape(late[n], wide, layers)) for n in LATE_KEPT]
        + [
            whole(packs, *tile_shape),
            whole(cols + tile_w, layers),
            whole(cols + tile_w, layers),
            whole(nd * nc * CHUNK, LANES),
        ],
        [vmem] * (len(odd) + len(first_part)),
        scratch=[pltpu.VMEM(span_shape(late[n], wide, layers), FLOAT) for n in LATE_SCRATCH]
        + [pltpu.VMEM((nd * nc * CHUNK, LANES), FLOAT), pltpu.SemaphoreType.DMA],
        out_spaces=[vmem] * (len(pairings(nc)) + len(LATE_KEPT) + 3) + [pltpu.HBM],
    )(*odd, *first_part)
    n_side = len(pairings(nc))
    sides, late_arrays = late_arrays[:n_side], late_arrays[n_side:]
    *late_arrays, fix, near, far, chunks = late_arrays
    early_arrays = dict(zip(EARLY, first_part))
    late_arrays = dict(zip(LATE_KEPT, late_arrays))
    kept = [d[n] for d in (early_arrays, late_arrays) for n in KEPT]

    chunks = chunks.reshape(nd * nc, CHUNK, 1, LANES)
    arrived = lax.all_to_all(chunks, ("cross", "down"), 0, 0, tiled=True).reshape(nd * nc * CHUNK, LANES)
    far = lax.ppermute(far, axes, pairs_of(nd, nc, True, None))
    near = lax.ppermute(near, axes, pairs_of(nd, nc, False, None))
    sides = [
        lax.ppermute(m, axes, pairs_of(nd, nc, None, cross_kind))
        for m, cross_kind in zip(sides, pairings(nc))
    ]
    base = call(
        functools.partial(base_kernel, nd, nc, tiles),
        whole(rows + 4, wide, layers),
        [vmem] * (4 + n_side),
    )(near, fix, early_arrays["pres"], late_arrays["pres"], *sides)
    return call(
        functools.partial(last_kernel, nd, nc, tiles),
        block,
        [vmem] * (3 + len(kept)),
        scratch=[
            pltpu.VMEM((rows + 4, wide, layers), FLOAT),
            pltpu.VMEM((rows + 2, wide, layers), FLOAT),
            pltpu.VMEM((rows, cols, layers), FLOAT),
            pltpu.VMEM((nc, nd, LANES), FLOAT),
            pltpu.SemaphoreType.DMA((2,)),
        ],
        out_spaces=pltpu.HBM,
    )(arrived, far, base, *kept)


def solution(mesh):
    return jax.shard_map(
        functools.partial(body, mesh.shape["down"], mesh.shape["cross"]),
        mesh=mesh,
        in_specs=(
            P("down", "cross", None),
            P("down", "cross", None),
            P("down", "cross", None),
            P("down", "cross"),
        ),
        out_specs=P("down", "cross", None),
        check_vma=False,
    )
```

```python
import functools

import jax
import jax.numpy as jnp
from jax import lax
from jax.experimental import pallas as pl
from jax.experimental.pallas import tpu as pltpu
from jax.sharding import PartitionSpec as P

BLOCK_SWEEPS = 4
COARSE_ITERS = 12
OMEGA = 0.8
KEEP = 1.0 - OMEGA
SNOW_FACTOR = 3.0

DEPTH = 3
CORNER = DEPTH
STRIP = 8
LANES = 128
CHUNK = 2
FLOAT = jnp.float32
VMEM_BYTES = 24 * 1024 * 1024


def partners(count, odd):
    found = []
    for i in range(count):
        j = ((i + 1) ^ 1) - 1 if odd else i ^ 1
        found.append(j if 0 <= j < count else i)
    return found


def pairings(count):
    return [k for k in (False, True) if any(j != i for i, j in enumerate(partners(count, k)))]


def pairs_of(count_down, count_cross, down_kind, cross_kind):
    rows = list(range(count_down)) if down_kind is None else partners(count_down, down_kind)
    cols = list(range(count_cross)) if cross_kind is None else partners(count_cross, cross_kind)
    return [
        (i * count_cross + j, rows[i] * count_cross + cols[j])
        for i in range(count_down)
        for j in range(count_cross)
    ]


def facing(index, count, kind):
    ahead = (index % 2 == 0) != kind
    return ahead, jnp.where(ahead, index < count - 1, index > 0)


def beside(index, count, step):
    return (index + step >= 0) & (index + step < count)


def roll(x, amount, axis):
    return pltpu.roll(x, amount % x.shape[axis], axis)


def iota(shape, axis):
    return lax.broadcasted_iota(jnp.int32, shape, axis)


def gather(value, low, high, wx_low, wx_high, wy, wz):
    total = wx_high * high + wx_low * low
    total = total + wy * roll(value, -1, 0) + roll(wy * value, 1, 0)
    return total + wz * roll(value, -1, 1) + roll(wz * value, 1, 1)


class Rows:
    def __init__(self, *parts):
        self.parts = parts

    def place(self, x):
        for ref, first, count in self.parts:
            if first <= x < first + count:
                return ref, x - first
        raise IndexError(x)

    def __getitem__(self, x):
        ref, i = self.place(x)
        return ref[i]

    def __setitem__(self, x, value):
        ref, i = self.place(x)
        ref[i] = value


def smooth(field, gain, src, wx, wy, wz, x):
    spread = gather(field[x], field[x - 1], field[x + 1], wx[x - 1], wx[x], wy[x], wz[x])
    return KEEP * field[x] + gain[x] * (src[x] + spread)


def counted(x, rows):
    return jnp.where(lax.axis_index("down") % 2 == 0, x, rows - 1 - x)


def edge_strip(right, cols):
    return pl.ds(pl.multiple_of(jnp.where(right, cols - STRIP, 0), STRIP), STRIP)


def pack_rows(out, start, tiles, right):
    for i in range(0, len(tiles), 2):
        a, b = tiles[i], tiles[min(i + 1, len(tiles) - 1)]
        upper = iota(a.shape, 0) < STRIP // 2
        a, b = jnp.where(right, roll(a, STRIP // 2, 0), a), jnp.where(right, b, roll(b, STRIP // 2, 0))
        out[start + i // 2] = jnp.where(upper, a, b)


def unpack_row(message, start, i, right):
    tile = message[start + i // 2]
    return jnp.where(right == (i % 2 == 0), tile, roll(tile, STRIP // 2, 0))


def pack_kernel(nd, nc, rhs_hbm, kappa_hbm, mask_hbm, conduct, *refs):
    *messages, rhs, kappa, mask, sems = refs
    rows, cols, _ = rhs.shape
    messages = iter(messages)
    cross = lax.axis_index("cross")
    copies = [
        pltpu.make_async_copy(src, dst, sems.at[i])
        for i, (src, dst) in enumerate(((kappa_hbm, kappa), (mask_hbm, mask), (rhs_hbm, rhs)))
    ]
    for copy in copies:
        copy.start()
    copies[0].wait()
    copies[1].wait()
    for x in range(rows):
        at = counted(x, rows)
        conduct[x] = kappa[at] / (1.0 + SNOW_FACTOR * mask[at].astype(FLOAT))
    copies[2].wait()
    for kind in pairings(nd):
        near = [i if kind else rows - 1 - i for i in range(DEPTH)]
        out = next(messages)
        for i, x in enumerate(near):
            out[i] = conduct[x]
        for i, x in enumerate(near[:-1]):
            out[DEPTH + i] = rhs[counted(x, rows)]
        if kind:
            for cross_kind in pairings(nc):
                right, _ = facing(cross, nc, cross_kind)
                strip = edge_strip(right, cols)
                tiles = [conduct[x, strip, :] for x in near]
                tiles += [rhs[counted(x, rows), strip, :] for x in near[:-1]]
                pack_rows(next(messages), 0, tiles, right)
    for cross_kind in pairings(nc):
        right, _ = facing(cross, nc, cross_kind)
        strip = edge_strip(right, cols)
        tiles = [conduct[x, strip, :] for x in range(rows)]
        tiles += [rhs[counted(x, rows), strip, :] for x in range(rows)]
        pack_rows(next(messages), 0, tiles, right)


def strip_kernel(nd, nc, even, *refs):
    cols = even.shape[1]
    count = len(pairings(nc))
    for cross_kind, own, out in zip(pairings(nc), refs[:count], refs[count:]):
        right, _ = facing(lax.axis_index("cross"), nc, cross_kind)
        strip = edge_strip(right, cols)
        rows = own.shape[0]
        out[:rows] = own[...]
        tiles = [even[i, strip, :] for i in range(2 * DEPTH - 1)]
        pack_rows(out, rows, tiles, right)


def fold(x):
    x = sum(x[:, i : i + LANES] for i in range(0, x.shape[1], LANES))
    return jnp.sum(x, axis=0, keepdims=True)


def swap_pairs(x, axis):
    return jnp.where(iota(x.shape, axis) % 2 == 0, roll(x, -1, axis), roll(x, 1, axis))


def pack_pairs(a, b, axis):
    even = iota(a.shape, axis) % 2 == 0
    return jnp.where(even, a, b) + swap_pairs(jnp.where(even, b, a), axis)


def unpack_pairs(x, axis):
    even = iota(x.shape, axis) % 2 == 0
    return jnp.where(even, x, roll(x, 1, axis)), jnp.where(even, roll(x, -1, axis), x)


class Frame:
    def __init__(self, nd, nc, cols, layers):
        self.cols, self.layers, self.wide = cols, layers, cols + STRIP
        self.own, self.halo = slice(0, cols), slice(cols, cols + STRIP)
        cross = lax.axis_index("cross")
        half = STRIP // 2
        self.lane = iota((self.wide, layers), 1)
        self.last_lane = self.lane == layers - 1
        col = iota((self.wide, layers), 0)
        self.col_ok = (col < jnp.where(cross < nc - 1, cols + half, cols)) | (
            col >= jnp.where(cross > 0, cols + half, self.wide)
        )
        halo_col = iota((STRIP, layers), 0)
        self.sides, self.rights = [], []
        for cross_kind in pairings(nc):
            right, valid = facing(cross, nc, cross_kind)
            start = jnp.where(right, 0, half)
            stop = jnp.where(valid, start + half, 0)
            self.sides.append((halo_col >= start) & (halo_col < stop))
            self.rights.append(right)

    def merged(self, messages, start, i):
        total = jnp.zeros((STRIP, self.layers), FLOAT)
        for side, right, message in zip(self.sides, self.rights, messages):
            total = jnp.where(side, unpack_row(message, start, i, right), total)
        return total

    def row(self, own, halo):
        return jnp.concatenate([own, halo], axis=0)

    def diagonal(self, low, here, high, valid=None):
        above = jnp.where(self.last_lane, 0.0, roll(here, -1, 1))
        below = jnp.where(self.lane == 0, 0.0, roll(here, 1, 1))
        right = roll(here, -1, 0)
        doubled = 6.0 * here + (low + high) + (right + roll(here, 1, 0)) + (above + below)
        ok = self.col_ok & (doubled > 0.0)
        if valid is not None:
            ok = ok & valid
        return doubled, jnp.where(ok, (2.0 * OMEGA) / doubled, 0.0), right, above

    def weights(self, q, gain, src, first, diag, wx, wy, wz, x, valid=None):
        here = q[x]
        doubled, gain_here, right, above = self.diagonal(q[x - 1], here, q[x + 1], valid)
        gain[x] = gain_here
        first[x] = gain_here * src[x]
        if diag is not None:
            diag[x] = 0.5 * doubled
        if wx is not None:
            wx[x] = 0.5 * (here + q[x + 1])
        if wy is not None:
            self.plane_weights(wy, wz, x, here, right, above)

    def plane_weights(self, wy, wz, x, here, right, above):
        wy[x] = 0.5 * (here + right)
        wz[x] = jnp.where(self.last_lane, 0.0, 0.5 * (here + above))


def residual(frame, src, diag, pres, wx, wy, wz, x):
    spread = gather(pres[x], pres[x - 1], pres[x + 1], wx[x - 1], wx[x], wy[x], wz[x])
    return (src[x] - diag[x] * pres[x] + spread)[frame.own]


def spans(rows):
    early = dict(
        q=(0, rows + DEPTH), src=(0, rows + DEPTH - 1), gain=(1, rows + DEPTH - 1),
        first=(1, rows + DEPTH - 1), diag=(1, rows), wx=(0, rows + 1), wy=(0, rows + 1),
        wz=(0, rows + 1), pres=(2, rows + 1),
    )
    late = dict(
        q=(-DEPTH, 0), src=(1 - DEPTH, 0), gain=(1 - DEPTH, 1), first=(1 - DEPTH, 1), diag=(0, 1),
        wx=(1 - DEPTH, 0), wy=(-1, 0), wz=(-1, 0), pres=(-1, 2),
    )
    return early, late


EARLY = ("q", "src", "gain", "first", "diag", "wx", "wy", "wz", "pres")
LATE_KEPT = ("src", "gain", "wx", "wy", "wz", "pres")
LATE_SCRATCH = ("q", "first", "diag")


def span_shape(span, wide, layers):
    return (span[1] - span[0], wide, layers)


def joined(rows, name, early_ref, late_ref):
    early, late = (d[name] for d in spans(rows))
    return Rows((early_ref, early[0], early[1] - early[0]), (late_ref, late[0], late[1] - late[0]))


def coarse_rows(pair, couples, tile_w):
    t = pair.reshape(couples, 2, tile_w, pair.shape[1])
    return pack_pairs(t[:, 0], t[:, 1], 2)


def early_kernel(nd, nc, tiles, rhs, conduct, route, even, *refs):
    rows, cols, layers = conduct.shape
    tile_w = cols // tiles
    couples = tiles // 2
    n_cross = len(pairings(nc))
    strips = refs[:n_cross]
    *arrays, res_coarse, res_row, coef, sums, touched = refs[n_cross:]
    early, _ = spans(rows)
    at = {n: Rows((r, early[n][0], r.shape[0])) for n, r in zip(EARLY, arrays)}
    q, src, gain, first, diag, wx, wy, wz, pres = (at[n] for n in EARLY)
    frame = Frame(nd, nc, cols, layers)
    own, halo = frame.own, frame.halo

    for x in range(rows):
        q[x] = frame.row(conduct[x], frame.merged(strips, 0, x))
        src[x] = frame.row(rhs[counted(x, rows)], frame.merged(strips, 0, rows + x))
    _, valid = facing(lax.axis_index("down"), nd, False)
    for i in range(DEPTH):
        q[rows + i] = jnp.where(valid, frame.row(even[i], frame.merged(strips, rows, i)), 0.0)
    for i in range(DEPTH - 1):
        corner = frame.merged(strips, rows, DEPTH + i)
        src[rows + i] = jnp.where(valid, frame.row(even[DEPTH + i], corner), 0.0)

    here = q[0]
    above = jnp.where(frame.last_lane, 0.0, roll(here, -1, 1))
    frame.plane_weights(wy, wz, 0, here, roll(here, -1, 0), above)
    wx[0] = 0.5 * (here + q[1])
    for x in range(*early["gain"]):
        frame.weights(
            q, gain, src, first,
            diag if x < rows else None,
            wx if x < early["wx"][1] else None,
            wy if x < early["wy"][1] else None,
            wz, x, valid if x >= rows else None,
        )
    for x in range(*early["pres"]):
        pres[x] = smooth(first, gain, src, wx, wy, wz, x)

    res = {x: residual(frame, src, diag, pres, wx, wy, wz, x) for x in range(3, rows)}
    res_row[...] = res[3]
    for k in range(2, rows // 2):
        res_coarse[k - 2] = coarse_rows(res[2 * k] + res[2 * k + 1], couples, tile_w)

    even_lane = iota((tile_w, layers), 1) % 2 == 0
    for t in range(couples):
        numbers = [jnp.broadcast_to(route[0:1, i : i + 1], (tile_w, layers)) for i in (2 * t, 2 * t + 1)]
        touched[t] = jnp.where(jnp.where(even_lane, *numbers) >= 0, 1.0, 0.0)

    strip_col = iota((STRIP, layers), 0)
    plane = sum(q[x][own] for x in range(rows))
    beyond = sum(q[x][halo] for x in range(rows))
    own_lane = iota((cols, layers), 1)
    low, high = strip_col < 2, strip_col >= STRIP - 2
    sums[0:1] = fold(sum(res.values()))
    sums[1:2] = fold(sum(q[x][own] for x in range(rows - 2, rows + 2)))
    sums[2:3] = fold(jnp.where(high, plane[cols - STRIP :], 0.0) + jnp.where(low, beyond, 0.0))
    sums[3:4] = fold(jnp.where(low, plane[:STRIP], 0.0) + jnp.where(high, beyond, 0.0))
    sums[4:5] = fold(jnp.where((own_lane < 2) | (own_lane >= layers - 2), plane, 0.0))

    packs = rows // 4
    by_row = [
        coarse_rows(0.125 * (q[2 * k][own] + q[2 * k + 1][own]), couples, tile_w)
        for k in range(rows // 2)
    ]
    con = [pack_pairs(by_row[k], by_row[k + packs], 1) for k in range(packs)]
    shape = (couples, tile_w, layers)
    tile_col, tile_lane = iota(shape, 1), iota(shape, 2)
    even_col = tile_col % 2 == 0
    y_end, y_start = tile_col >= tile_w - 2, tile_col < 2
    z_end, z_start = tile_lane >= layers - 2, tile_lane < 2
    for k in range(packs - 1):
        coef[3 * packs + 2 + k] = 2.0 * (con[k] + con[k + 1])
    middle = 2.0 * (con[packs - 1] + roll(con[0], -1, 1))
    coef[3 * packs] = jnp.where(even_col, middle, 0.0)
    coef[3 * packs + 1] = jnp.where(even_col, 0.0, roll(middle, 1, 1))
    for k in range(packs):
        c = con[k]
        y_high = jnp.where(y_end, 0.0, roll(c, -2, 1))
        z_high = jnp.where(z_end, 0.0, roll(c, -2, 2))
        y_low = jnp.where(y_start, 0.0, roll(c, 2, 1))
        z_low = jnp.where(z_start, 0.0, roll(c, 2, 2))
        total = 6.0 * c + (y_high + y_low) + (z_high + z_low)
        if k > 0:
            total = total + con[k - 1]
        else:
            total = total + jnp.where(even_col, 0.0, roll(con[packs - 1], 1, 1))
        if k < packs - 1:
            total = total + con[k + 1]
        else:
            total = total + jnp.where(even_col, roll(con[0], -1, 1), 0.0)
        total = 2.0 * total
        coef[k] = OMEGA / jnp.where(total > 0.0, total, 1.0)
        coef[packs + k] = jnp.where(y_end, 0.0, 2.0 * (c + y_high))
        coef[2 * packs + k] = jnp.where(z_end, 0.0, 2.0 * (c + z_high))


def late_kernel(nd, nc, tiles, rows, odd, *refs):
    n_cross = len(pairings(nc)) if len(pairings(nd)) > 1 else 0
    corners = refs[:n_cross]
    n_in = n_cross + len(EARLY) + 5
    early_refs = dict(zip(EARLY, refs[n_cross:]))
    res_coarse, res_row, coef, sums, touched = refs[n_in - 5 : n_in]
    names = LATE_KEPT + ("fix", "near", "far", "chunks_hbm") + LATE_SCRATCH + ("chunks", "sem")
    n_side = len(pairings(nc))
    sides = refs[n_in : n_in + n_side]
    late_refs = dict(zip(names, refs[n_in + n_side :]))
    fix_out, near_out, far_out = (late_refs[n] for n in ("fix", "near", "far"))
    chunks_hbm, chunks, sem = (late_refs[n] for n in ("chunks_hbm", "chunks", "sem"))
    wide, layers = early_refs["q"].shape[1:]
    cols = wide - STRIP
    tile_w = cols // tiles
    couples = tiles // 2
    down = lax.axis_index("down")
    even = down % 2 == 0
    q, src, gain, first, diag, wx, wy, wz, pres = (
        joined(rows, n, early_refs[n], late_refs[n]) for n in EARLY
    )
    frame = Frame(nd, nc, cols, layers)
    _, late = spans(rows)

    valid = beside(down, nd, jnp.where(even, -1, 1))
    for i in range(DEPTH):
        q[-1 - i] = jnp.where(valid, frame.row(odd[i], frame.merged(corners, 0, i)), 0.0)
    for i in range(DEPTH - 1):
        corner = frame.merged(corners, 0, DEPTH + i)
        src[-1 - i] = jnp.where(valid, frame.row(odd[DEPTH + i], corner), 0.0)
    for x in range(*late["gain"]):
        frame.weights(
            q, gain, src, first,
            diag if x == 0 else None,
            wx if x < 0 else None,
            wy if x == -1 else None,
            wz, x, valid if x < 0 else None,
        )
    for x in range(*late["pres"]):
        pres[x] = smooth(first, gain, src, wx, wy, wz, x)
    res = [residual(frame, src, diag, pres, wx, wy, wz, x) for x in range(3)]
    res.append(res_row[...])

    res_total = sums[0:1] + fold(res[0] + res[1] + res[2])
    link_odd = fold(sum(q[x][frame.own] for x in range(-2, 2)))
    link_even, link_cross, link_back, ends = (sums[i : i + 1] for i in range(1, 5))
    outflow = link_even + link_odd + link_cross + link_back + ends
    link_down = jnp.where(even, link_even, link_odd)
    lines = jnp.concatenate([res_total, 0.25 * link_down, 0.25 * link_cross, 0.25 * outflow])
    lines = jnp.sum(lines, axis=1, keepdims=True)
    line = iota((1, layers), 1)
    summary = jnp.zeros((1, layers), FLOAT)
    for i in range(4):
        summary = jnp.where(line == 2 * i + 1, lines[i : i + 1], summary)

    packs = rows // 4
    by_row = [coarse_rows(res[2 * k] + res[2 * k + 1], couples, tile_w) for k in range(2)]
    by_row += [res_coarse[k] for k in range(rows // 2 - 2)]
    r = [pack_pairs(by_row[k], by_row[k + packs], 1) for k in range(packs)]
    middle_low, middle_high = coef[3 * packs], coef[3 * packs + 1]
    fix = [coef[k] * r[k] for k in range(packs)]
    for _ in range(BLOCK_SWEEPS - 1):
        updated = []
        for k in range(packs):
            value, link_y, link_z = fix[k], coef[packs + k], coef[2 * packs + k]
            acc = r[k] + link_y * roll(value, -2, 1) + roll(link_y * value, 2, 1)
            acc = acc + link_z * roll(value, -2, 2) + roll(link_z * value, 2, 2)
            if k > 0:
                acc = acc + coef[3 * packs + 1 + k] * fix[k - 1]
            else:
                acc = acc + middle_high * roll(fix[packs - 1], 1, 1)
            if k < packs - 1:
                acc = acc + coef[3 * packs + 2 + k] * fix[k + 1]
            else:
                acc = acc + middle_low * roll(fix[0], -1, 1)
            updated.append(KEEP * value + coef[k] * acc)
        fix = updated
    fix = [jnp.where(touched[...] > 0.0, f, 0.0) for f in fix]
    for k in range(packs):
        fix_out[k] = fix[k]

    parts = [unpack_pairs(fix[k % packs], 1)[k // packs] for k in range(rows // 2)]
    count = nd * nc
    for i in range(CHUNK):
        part = summary[:, i * LANES : (i + 1) * LANES]
        chunks[pl.ds(i, count, stride=CHUNK), :] = jnp.broadcast_to(part, (count, LANES))
    cross = lax.axis_index("cross")
    odd_step = jnp.where(even, -1, 1)
    edges = {}
    for dy in (-1, 1):
        at_couple, at_col = (0, 0) if dy < 0 else (couples - 1, tile_w - 1)
        edge = jnp.concatenate([p[at_couple][at_col : at_col + 1] for p in parts])
        edges[dy] = edge = unpack_pairs(edge, 1)[0 if dy < 0 else 1]
        for k, step in ((0, odd_step), (rows // 2 - 1, -odd_step)):

            @pl.when(beside(cross, nc, dy) & beside(down, nd, step))
            def _(k=k, step=step, dy=dy, edge=edge):
                both = jnp.where(line % 2 == 0, edge[k : k + 1], summary)
                at = ((cross + dy) * nd + down + step) * CHUNK
                for i in range(CHUNK):
                    chunks[pl.ds(at + i, 1), :] = both[:, i * LANES : (i + 1) * LANES]

    copy = pltpu.make_async_copy(chunks, chunks_hbm, sem)
    copy.start()

    sub = iota((tile_w, layers), 0) % couples
    for out, k, x in ((far_out, 0, 1), (near_out, rows // 2 - 1, rows - 2)):
        packed = parts[k][0]
        for t in range(1, couples):
            packed = jnp.where(sub == t, parts[k][t], packed)
        out[cols:] = packed
        fine = jnp.stack(unpack_pairs(parts[k], 2), axis=1).reshape(cols, layers)
        out[:cols] = pres[x][frame.own] + fine
    for cross_kind, out in zip(pairings(nc), sides):
        right, _ = facing(cross, nc, cross_kind)
        out[: rows // 2] = jnp.where(right, edges[1], edges[-1])
    copy.wait()


def coarse_solve(totals, outflow, link_down, link_up, link_cross):
    nc = len(totals)

    def operate(v):
        out = []
        for c in range(nc):
            image = outflow[c] * v[c] - link_down[c] * roll(v[c], -1, 0) - link_up[c] * roll(v[c], 1, 0)
            if c < nc - 1:
                image = image - link_cross[c] * v[c + 1]
            if c > 0:
                image = image - link_cross[c - 1] * v[c - 1]
            out.append(image)
        return out

    def dot(a, b):
        return jnp.sum(sum(x * y for x, y in zip(a, b)), axis=0, keepdims=True)

    answer = [jnp.zeros_like(t) for t in totals]
    resid = search = totals
    norm = dot(totals, totals)
    for step in range(COARSE_ITERS):
        image = operate(search)
        alpha = norm / dot(search, image)
        answer = [a + alpha * s for a, s in zip(answer, search)]
        if step == COARSE_ITERS - 1:
            break
        resid = [r - alpha * m for r, m in zip(resid, image)]
        norm_next = dot(resid, resid)
        beta = norm_next / norm
        search = [r + beta * s for r, s in zip(resid, search)]
        norm = norm_next
    return answer


KEPT = ("src", "gain", "wx", "wy", "wz")


def around(nd, nc, step, dy):
    row = jnp.clip(lax.axis_index("down") + step, 0, nd - 1)
    return row, jnp.clip(lax.axis_index("cross") + dy, 0, nc - 1)


def fine_row(packed, couples):
    sub = iota(packed.shape, 0) % couples
    parts = []
    for t in range(couples):
        tall = jnp.where(sub == t, packed, 0.0)
        for s in range(couples):
            if s != t:
                tall = tall + jnp.where(sub == s, roll(packed, s - t, 0), 0.0)
        parts += unpack_pairs(tall, 1)
    return jnp.concatenate(parts, axis=0)


def strip_mask(nc, layers):
    cross, half = lax.axis_index("cross"), STRIP // 2
    col = iota((STRIP, layers), 0)
    there = (col < jnp.where(cross < nc - 1, half, 0)) | (col >= jnp.where(cross > 0, half, STRIP))
    return there, col < half


def sides_of(nd):
    down = lax.axis_index("down")
    step = jnp.where(down % 2 == 0, -1, 1)
    return step, beside(down, nd, step), beside(down, nd, -step)


def base_kernel(nd, nc, tiles, near, far, fix, pres_early, pres_late, *refs):
    n_side = len(pairings(nc))
    sides = refs[:n_side]
    early = dict(zip(KEPT, refs[n_side:]))
    late = dict(zip(KEPT, refs[n_side + len(KEPT) :]))
    out, pres_ref, third_ref = refs[n_side + 2 * len(KEPT) :]
    packs, couples, tile_w, layers = fix.shape
    rows, cols = 4 * packs, tiles * tile_w
    src, gain, wx, wy, wz = (joined(rows, n, early[n], late[n]) for n in KEPT)
    start = joined(rows, "pres", pres_early, pres_late)
    own, halo = slice(0, cols), slice(cols, cols + STRIP)
    frame = Frame(nd, nc, cols, layers)
    pres = Rows((pres_ref, -2, rows + 4))
    third = Rows((third_ref, -1, rows + 2))
    for k in range(packs):
        for j, part in enumerate(unpack_pairs(fix[k], 1)):
            both = unpack_pairs(part, 2)
            fine = jnp.stack(both, axis=1).reshape(cols, layers)
            row = k + j * packs
            edge = jnp.zeros((STRIP, layers), FLOAT)
            for place, side in zip(frame.sides, sides):
                edge = jnp.where(place, side[row : row + 1], edge)
            for x in (2 * row, 2 * row + 1):
                pres_ref[x + 2, own, :] = start[x][own] + fine
                pres_ref[x + 2, halo, :] = start[x][halo] + edge
    _, odd_there, even_there = sides_of(nd)
    for message, there, xs in ((near, even_there, (rows, rows + 1)), (far, odd_there, (-1, -2))):
        rim = jnp.where(there, fine_row(message[cols:], couples), 0.0)
        pres_ref[xs[0] + 2, own, :] = start[xs[0]][own] + rim
        pres_ref[xs[0] + 2, halo, :] = start[xs[0]][halo]
        pres_ref[xs[1] + 2, own, :] = jnp.where(there, message[:cols], 0.0)
        pres_ref[xs[1] + 2, halo, :] = jnp.zeros((STRIP, layers), FLOAT)
    for x in range(-1, rows + 1):
        third[x] = smooth(pres, gain, src, wx, wy, wz, x)
    for x in range(rows):
        out[x] = smooth(third, gain, src, wx, wy, wz, x)[own]


def plain_sweep(field, gain, wx, wy, wz, x):
    total = 0.0
    if x in field:
        value = field[x]
        total = wy[x] * roll(value, -1, 0) + roll(wy[x] * value, 1, 0)
        total = total + wz[x] * roll(value, -1, 1) + roll(wz[x] * value, 1, 1)
    if x + 1 in field:
        total = total + wx[x] * field[x + 1]
    if x - 1 in field:
        total = total + wx[x - 1] * field[x - 1]
    total = gain[x] * total
    return KEEP * field[x] + total if x in field else total


def response_kernel(nd, nc, rows, *refs):
    early = dict(zip(KEPT, refs))
    late = dict(zip(KEPT, refs[len(KEPT) :]))
    every, by_odd, by_even, by_side, by_corner = refs[2 * len(KEPT) :]
    _, gain, wx, wy, wz = (joined(rows, n, early[n], late[n]) for n in KEPT)
    cols, layers = every.shape[1:]
    _, odd_there, even_there = sides_of(nd)
    there, _ = strip_mask(nc, layers)
    strip = jnp.where(there, 1.0, 0.0)
    blank = jnp.zeros((cols, layers), FLOAT)
    ones = jnp.ones((cols, layers), FLOAT)
    row_all = jnp.concatenate([ones, strip])
    row_own = jnp.concatenate([ones, jnp.zeros((STRIP, layers), FLOAT)])
    row_strip = jnp.concatenate([blank, strip])

    def sweeps(field, first, second):
        once = {x: plain_sweep(field, gain, wx, wy, wz, x) for x in first}
        return [plain_sweep(once, gain, wx, wy, wz, x)[:cols] for x in second]

    def ends(value):
        return value[:STRIP], value[cols - STRIP :]

    def put(ref, x, value):
        ref[x, :STRIP, :], ref[x, STRIP:, :] = ends(value)

    odd_row, even_row = (jnp.where(t, row_own, 0.0) for t in (odd_there, even_there))
    field = {x: row_all for x in range(rows)}
    field |= {-2: odd_row, rows + 1: even_row}
    field |= {-1: jnp.where(odd_there, row_all, 0.0), rows: jnp.where(even_there, row_all, 0.0)}
    for x, value in enumerate(sweeps(field, range(-1, rows + 1), range(rows))):
        every[x] = value
    for x, value in enumerate(sweeps({-2: odd_row, -1: odd_row}, (-1, 0), (0, 1))):
        by_odd[x] = value
    field = {rows: even_row, rows + 1: even_row}
    for x, value in enumerate(sweeps(field, (rows - 1, rows), (rows - 2, rows - 1))):
        by_even[x] = value
    field = {x: row_strip for x in range(rows)}
    for x, value in enumerate(sweeps(field, range(-1, rows + 1), range(rows))):
        put(by_side, x, value)
    for i, (at, x, t) in enumerate(((-1, 0, odd_there), (rows, rows - 1, even_there))):
        field = {at: jnp.where(t, row_strip, 0.0)}
        put(by_corner, i, sweeps(field, (at, x), (x,))[0])


def last_kernel(nd, nc, got, base, every, by_odd, by_even, by_side, by_corner, *refs):
    out, new, bricks, sems = refs
    rows, cols, layers = out.shape
    down, cross = lax.axis_index("down"), lax.axis_index("cross")
    even = down % 2 == 0

    tables = [got[pl.ds(c * nd * CHUNK, nd, stride=CHUNK), :] for c in range(nc)]

    def spread_lane(table, at):
        return jnp.broadcast_to(table[:, 2 * at + 1 : 2 * at + 2], (nd, LANES))

    last = iota((nd, LANES), 0) == nd - 1
    totals = [spread_lane(t, 0) for t in tables]
    link_down = [jnp.where(last, 0.0, spread_lane(t, 1)) for t in tables]
    link_up = [roll(link, 1, 0) for link in link_down]
    link_cross = [spread_lane(t, 2) for t in tables]
    outflow = [spread_lane(t, 3) for t in tables]
    answer = coarse_solve(totals, outflow, link_down, link_up, link_cross)
    for c in range(nc):
        bricks[c] = answer[c]

    def brick(step, dy):
        row, col = around(nd, nc, step, dy)
        return jnp.concatenate([bricks[col, pl.ds(row, 1), :]] * (layers // LANES), axis=1)

    def corner(step, dy):
        row, col = around(nd, nc, step, dy)
        at = (col * nd + row) * CHUNK
        both = jnp.concatenate([got[pl.ds(at + i, 1), :] for i in range(CHUNK)], axis=1)
        return unpack_pairs(both, 1)[0] + brick(step, dy) - mine

    odd_step, _, _ = sides_of(nd)
    mine = brick(0, 0)
    more_odd, more_even = brick(odd_step, 0) - mine, brick(-odd_step, 0) - mine
    more_side = brick(0, -1) - mine, brick(0, 1) - mine
    more_corner = [[corner(step, dy) for dy in (-1, 1)] for step in (odd_step, -odd_step)]
    halves = slice(0, STRIP), slice(STRIP, 2 * STRIP)
    ends = slice(0, STRIP), slice(cols - STRIP, cols)
    copies = []
    for x in reversed(range(rows)):
        at = counted(x, rows)
        value = base[x] + mine * every[x]
        if x < 2:
            value = value + more_odd * by_odd[x]
        if x >= rows - 2:
            value = value + more_even * by_even[x - (rows - 2)]
        new[at] = value
        for end, half, side, odd_corner, even_corner in zip(ends, halves, more_side, *more_corner):
            part = value[end] + side * by_side[x, half, :]
            if x == 0:
                part = part + odd_corner * by_corner[0, half, :]
            if x == rows - 1:
                part = part + even_corner * by_corner[1, half, :]
            new[at, end, :] = part
        if x % 2 == 0:
            span = pl.ds(jnp.where(even, x, rows - 2 - x), 2)
            copies.append(pltpu.make_async_copy(new.at[span], out.at[span], sems.at[len(copies)]))
            copies[-1].start()
    for copy in copies:
        copy.wait()


def whole(*shape):
    return jax.ShapeDtypeStruct(shape, FLOAT)


def call(kernel, out_shape, spaces, scratch=(), vmem_bytes=VMEM_BYTES, out_spaces=None):
    return pl.pallas_call(
        kernel,
        out_shape=out_shape,
        in_specs=[pl.BlockSpec(memory_space=s) for s in spaces],
        out_specs=jax.tree.map(
            lambda _, s: pl.BlockSpec(memory_space=s),
            out_shape,
            out_spaces or jax.tree.map(lambda _: pltpu.VMEM, out_shape),
        ),
        scratch_shapes=list(scratch),
        compiler_params=pltpu.CompilerParams(vmem_limit_bytes=vmem_bytes),
    )


def body(nd, nc, right_side, kappa, band_mask, tile_route):
    rows, cols, layers = right_side.shape
    tiles = tile_route.shape[1]
    axes = ("down", "cross")
    wide = cols + STRIP
    block = whole(rows, cols, layers)
    vmem = pltpu.VMEM
    early, late = spans(rows)

    shapes, perms = [], []
    for kind in pairings(nd):
        shapes.append(whole(2 * DEPTH - 1, cols, layers))
        perms.append(pairs_of(nd, nc, kind, None))
        if kind:
            for cross_kind in pairings(nc):
                shapes.append(whole(CORNER, STRIP, layers))
                perms.append(pairs_of(nd, nc, kind, cross_kind))
    strips = [whole(rows, STRIP, layers) for _ in pairings(nc)]
    packs, couples, tile_w = rows // 4, tiles // 2, cols // tiles
    tile_shape = (couples, tile_w, layers)
    conduct, *messages = call(
        functools.partial(pack_kernel, nd, nc),
        [block] + shapes + strips,
        [pltpu.HBM] * 3,
        scratch=[
            pltpu.VMEM((rows, cols, layers), FLOAT),
            pltpu.VMEM((rows, cols, layers), FLOAT),
            pltpu.VMEM((rows, cols, layers), band_mask.dtype),
            pltpu.SemaphoreType.DMA((3,)),
        ],
        vmem_bytes=54400 * 1024,
    )(right_side, kappa, band_mask)

    received = [lax.ppermute(m, axes, p) for m, p in zip(messages, perms)]
    even, odd = received[0], received[1:]
    if strips:
        strips = call(
            functools.partial(strip_kernel, nd, nc),
            [whole(rows + CORNER, STRIP, layers) for _ in strips],
            [vmem] * (1 + len(strips)),
        )(even, *messages[len(perms) :])
        strips = [
            lax.ppermute(m, axes, pairs_of(nd, nc, None, cross_kind))
            for m, cross_kind in zip(strips, pairings(nc))
        ]
    if not odd:
        odd = [jnp.zeros((2 * DEPTH - 1, cols, layers), FLOAT)]

    first_part = call(
        functools.partial(early_kernel, nd, nc, tiles),
        [whole(*span_shape(early[n], wide, layers)) for n in EARLY]
        + [
            whole(rows // 2 - 2, *tile_shape),
            whole(cols, layers),
            whole(4 * packs + 1, *tile_shape),
            whole(5, LANES),
            whole(*tile_shape),
        ],
        [vmem] * (4 + len(strips)),
    )(right_side, conduct, tile_route, even, *strips)
    late_arrays = call(
        functools.partial(late_kernel, nd, nc, tiles, rows),
        [whole(STRIP, layers) for _ in pairings(nc)]
        + [whole(*span_shape(late[n], wide, layers)) for n in LATE_KEPT]
        + [
            whole(packs, *tile_shape),
            whole(cols + tile_w, layers),
            whole(cols + tile_w, layers),
            whole(nd * nc * CHUNK, LANES),
        ],
        [vmem] * (len(odd) + len(first_part)),
        scratch=[pltpu.VMEM(span_shape(late[n], wide, layers), FLOAT) for n in LATE_SCRATCH]
        + [pltpu.VMEM((nd * nc * CHUNK, LANES), FLOAT), pltpu.SemaphoreType.DMA],
        out_spaces=[vmem] * (len(pairings(nc)) + len(LATE_KEPT) + 3) + [pltpu.HBM],
    )(*odd, *first_part)
    n_side = len(pairings(nc))
    sides, late_arrays = late_arrays[:n_side], late_arrays[n_side:]
    *late_arrays, fix, near, far, chunks = late_arrays
    early_arrays = dict(zip(EARLY, first_part))
    late_arrays = dict(zip(LATE_KEPT, late_arrays))
    kept = [d[n] for d in (early_arrays, late_arrays) for n in KEPT]

    chunks = chunks.reshape(nd * nc, CHUNK, 1, LANES)
    arrived = lax.all_to_all(chunks, ("cross", "down"), 0, 0, tiled=True).reshape(nd * nc * CHUNK, LANES)
    far = lax.ppermute(far, axes, pairs_of(nd, nc, True, None))
    near = lax.ppermute(near, axes, pairs_of(nd, nc, False, None))
    sides = [
        lax.ppermute(m, axes, pairs_of(nd, nc, None, cross_kind))
        for m, cross_kind in zip(sides, pairings(nc))
    ]
    base = call(
        functools.partial(base_kernel, nd, nc, tiles),
        block,
        [vmem] * (5 + n_side + len(kept)),
        scratch=[
            pltpu.VMEM((rows + 4, wide, layers), FLOAT),
            pltpu.VMEM((rows + 2, wide, layers), FLOAT),
        ],
    )(near, far, fix, early_arrays["pres"], late_arrays["pres"], *sides, *kept)
    responses = call(
        functools.partial(response_kernel, nd, nc, rows),
        [
            block,
            whole(2, cols, layers),
            whole(2, cols, layers),
            whole(rows, 2 * STRIP, layers),
            whole(2, 2 * STRIP, layers),
        ],
        [vmem] * len(kept),
    )(*kept)
    return call(
        functools.partial(last_kernel, nd, nc),
        block,
        [vmem] * (2 + len(responses)),
        scratch=[
            pltpu.VMEM((rows, cols, layers), FLOAT),
            pltpu.VMEM((nc, nd, LANES), FLOAT),
            pltpu.SemaphoreType.DMA((rows // 2,)),
        ],
        out_spaces=pltpu.HBM,
    )(arrived, base, *responses)


def solution(mesh):
    return jax.shard_map(
        functools.partial(body, mesh.shape["down"], mesh.shape["cross"]),
        mesh=mesh,
        in_specs=(
            P("down", "cross", None),
            P("down", "cross", None),
            P("down", "cross", None),
            P("down", "cross"),
        ),
        out_specs=P("down", "cross", None),
        check_vma=False,
    )
```

```python
import functools

import jax
import jax.numpy as jnp
from jax import lax
from jax.experimental import pallas as pl
from jax.experimental.pallas import tpu as pltpu
from jax.sharding import PartitionSpec as P

BLOCK_SWEEPS = 4
COARSE_ITERS = 12
OMEGA = 0.8
KEEP = 1.0 - OMEGA
SNOW_FACTOR = 3.0

DEPTH = 3
CORNER = DEPTH
STRIP = 8
LANES = 128
CHUNK = 2
FLOAT = jnp.float32
VMEM_BYTES = 24 * 1024 * 1024


def partners(count, odd):
    found = []
    for i in range(count):
        j = ((i + 1) ^ 1) - 1 if odd else i ^ 1
        found.append(j if 0 <= j < count else i)
    return found


def pairings(count):
    return [k for k in (False, True) if any(j != i for i, j in enumerate(partners(count, k)))]


def pairs_of(count_down, count_cross, down_kind, cross_kind):
    rows = list(range(count_down)) if down_kind is None else partners(count_down, down_kind)
    cols = list(range(count_cross)) if cross_kind is None else partners(count_cross, cross_kind)
    return [
        (i * count_cross + j, rows[i] * count_cross + cols[j])
        for i in range(count_down)
        for j in range(count_cross)
    ]


def facing(index, count, kind):
    ahead = (index % 2 == 0) != kind
    return ahead, jnp.where(ahead, index < count - 1, index > 0)


def beside(index, count, step):
    return (index + step >= 0) & (index + step < count)


def roll(x, amount, axis):
    return pltpu.roll(x, amount % x.shape[axis], axis)


def iota(shape, axis):
    return lax.broadcasted_iota(jnp.int32, shape, axis)


def gather(value, low, high, wx_low, wx_high, wy, wz):
    total = wx_high * high
    if low is not None:
        total = total + wx_low * low
    total = total + wy * roll(value, -1, 0) + roll(wy * value, 1, 0)
    return total + wz * roll(value, -1, 1) + roll(wz * value, 1, 1)


class Rows:
    def __init__(self, *parts):
        self.parts = parts

    def place(self, x):
        for ref, first, count in self.parts:
            if first <= x < first + count:
                return ref, x - first
        raise IndexError(x)

    def __getitem__(self, x):
        ref, i = self.place(x)
        return ref[i]

    def __setitem__(self, x, value):
        ref, i = self.place(x)
        ref[i] = value


def smooth(field, gain, src, wx, wy, wz, x):
    spread = gather(field[x], field[x - 1], field[x + 1], wx[x - 1], wx[x], wy[x], wz[x])
    return KEEP * field[x] + gain[x] * (src[x] + spread)


def counted(x, rows):
    return jnp.where(lax.axis_index("down") % 2 == 0, x, rows - 1 - x)


def edge_strip(right, cols):
    return pl.ds(pl.multiple_of(jnp.where(right, cols - STRIP, 0), STRIP), STRIP)


def pack_rows(out, start, tiles, right):
    for i in range(0, len(tiles), 2):
        a, b = tiles[i], tiles[min(i + 1, len(tiles) - 1)]
        upper = iota(a.shape, 0) < STRIP // 2
        a, b = jnp.where(right, roll(a, STRIP // 2, 0), a), jnp.where(right, b, roll(b, STRIP // 2, 0))
        out[start + i // 2] = jnp.where(upper, a, b)


def unpack_row(message, start, i, right):
    tile = message[start + i // 2]
    return jnp.where(right == (i % 2 == 0), tile, roll(tile, STRIP // 2, 0))


def pack_kernel(nd, nc, rhs_hbm, kappa_hbm, mask_hbm, conduct, *refs):
    *messages, rhs, kappa, mask, sems = refs
    rows, cols, _ = rhs.shape
    messages = iter(messages)
    cross = lax.axis_index("cross")
    copies = [
        pltpu.make_async_copy(src, dst, sems.at[i])
        for i, (src, dst) in enumerate(((kappa_hbm, kappa), (mask_hbm, mask), (rhs_hbm, rhs)))
    ]
    for copy in copies:
        copy.start()
    copies[0].wait()
    copies[1].wait()
    for x in range(rows):
        at = counted(x, rows)
        conduct[x] = kappa[at] / (1.0 + SNOW_FACTOR * mask[at].astype(FLOAT))
    copies[2].wait()
    for kind in pairings(nd):
        near = [i if kind else rows - 1 - i for i in range(DEPTH)]
        out = next(messages)
        for i, x in enumerate(near):
            out[i] = conduct[x]
        for i, x in enumerate(near[:-1]):
            out[DEPTH + i] = rhs[counted(x, rows)]
        if kind:
            for cross_kind in pairings(nc):
                right, _ = facing(cross, nc, cross_kind)
                strip = edge_strip(right, cols)
                tiles = [conduct[x, strip, :] for x in near]
                tiles += [rhs[counted(x, rows), strip, :] for x in near[:-1]]
                pack_rows(next(messages), 0, tiles, right)
    for cross_kind in pairings(nc):
        right, _ = facing(cross, nc, cross_kind)
        strip = edge_strip(right, cols)
        tiles = [conduct[x, strip, :] for x in range(rows)]
        tiles += [rhs[counted(x, rows), strip, :] for x in range(rows)]
        pack_rows(next(messages), 0, tiles, right)


def strip_kernel(nd, nc, even, *refs):
    cols = even.shape[1]
    count = len(pairings(nc))
    for cross_kind, own, out in zip(pairings(nc), refs[:count], refs[count:]):
        right, _ = facing(lax.axis_index("cross"), nc, cross_kind)
        strip = edge_strip(right, cols)
        rows = own.shape[0]
        out[:rows] = own[...]
        tiles = [even[i, strip, :] for i in range(2 * DEPTH - 1)]
        pack_rows(out, rows, tiles, right)


def fold(x):
    x = sum(x[:, i : i + LANES] for i in range(0, x.shape[1], LANES))
    return jnp.sum(x, axis=0, keepdims=True)


def swap_pairs(x, axis):
    return jnp.where(iota(x.shape, axis) % 2 == 0, roll(x, -1, axis), roll(x, 1, axis))


def pack_pairs(a, b, axis):
    even = iota(a.shape, axis) % 2 == 0
    return jnp.where(even, a, b) + swap_pairs(jnp.where(even, b, a), axis)


def unpack_pairs(x, axis):
    even = iota(x.shape, axis) % 2 == 0
    return jnp.where(even, x, roll(x, 1, axis)), jnp.where(even, roll(x, -1, axis), x)


class Frame:
    def __init__(self, nd, nc, cols, layers):
        self.cols, self.layers, self.wide = cols, layers, cols + STRIP
        self.own, self.halo = slice(0, cols), slice(cols, cols + STRIP)
        cross = lax.axis_index("cross")
        half = STRIP // 2
        self.lane = iota((self.wide, layers), 1)
        self.last_lane = self.lane == layers - 1
        col = iota((self.wide, layers), 0)
        self.col_ok = (col < jnp.where(cross < nc - 1, cols + half, cols)) | (
            col >= jnp.where(cross > 0, cols + half, self.wide)
        )
        halo_col = iota((STRIP, layers), 0)
        self.sides, self.rights = [], []
        for cross_kind in pairings(nc):
            right, valid = facing(cross, nc, cross_kind)
            start = jnp.where(right, 0, half)
            stop = jnp.where(valid, start + half, 0)
            self.sides.append((halo_col >= start) & (halo_col < stop))
            self.rights.append(right)

    def merged(self, messages, start, i):
        total = jnp.zeros((STRIP, self.layers), FLOAT)
        for side, right, message in zip(self.sides, self.rights, messages):
            total = jnp.where(side, unpack_row(message, start, i, right), total)
        return total

    def row(self, own, halo):
        return jnp.concatenate([own, halo], axis=0)

    def doubled(self, low, here, high):
        above = jnp.where(self.last_lane, 0.0, roll(here, -1, 1))
        below = jnp.where(self.lane == 0, 0.0, roll(here, 1, 1))
        right = roll(here, -1, 0)
        ends = high if low is None else low + high
        return 6.0 * here + ends + (right + roll(here, 1, 0)) + (above + below), right, above

    def gain_of(self, doubled, valid=None):
        ok = self.col_ok & (doubled > 0.0)
        if valid is not None:
            ok = ok & valid
        return jnp.where(ok, (2.0 * OMEGA) / doubled, 0.0)

    def weights(self, q, gain, src, first, diag, wx, wy, wz, x, valid=None):
        here = q[x]
        doubled, right, above = self.doubled(q[x - 1], here, q[x + 1])
        gain_here = self.gain_of(doubled, valid)
        gain[x] = gain_here
        first[x] = gain_here * src[x]
        if diag is not None:
            diag[x] = 0.5 * doubled
        if wx is not None:
            wx[x] = 0.5 * (here + q[x + 1])
        if wy is not None:
            self.plane_weights(wy, wz, x, here, right, above)

    def plane_weights(self, wy, wz, x, here, right, above):
        wy[x] = 0.5 * (here + right)
        wz[x] = jnp.where(self.last_lane, 0.0, 0.5 * (here + above))


def residual(frame, src, diag, pres, wx, wy, wz, x):
    spread = gather(pres[x], pres[x - 1], pres[x + 1], wx[x - 1], wx[x], wy[x], wz[x])
    return (src[x] - diag[x] * pres[x] + spread)[frame.own]


def spans(rows):
    early = dict(
        q=(0, rows + DEPTH), src=(0, rows + DEPTH - 1), gain=(1, rows + DEPTH - 1),
        first=(1, rows + DEPTH - 1), diag=(1, rows), wx=(0, rows + 1), wy=(0, rows + 1),
        wz=(0, rows + 1), pres=(2, rows + 1),
    )
    late = dict(
        q=(-DEPTH, 0), src=(1 - DEPTH, 0), gain=(1 - DEPTH, 1), first=(1 - DEPTH, 1), diag=(0, 1),
        wx=(1 - DEPTH, 0), wy=(-1, 0), wz=(-1, 0), pres=(-1, 2),
    )
    return early, late


EARLY = ("q", "src", "gain", "first", "diag", "wx", "wy", "wz", "pres")
LATE_KEPT = ("src", "gain", "wx", "wy", "wz", "pres")
LATE_SCRATCH = ("q", "first", "diag")


def span_shape(span, wide, layers):
    return (span[1] - span[0], wide, layers)


def joined(rows, name, early_ref, late_ref):
    early, late = (d[name] for d in spans(rows))
    return Rows((early_ref, early[0], early[1] - early[0]), (late_ref, late[0], late[1] - late[0]))


def coarse_rows(pair, couples, tile_w):
    t = pair.reshape(couples, 2, tile_w, pair.shape[1])
    return pack_pairs(t[:, 0], t[:, 1], 2)


def tile_kernel(tiles, conduct, route, coef, touched):
    rows, cols, layers = conduct.shape
    tile_w = cols // tiles
    couples = tiles // 2
    even_lane = iota((tile_w, layers), 1) % 2 == 0
    for t in range(couples):
        numbers = [jnp.broadcast_to(route[0:1, i : i + 1], (tile_w, layers)) for i in (2 * t, 2 * t + 1)]
        touched[t] = jnp.where(jnp.where(even_lane, *numbers) >= 0, 1.0, 0.0)

    packs = rows // 4
    by_row = [
        coarse_rows(0.125 * (conduct[2 * k] + conduct[2 * k + 1]), couples, tile_w)
        for k in range(rows // 2)
    ]
    con = [pack_pairs(by_row[k], by_row[k + packs], 1) for k in range(packs)]
    shape = (couples, tile_w, layers)
    tile_col, tile_lane = iota(shape, 1), iota(shape, 2)
    even_col = tile_col % 2 == 0
    y_end, y_start = tile_col >= tile_w - 2, tile_col < 2
    z_end, z_start = tile_lane >= layers - 2, tile_lane < 2
    for k in range(packs - 1):
        coef[3 * packs + 2 + k] = 2.0 * (con[k] + con[k + 1])
    middle = 2.0 * (con[packs - 1] + roll(con[0], -1, 1))
    coef[3 * packs] = jnp.where(even_col, middle, 0.0)
    coef[3 * packs + 1] = jnp.where(even_col, 0.0, roll(middle, 1, 1))
    for k in range(packs):
        c = con[k]
        y_high = jnp.where(y_end, 0.0, roll(c, -2, 1))
        z_high = jnp.where(z_end, 0.0, roll(c, -2, 2))
        y_low = jnp.where(y_start, 0.0, roll(c, 2, 1))
        z_low = jnp.where(z_start, 0.0, roll(c, 2, 2))
        total = 6.0 * c + (y_high + y_low) + (z_high + z_low)
        if k > 0:
            total = total + con[k - 1]
        else:
            total = total + jnp.where(even_col, 0.0, roll(con[packs - 1], 1, 1))
        if k < packs - 1:
            total = total + con[k + 1]
        else:
            total = total + jnp.where(even_col, roll(con[0], -1, 1), 0.0)
        total = 2.0 * total
        coef[k] = OMEGA / jnp.where(total > 0.0, total, 1.0)
        coef[packs + k] = jnp.where(y_end, 0.0, 2.0 * (c + y_high))
        coef[2 * packs + k] = jnp.where(z_end, 0.0, 2.0 * (c + z_high))


def early_kernel(nd, nc, tiles, rhs, conduct, even, *refs):
    rows, cols, layers = conduct.shape
    tile_w = cols // tiles
    couples = tiles // 2
    n_cross = len(pairings(nc))
    strips = refs[:n_cross]
    *arrays, res_coarse, res_row, part, sums = refs[n_cross:]
    early, _ = spans(rows)
    at = {n: Rows((r, early[n][0], r.shape[0])) for n, r in zip(EARLY, arrays)}
    q, src, gain, first, diag, wx, wy, wz, pres = (at[n] for n in EARLY)
    frame = Frame(nd, nc, cols, layers)
    own, halo = frame.own, frame.halo

    for x in range(rows):
        q[x] = frame.row(conduct[x], frame.merged(strips, 0, x))
        src[x] = frame.row(rhs[counted(x, rows)], frame.merged(strips, 0, rows + x))
    _, valid = facing(lax.axis_index("down"), nd, False)
    for i in range(DEPTH):
        q[rows + i] = jnp.where(valid, frame.row(even[i], frame.merged(strips, rows, i)), 0.0)
    for i in range(DEPTH - 1):
        corner = frame.merged(strips, rows, DEPTH + i)
        src[rows + i] = jnp.where(valid, frame.row(even[DEPTH + i], corner), 0.0)

    here = q[0]
    above = jnp.where(frame.last_lane, 0.0, roll(here, -1, 1))
    frame.plane_weights(wy, wz, 0, here, roll(here, -1, 0), above)
    wx[0] = 0.5 * (here + q[1])
    part[0] = frame.doubled(None, here, q[1])[0]
    for x in range(*early["gain"]):
        frame.weights(
            q, gain, src, first,
            diag if x < rows else None,
            wx if x < early["wx"][1] else None,
            wy if x < early["wy"][1] else None,
            wz, x, valid if x >= rows else None,
        )
    for x in range(*early["pres"]):
        pres[x] = smooth(first, gain, src, wx, wy, wz, x)

    spread = gather(first[1], None, first[2], None, wx[1], wy[1], wz[1])
    part[1] = KEEP * first[1] + gain[1] * (src[1] + spread)
    part[2] = gain[1] * wx[0]
    spread = gather(pres[2], None, pres[3], None, wx[2], wy[2], wz[2])
    part[3] = src[2] - diag[2] * pres[2] + spread

    res = {x: residual(frame, src, diag, pres, wx, wy, wz, x) for x in range(3, rows)}
    res_row[...] = res[3]
    for k in range(2, rows // 2):
        res_coarse[k - 2] = coarse_rows(res[2 * k] + res[2 * k + 1], couples, tile_w)

    strip_col = iota((STRIP, layers), 0)
    plane = sum(q[x][own] for x in range(rows))
    beyond = sum(q[x][halo] for x in range(rows))
    own_lane = iota((cols, layers), 1)
    low, high = strip_col < 2, strip_col >= STRIP - 2
    sums[0:1] = fold(sum(res.values()))
    sums[1:2] = fold(sum(q[x][own] for x in range(rows - 2, rows + 2)))
    sums[2:3] = fold(jnp.where(high, plane[cols - STRIP :], 0.0) + jnp.where(low, beyond, 0.0))
    sums[3:4] = fold(jnp.where(low, plane[:STRIP], 0.0) + jnp.where(high, beyond, 0.0))
    sums[4:5] = fold(jnp.where((own_lane < 2) | (own_lane >= layers - 2), plane, 0.0))


def late_kernel(nd, nc, tiles, rows, odd, *refs):
    n_cross = len(pairings(nc)) if len(pairings(nd)) > 1 else 0
    corners = refs[:n_cross]
    n_in = n_cross + len(EARLY) + 6
    early_refs = dict(zip(EARLY, refs[n_cross:]))
    res_coarse, res_row, part, sums, coef, touched = refs[n_in - 6 : n_in]
    names = LATE_KEPT + ("fix", "near", "far", "chunks_hbm") + LATE_SCRATCH + ("chunks", "sem")
    n_side = len(pairings(nc))
    sides = refs[n_in : n_in + n_side]
    late_refs = dict(zip(names, refs[n_in + n_side :]))
    fix_out, near_out, far_out = (late_refs[n] for n in ("fix", "near", "far"))
    chunks_hbm, chunks, sem = (late_refs[n] for n in ("chunks_hbm", "chunks", "sem"))
    wide, layers = early_refs["q"].shape[1:]
    cols = wide - STRIP
    tile_w = cols // tiles
    couples = tiles // 2
    down = lax.axis_index("down")
    even = down % 2 == 0
    q, src, gain, first, diag, wx, wy, wz, pres = (
        joined(rows, n, early_refs[n], late_refs[n]) for n in EARLY
    )
    frame = Frame(nd, nc, cols, layers)
    _, late = spans(rows)

    valid = beside(down, nd, jnp.where(even, -1, 1))
    for i in range(DEPTH):
        q[-1 - i] = jnp.where(valid, frame.row(odd[i], frame.merged(corners, 0, i)), 0.0)
    for i in range(DEPTH - 1):
        corner = frame.merged(corners, 0, DEPTH + i)
        src[-1 - i] = jnp.where(valid, frame.row(odd[DEPTH + i], corner), 0.0)
    for x in range(*late["wx"]):
        frame.weights(
            q, gain, src, first, None, wx, wy if x == -1 else None, wz, x, valid
        )
    doubled = part[0] + q[-1]
    gain[0] = frame.gain_of(doubled)
    first[0] = gain[0] * src[0]
    diag[0] = 0.5 * doubled
    for x in (-1, 0):
        pres[x] = smooth(first, gain, src, wx, wy, wz, x)
    pres[1] = part[1] + part[2] * first[0]
    res = [residual(frame, src, diag, pres, wx, wy, wz, x) for x in (0, 1)]
    res.append((part[3] + wx[1] * pres[1])[frame.own])
    res.append(res_row[...])

    res_total = sums[0:1] + fold(res[0] + res[1] + res[2])
    link_odd = fold(sum(q[x][frame.own] for x in range(-2, 2)))
    link_even, link_cross, link_back, ends = (sums[i : i + 1] for i in range(1, 5))
    outflow = link_even + link_odd + link_cross + link_back + ends
    link_down = jnp.where(even, link_even, link_odd)
    lines = jnp.concatenate([res_total, 0.25 * link_down, 0.25 * link_cross, 0.25 * outflow])
    lines = jnp.sum(lines, axis=1, keepdims=True)
    line = iota((1, layers), 1)
    summary = jnp.zeros((1, layers), FLOAT)
    for i in range(4):
        summary = jnp.where(line == 2 * i + 1, lines[i : i + 1], summary)

    packs = rows // 4
    by_row = [coarse_rows(res[2 * k] + res[2 * k + 1], couples, tile_w) for k in range(2)]
    by_row += [res_coarse[k] for k in range(rows // 2 - 2)]
    r = [pack_pairs(by_row[k], by_row[k + packs], 1) for k in range(packs)]
    middle_low, middle_high = coef[3 * packs], coef[3 * packs + 1]
    fix = [coef[k] * r[k] for k in range(packs)]
    for _ in range(BLOCK_SWEEPS - 1):
        updated = []
        for k in range(packs):
            value, link_y, link_z = fix[k], coef[packs + k], coef[2 * packs + k]
            acc = r[k] + link_y * roll(value, -2, 1) + roll(link_y * value, 2, 1)
            acc = acc + link_z * roll(value, -2, 2) + roll(link_z * value, 2, 2)
            if k > 0:
                acc = acc + coef[3 * packs + 1 + k] * fix[k - 1]
            else:
                acc = acc + middle_high * roll(fix[packs - 1], 1, 1)
            if k < packs - 1:
                acc = acc + coef[3 * packs + 2 + k] * fix[k + 1]
            else:
                acc = acc + middle_low * roll(fix[0], -1, 1)
            updated.append(KEEP * value + coef[k] * acc)
        fix = updated
    fix = [jnp.where(touched[...] > 0.0, f, 0.0) for f in fix]
    for k in range(packs):
        fix_out[k] = fix[k]

    parts = [unpack_pairs(fix[k % packs], 1)[k // packs] for k in range(rows // 2)]
    count = nd * nc
    for i in range(CHUNK):
        part = summary[:, i * LANES : (i + 1) * LANES]
        chunks[pl.ds(i, count, stride=CHUNK), :] = jnp.broadcast_to(part, (count, LANES))
    cross = lax.axis_index("cross")
    odd_step = jnp.where(even, -1, 1)
    edges = {}
    for dy in (-1, 1):
        at_couple, at_col = (0, 0) if dy < 0 else (couples - 1, tile_w - 1)
        edge = jnp.concatenate([p[at_couple][at_col : at_col + 1] for p in parts])
        edges[dy] = edge = unpack_pairs(edge, 1)[0 if dy < 0 else 1]
        for k, step in ((0, odd_step), (rows // 2 - 1, -odd_step)):

            @pl.when(beside(cross, nc, dy) & beside(down, nd, step))
            def _(k=k, step=step, dy=dy, edge=edge):
                both = jnp.where(line % 2 == 0, edge[k : k + 1], summary)
                at = ((cross + dy) * nd + down + step) * CHUNK
                for i in range(CHUNK):
                    chunks[pl.ds(at + i, 1), :] = both[:, i * LANES : (i + 1) * LANES]

    copy = pltpu.make_async_copy(chunks, chunks_hbm, sem)
    copy.start()

    sub = iota((tile_w, layers), 0) % couples
    for out, k, x in ((far_out, 0, 1), (near_out, rows // 2 - 1, rows - 2)):
        packed = parts[k][0]
        for t in range(1, couples):
            packed = jnp.where(sub == t, parts[k][t], packed)
        out[cols:] = packed
        fine = jnp.stack(unpack_pairs(parts[k], 2), axis=1).reshape(cols, layers)
        out[:cols] = pres[x][frame.own] + fine
    for cross_kind, out in zip(pairings(nc), sides):
        right, _ = facing(cross, nc, cross_kind)
        out[: rows // 2] = jnp.where(right, edges[1], edges[-1])
    copy.wait()


def coarse_solve(totals, outflow, link_down, link_up, link_cross):
    nc = len(totals)

    def operate(v):
        out = []
        for c in range(nc):
            image = outflow[c] * v[c] - link_down[c] * roll(v[c], -1, 0) - link_up[c] * roll(v[c], 1, 0)
            if c < nc - 1:
                image = image - link_cross[c] * v[c + 1]
            if c > 0:
                image = image - link_cross[c - 1] * v[c - 1]
            out.append(image)
        return out

    def dot(a, b):
        return jnp.sum(sum(x * y for x, y in zip(a, b)), axis=0, keepdims=True)

    answer = [jnp.zeros_like(t) for t in totals]
    resid = search = totals
    image = operate(resid)
    norm, bend = dot(resid, resid), dot(resid, image)
    alpha = norm / bend
    for step in range(COARSE_ITERS):
        answer = [a + alpha * s for a, s in zip(answer, search)]
        if step == COARSE_ITERS - 1:
            break
        scale = 1.0 / norm
        resid = [r - alpha * m for r, m in zip(resid, image)]
        moved = operate(resid)
        norm, bend = dot(resid, resid), dot(resid, moved)
        beta = norm * scale
        alpha = norm / (bend - beta * norm / alpha)
        search = [r + beta * s for r, s in zip(resid, search)]
        image = [m + beta * i for m, i in zip(moved, image)]
    return answer


KEPT = ("src", "gain", "wx", "wy", "wz")


def around(nd, nc, step, dy):
    row = jnp.clip(lax.axis_index("down") + step, 0, nd - 1)
    return row, jnp.clip(lax.axis_index("cross") + dy, 0, nc - 1)


def fine_row(packed, couples):
    sub = iota(packed.shape, 0) % couples
    parts = []
    for t in range(couples):
        tall = jnp.where(sub == t, packed, 0.0)
        for s in range(couples):
            if s != t:
                tall = tall + jnp.where(sub == s, roll(packed, s - t, 0), 0.0)
        parts += unpack_pairs(tall, 1)
    return jnp.concatenate(parts, axis=0)


def strip_mask(nc, layers):
    cross, half = lax.axis_index("cross"), STRIP // 2
    col = iota((STRIP, layers), 0)
    there = (col < jnp.where(cross < nc - 1, half, 0)) | (col >= jnp.where(cross > 0, half, STRIP))
    return there, col < half


def sides_of(nd):
    down = lax.axis_index("down")
    step = jnp.where(down % 2 == 0, -1, 1)
    return step, beside(down, nd, step), beside(down, nd, -step)


def base_kernel(nd, nc, tiles, near, far, fix, pres_early, pres_late, *refs):
    n_side = len(pairings(nc))
    sides = refs[:n_side]
    early = dict(zip(KEPT, refs[n_side:]))
    late = dict(zip(KEPT, refs[n_side + len(KEPT) :]))
    out, pres_ref, third_ref = refs[n_side + 2 * len(KEPT) :]
    packs, couples, tile_w, layers = fix.shape
    rows, cols = 4 * packs, tiles * tile_w
    src, gain, wx, wy, wz = (joined(rows, n, early[n], late[n]) for n in KEPT)
    start = joined(rows, "pres", pres_early, pres_late)
    own, halo = slice(0, cols), slice(cols, cols + STRIP)
    frame = Frame(nd, nc, cols, layers)
    pres = Rows((pres_ref, -2, rows + 4))
    third = Rows((third_ref, -1, rows + 2))
    for k in range(packs):
        for j, part in enumerate(unpack_pairs(fix[k], 1)):
            both = unpack_pairs(part, 2)
            fine = jnp.stack(both, axis=1).reshape(cols, layers)
            row = k + j * packs
            edge = jnp.zeros((STRIP, layers), FLOAT)
            for place, side in zip(frame.sides, sides):
                edge = jnp.where(place, side[row : row + 1], edge)
            for x in (2 * row, 2 * row + 1):
                pres_ref[x + 2, own, :] = start[x][own] + fine
                pres_ref[x + 2, halo, :] = start[x][halo] + edge
    _, odd_there, even_there = sides_of(nd)
    for message, there, xs in ((near, even_there, (rows, rows + 1)), (far, odd_there, (-1, -2))):
        rim = jnp.where(there, fine_row(message[cols:], couples), 0.0)
        pres_ref[xs[0] + 2, own, :] = start[xs[0]][own] + rim
        pres_ref[xs[0] + 2, halo, :] = start[xs[0]][halo]
        pres_ref[xs[1] + 2, own, :] = jnp.where(there, message[:cols], 0.0)
        pres_ref[xs[1] + 2, halo, :] = jnp.zeros((STRIP, layers), FLOAT)
    for x in range(-1, rows + 1):
        third[x] = smooth(pres, gain, src, wx, wy, wz, x)
    for x in range(rows):
        out[x] = smooth(third, gain, src, wx, wy, wz, x)[own]


def plain_sweep(field, gain, wx, wy, wz, x):
    total = 0.0
    if x in field:
        value = field[x]
        total = wy[x] * roll(value, -1, 0) + roll(wy[x] * value, 1, 0)
        total = total + wz[x] * roll(value, -1, 1) + roll(wz[x] * value, 1, 1)
    if x + 1 in field:
        total = total + wx[x] * field[x + 1]
    if x - 1 in field:
        total = total + wx[x - 1] * field[x - 1]
    total = gain[x] * total
    return KEEP * field[x] + total if x in field else total


def response_kernel(nd, nc, rows, *refs):
    early = dict(zip(KEPT, refs))
    late = dict(zip(KEPT, refs[len(KEPT) :]))
    every, by_odd, by_even, by_side, by_corner = refs[2 * len(KEPT) :]
    _, gain, wx, wy, wz = (joined(rows, n, early[n], late[n]) for n in KEPT)
    cols, layers = every.shape[1:]
    _, odd_there, even_there = sides_of(nd)
    there, _ = strip_mask(nc, layers)
    strip = jnp.where(there, 1.0, 0.0)
    blank = jnp.zeros((cols, layers), FLOAT)
    ones = jnp.ones((cols, layers), FLOAT)
    row_all = jnp.concatenate([ones, strip])
    row_own = jnp.concatenate([ones, jnp.zeros((STRIP, layers), FLOAT)])
    row_strip = jnp.concatenate([blank, strip])

    def sweeps(field, first, second):
        once = {x: plain_sweep(field, gain, wx, wy, wz, x) for x in first}
        return [plain_sweep(once, gain, wx, wy, wz, x)[:cols] for x in second]

    def ends(value):
        return value[:STRIP], value[cols - STRIP :]

    def put(ref, x, value):
        ref[x, :STRIP, :], ref[x, STRIP:, :] = ends(value)

    odd_row, even_row = (jnp.where(t, row_own, 0.0) for t in (odd_there, even_there))
    field = {x: row_all for x in range(rows)}
    field |= {-2: odd_row, rows + 1: even_row}
    field |= {-1: jnp.where(odd_there, row_all, 0.0), rows: jnp.where(even_there, row_all, 0.0)}
    for x, value in enumerate(sweeps(field, range(-1, rows + 1), range(rows))):
        every[x] = value
    for x, value in enumerate(sweeps({-2: odd_row, -1: odd_row}, (-1, 0), (0, 1))):
        by_odd[x] = value
    field = {rows: even_row, rows + 1: even_row}
    for x, value in enumerate(sweeps(field, (rows - 1, rows), (rows - 2, rows - 1))):
        by_even[x] = value
    field = {x: row_strip for x in range(rows)}
    for x, value in enumerate(sweeps(field, range(-1, rows + 1), range(rows))):
        put(by_side, x, value)
    for i, (at, x, t) in enumerate(((-1, 0, odd_there), (rows, rows - 1, even_there))):
        field = {at: jnp.where(t, row_strip, 0.0)}
        put(by_corner, i, sweeps(field, (at, x), (x,))[0])


def last_kernel(nd, nc, got, base, every, by_odd, by_even, by_side, by_corner, *refs):
    out, new, bricks, sems = refs
    rows, cols, layers = out.shape
    down, cross = lax.axis_index("down"), lax.axis_index("cross")
    even = down % 2 == 0

    tables = [got[pl.ds(c * nd * CHUNK, nd, stride=CHUNK), :] for c in range(nc)]

    def spread_lane(table, at):
        return jnp.broadcast_to(table[:, 2 * at + 1 : 2 * at + 2], (nd, LANES))

    last = iota((nd, LANES), 0) == nd - 1
    totals = [spread_lane(t, 0) for t in tables]
    link_down = [jnp.where(last, 0.0, spread_lane(t, 1)) for t in tables]
    link_up = [roll(link, 1, 0) for link in link_down]
    link_cross = [spread_lane(t, 2) for t in tables]
    outflow = [spread_lane(t, 3) for t in tables]
    answer = coarse_solve(totals, outflow, link_down, link_up, link_cross)
    for c in range(nc):
        bricks[c] = answer[c]

    def brick(step, dy):
        row, col = around(nd, nc, step, dy)
        return jnp.concatenate([bricks[col, pl.ds(row, 1), :]] * (layers // LANES), axis=1)

    def corner(step, dy):
        row, col = around(nd, nc, step, dy)
        at = (col * nd + row) * CHUNK
        both = jnp.concatenate([got[pl.ds(at + i, 1), :] for i in range(CHUNK)], axis=1)
        return unpack_pairs(both, 1)[0] + brick(step, dy) - mine

    odd_step, _, _ = sides_of(nd)
    mine = brick(0, 0)
    more_odd, more_even = brick(odd_step, 0) - mine, brick(-odd_step, 0) - mine
    more_side = brick(0, -1) - mine, brick(0, 1) - mine
    more_corner = [[corner(step, dy) for dy in (-1, 1)] for step in (odd_step, -odd_step)]
    halves = slice(0, STRIP), slice(STRIP, 2 * STRIP)
    ends = slice(0, STRIP), slice(cols - STRIP, cols)
    copies = []
    for x in reversed(range(rows)):
        at = counted(x, rows)
        value = base[x] + mine * every[x]
        if x < 2:
            value = value + more_odd * by_odd[x]
        if x >= rows - 2:
            value = value + more_even * by_even[x - (rows - 2)]
        new[at] = value
        for end, half, side, odd_corner, even_corner in zip(ends, halves, more_side, *more_corner):
            part = value[end] + side * by_side[x, half, :]
            if x == 0:
                part = part + odd_corner * by_corner[0, half, :]
            if x == rows - 1:
                part = part + even_corner * by_corner[1, half, :]
            new[at, end, :] = part
        if x % 2 == 0:
            span = pl.ds(jnp.where(even, x, rows - 2 - x), 2)
            copies.append(pltpu.make_async_copy(new.at[span], out.at[span], sems.at[len(copies)]))
            copies[-1].start()
    for copy in copies:
        copy.wait()


def whole(*shape):
    return jax.ShapeDtypeStruct(shape, FLOAT)


def call(kernel, out_shape, spaces, scratch=(), vmem_bytes=VMEM_BYTES, out_spaces=None):
    return pl.pallas_call(
        kernel,
        out_shape=out_shape,
        in_specs=[pl.BlockSpec(memory_space=s) for s in spaces],
        out_specs=jax.tree.map(
            lambda _, s: pl.BlockSpec(memory_space=s),
            out_shape,
            out_spaces or jax.tree.map(lambda _: pltpu.VMEM, out_shape),
        ),
        scratch_shapes=list(scratch),
        compiler_params=pltpu.CompilerParams(vmem_limit_bytes=vmem_bytes),
    )


def body(nd, nc, right_side, kappa, band_mask, tile_route):
    rows, cols, layers = right_side.shape
    tiles = tile_route.shape[1]
    axes = ("down", "cross")
    wide = cols + STRIP
    block = whole(rows, cols, layers)
    vmem = pltpu.VMEM
    early, late = spans(rows)

    shapes, perms = [], []
    for kind in pairings(nd):
        shapes.append(whole(2 * DEPTH - 1, cols, layers))
        perms.append(pairs_of(nd, nc, kind, None))
        if kind:
            for cross_kind in pairings(nc):
                shapes.append(whole(CORNER, STRIP, layers))
                perms.append(pairs_of(nd, nc, kind, cross_kind))
    strips = [whole(rows, STRIP, layers) for _ in pairings(nc)]
    packs, couples, tile_w = rows // 4, tiles // 2, cols // tiles
    tile_shape = (couples, tile_w, layers)
    conduct, *messages = call(
        functools.partial(pack_kernel, nd, nc),
        [block] + shapes + strips,
        [pltpu.HBM] * 3,
        scratch=[
            pltpu.VMEM((rows, cols, layers), FLOAT),
            pltpu.VMEM((rows, cols, layers), FLOAT),
            pltpu.VMEM((rows, cols, layers), band_mask.dtype),
            pltpu.SemaphoreType.DMA((3,)),
        ],
        vmem_bytes=54400 * 1024,
    )(right_side, kappa, band_mask)

    received = [lax.ppermute(m, axes, p) for m, p in zip(messages, perms)]
    even, odd = received[0], received[1:]
    if strips:
        strips = call(
            functools.partial(strip_kernel, nd, nc),
            [whole(rows + CORNER, STRIP, layers) for _ in strips],
            [vmem] * (1 + len(strips)),
        )(even, *messages[len(perms) :])
        strips = [
            lax.ppermute(m, axes, pairs_of(nd, nc, None, cross_kind))
            for m, cross_kind in zip(strips, pairings(nc))
        ]
    if not odd:
        odd = [jnp.zeros((2 * DEPTH - 1, cols, layers), FLOAT)]

    first_part = call(
        functools.partial(early_kernel, nd, nc, tiles),
        [whole(*span_shape(early[n], wide, layers)) for n in EARLY]
        + [
            whole(rows // 2 - 2, *tile_shape),
            whole(cols, layers),
            whole(4, wide, layers),
            whole(5, LANES),
        ],
        [vmem] * (3 + len(strips)),
    )(right_side, conduct, even, *strips)
    first_part += call(
        functools.partial(tile_kernel, tiles),
        [whole(4 * packs + 1, *tile_shape), whole(*tile_shape)],
        [vmem] * 2,
    )(conduct, tile_route)
    late_arrays = call(
        functools.partial(late_kernel, nd, nc, tiles, rows),
        [whole(STRIP, layers) for _ in pairings(nc)]
        + [whole(*span_shape(late[n], wide, layers)) for n in LATE_KEPT]
        + [
            whole(packs, *tile_shape),
            whole(cols + tile_w, layers),
            whole(cols + tile_w, layers),
            whole(nd * nc * CHUNK, LANES),
        ],
        [vmem] * (len(odd) + len(first_part)),
        scratch=[pltpu.VMEM(span_shape(late[n], wide, layers), FLOAT) for n in LATE_SCRATCH]
        + [pltpu.VMEM((nd * nc * CHUNK, LANES), FLOAT), pltpu.SemaphoreType.DMA],
        out_spaces=[vmem] * (len(pairings(nc)) + len(LATE_KEPT) + 3) + [pltpu.HBM],
    )(*odd, *first_part)
    n_side = len(pairings(nc))
    sides, late_arrays = late_arrays[:n_side], late_arrays[n_side:]
    *late_arrays, fix, near, far, chunks = late_arrays
    early_arrays = dict(zip(EARLY, first_part))
    late_arrays = dict(zip(LATE_KEPT, late_arrays))
    kept = [d[n] for d in (early_arrays, late_arrays) for n in KEPT]

    chunks = chunks.reshape(nd * nc, CHUNK, 1, LANES)
    arrived = lax.all_to_all(chunks, ("cross", "down"), 0, 0, tiled=True).reshape(nd * nc * CHUNK, LANES)
    far = lax.ppermute(far, axes, pairs_of(nd, nc, True, None))
    near = lax.ppermute(near, axes, pairs_of(nd, nc, False, None))
    sides = [
        lax.ppermute(m, axes, pairs_of(nd, nc, None, cross_kind))
        for m, cross_kind in zip(sides, pairings(nc))
    ]
    base = call(
        functools.partial(base_kernel, nd, nc, tiles),
        block,
        [vmem] * (5 + n_side + len(kept)),
        scratch=[
            pltpu.VMEM((rows + 4, wide, layers), FLOAT),
            pltpu.VMEM((rows + 2, wide, layers), FLOAT),
        ],
    )(near, far, fix, early_arrays["pres"], late_arrays["pres"], *sides, *kept)
    responses = call(
        functools.partial(response_kernel, nd, nc, rows),
        [
            block,
            whole(2, cols, layers),
            whole(2, cols, layers),
            whole(rows, 2 * STRIP, layers),
            whole(2, 2 * STRIP, layers),
        ],
        [vmem] * len(kept),
    )(*kept)
    return call(
        functools.partial(last_kernel, nd, nc),
        block,
        [vmem] * (2 + len(responses)),
        scratch=[
            pltpu.VMEM((rows, cols, layers), FLOAT),
            pltpu.VMEM((nc, nd, LANES), FLOAT),
            pltpu.SemaphoreType.DMA((rows // 2,)),
        ],
        out_spaces=pltpu.HBM,
    )(arrived, base, *responses)


def solution(mesh):
    return jax.shard_map(
        functools.partial(body, mesh.shape["down"], mesh.shape["cross"]),
        mesh=mesh,
        in_specs=(
            P("down", "cross", None),
            P("down", "cross", None),
            P("down", "cross", None),
            P("down", "cross"),
        ),
        out_specs=P("down", "cross", None),
        check_vma=False,
    )
```

```python
import functools

import jax
import jax.numpy as jnp
from jax import lax
from jax.experimental import pallas as pl
from jax.experimental.pallas import tpu as pltpu
from jax.sharding import PartitionSpec as P

BLOCK_SWEEPS = 4
COARSE_ITERS = 12
OMEGA = 0.8
KEEP = 1.0 - OMEGA
SNOW_FACTOR = 3.0

DEPTH = 3
CORNER = 2
STRIP = 8
LANES = 128
CHUNK = 2
FLOAT = jnp.float32
VMEM_BYTES = 24 * 1024 * 1024


def partners(count, odd):
    found = []
    for i in range(count):
        j = ((i + 1) ^ 1) - 1 if odd else i ^ 1
        found.append(j if 0 <= j < count else i)
    return found


def pairings(count):
    return [k for k in (False, True) if any(j != i for i, j in enumerate(partners(count, k)))]


def pairs_of(count_down, count_cross, down_kind, cross_kind):
    rows = list(range(count_down)) if down_kind is None else partners(count_down, down_kind)
    cols = list(range(count_cross)) if cross_kind is None else partners(count_cross, cross_kind)
    return [
        (i * count_cross + j, rows[i] * count_cross + cols[j])
        for i in range(count_down)
        for j in range(count_cross)
    ]


def facing(index, count, kind):
    ahead = (index % 2 == 0) != kind
    return ahead, jnp.where(ahead, index < count - 1, index > 0)


def beside(index, count, step):
    return (index + step >= 0) & (index + step < count)


def roll(x, amount, axis):
    return pltpu.roll(x, amount % x.shape[axis], axis)


def iota(shape, axis):
    return lax.broadcasted_iota(jnp.int32, shape, axis)


def gather(value, low, high, wx_low, wx_high, wy, wz):
    total = wx_high * high
    if low is not None:
        total = total + wx_low * low
    total = total + wy * roll(value, -1, 0) + roll(wy * value, 1, 0)
    return total + wz * roll(value, -1, 1) + roll(wz * value, 1, 1)


class Rows:
    def __init__(self, *parts):
        self.parts = parts

    def place(self, x):
        for ref, first, count in self.parts:
            if first <= x < first + count:
                return ref, x - first
        raise IndexError(x)

    def __getitem__(self, x):
        ref, i = self.place(x)
        return ref[i]

    def __setitem__(self, x, value):
        ref, i = self.place(x)
        ref[i] = value


def smooth(field, gain, src, wx, wy, wz, x):
    spread = gather(field[x], field[x - 1], field[x + 1], wx[x - 1], wx[x], wy[x], wz[x])
    return KEEP * field[x] + gain[x] * (src[x] + spread)


def counted(x, rows):
    return jnp.where(lax.axis_index("down") % 2 == 0, x, rows - 1 - x)


def edge_strip(right, cols):
    return pl.ds(pl.multiple_of(jnp.where(right, cols - STRIP, 0), STRIP), STRIP)


def upper_half(tile, right):
    return jnp.where(right, roll(tile, STRIP // 2, 0), tile)


def lower_half(tile, right):
    return jnp.where(right, tile, roll(tile, STRIP // 2, 0))


def pack_rows(tiles, right):
    upper = iota(tiles[0].shape, 0) < STRIP // 2
    return [
        jnp.where(upper, upper_half(a, right), lower_half(b, right)) for a, b in zip(tiles[::2], tiles[1::2])
    ]


def pack_source(tiles, right):
    *packed, last = pack_rows(tiles, right)
    col = iota(last.shape, 0) % (STRIP // 2)
    free = col == jnp.where(right, 0, 3)
    for m in range(3):
        packed[m] = jnp.where(free, jnp.where(right, roll(last, -1 - m, 0), roll(last, 3 - m, 0)), packed[m])
    return packed


def pack_corner(tiles, right):
    near, far = pack_rows(tiles[:4], right)
    last = upper_half(tiles[4], right)
    free = iota(last.shape, 0) == jnp.where(right, 0, 3)
    return [near, jnp.where(free, jnp.where(right, roll(last, -3, 0), roll(last, 3, 0)), far)]


def unpack_row(message, start, i, right):
    tile = message[start + i // 2]
    return jnp.where(right == (i % 2 == 0), tile, roll(tile, STRIP // 2, 0))


def unpack_source(message, start, rows, i, right):
    if i < rows - 2:
        return unpack_row(message, start, i, right)
    tiles = [message[start + m] for m in range(3)]
    col = iota(tiles[0].shape, 0) % (STRIP // 2)
    last = jnp.zeros(tiles[0].shape, FLOAT)
    for m, tile in enumerate(tiles):
        from_right = jnp.where(col == m, roll(tile, m - 3, 0), last)
        last = jnp.where(right, from_right, jnp.where(col == m + 1, roll(tile, m + 1, 0), last))
    return jnp.where(right == (i % 2 == 0), last, roll(last, STRIP // 2, 0))


def unpack_corner(message, start, i, right):
    if i < 2 or i == 3:
        return unpack_row(message, start, i, right)
    tile = message[start + 1]
    col = iota(tile.shape, 0)
    if i == 2:
        tile = jnp.where(col == jnp.where(right, 3, 0), 0.0, tile)
    else:
        place = col == jnp.where(right, 0, 3)
        tile = jnp.where(place, jnp.where(right, roll(tile, -3, 0), roll(tile, 3, 0)), 0.0)
    return jnp.where(right, tile, roll(tile, STRIP // 2, 0))


def put_tiles(out, start, tiles):
    for i, tile in enumerate(tiles):
        out[start + i] = tile


def pack_kernel(nd, nc, rhs_hbm, kappa_hbm, mask_hbm, conduct, *refs):
    *messages, rhs, kappa, mask, sems = refs
    rows, cols, _ = rhs.shape
    messages = iter(messages)
    cross = lax.axis_index("cross")
    copies = [
        pltpu.make_async_copy(src, dst, sems.at[i])
        for i, (src, dst) in enumerate(((kappa_hbm, kappa), (mask_hbm, mask), (rhs_hbm, rhs)))
    ]
    for copy in copies:
        copy.start()
    copies[0].wait()
    copies[1].wait()
    for x in range(rows):
        at = counted(x, rows)
        conduct[x] = kappa[at] / (1.0 + SNOW_FACTOR * mask[at].astype(FLOAT))
    copies[2].wait()
    for kind in pairings(nd):
        near = [i if kind else rows - 1 - i for i in range(DEPTH)]
        out = next(messages)
        for i, x in enumerate(near):
            out[i] = conduct[x]
        for i, x in enumerate(near[:-1]):
            out[DEPTH + i] = rhs[counted(x, rows)]
        if kind:
            for cross_kind in pairings(nc):
                right, _ = facing(cross, nc, cross_kind)
                strip = edge_strip(right, cols)
                tiles = [conduct[x, strip, :] for x in near]
                tiles += [rhs[counted(x, rows), strip, :] for x in near[:-1]]
                put_tiles(next(messages), 0, pack_corner(tiles, right))
    for cross_kind in pairings(nc):
        right, _ = facing(cross, nc, cross_kind)
        strip = edge_strip(right, cols)
        tiles = pack_rows([conduct[x, strip, :] for x in range(rows)], right)
        tiles += pack_source([rhs[counted(x, rows), strip, :] for x in range(rows)], right)
        put_tiles(next(messages), 0, tiles)


def strip_kernel(nd, nc, even, *refs):
    cols = even.shape[1]
    count = len(pairings(nc))
    for cross_kind, own, out in zip(pairings(nc), refs[:count], refs[count:]):
        right, _ = facing(lax.axis_index("cross"), nc, cross_kind)
        strip = edge_strip(right, cols)
        count = own.shape[0]
        out[:count] = own[...]
        put_tiles(out, count, pack_corner([even[i, strip, :] for i in range(2 * DEPTH - 1)], right))


def fold(x):
    x = sum(x[:, i : i + LANES] for i in range(0, x.shape[1], LANES))
    return jnp.sum(x, axis=0, keepdims=True)


def swap_pairs(x, axis):
    return jnp.where(iota(x.shape, axis) % 2 == 0, roll(x, -1, axis), roll(x, 1, axis))


def pack_pairs(a, b, axis):
    even = iota(a.shape, axis) % 2 == 0
    return jnp.where(even, a, b) + swap_pairs(jnp.where(even, b, a), axis)


def unpack_pairs(x, axis):
    even = iota(x.shape, axis) % 2 == 0
    return jnp.where(even, x, roll(x, 1, axis)), jnp.where(even, roll(x, -1, axis), x)


class Frame:
    def __init__(self, nd, nc, cols, layers):
        self.cols, self.layers, self.wide = cols, layers, cols + STRIP
        self.own, self.halo = slice(0, cols), slice(cols, cols + STRIP)
        cross = lax.axis_index("cross")
        half = STRIP // 2
        self.lane = iota((self.wide, layers), 1)
        self.last_lane = self.lane == layers - 1
        col = iota((self.wide, layers), 0)
        self.col_ok = (col < jnp.where(cross < nc - 1, cols + half, cols)) | (
            col >= jnp.where(cross > 0, cols + half, self.wide)
        )
        halo_col = iota((STRIP, layers), 0)
        self.sides, self.rights = [], []
        for cross_kind in pairings(nc):
            right, valid = facing(cross, nc, cross_kind)
            start = jnp.where(right, 0, half)
            stop = jnp.where(valid, start + half, 0)
            self.sides.append((halo_col >= start) & (halo_col < stop))
            self.rights.append(right)

    def merged(self, messages, unpack, *place):
        total = jnp.zeros((STRIP, self.layers), FLOAT)
        for side, right, message in zip(self.sides, self.rights, messages):
            total = jnp.where(side, unpack(message, *place, right), total)
        return total

    def row(self, own, halo):
        return jnp.concatenate([own, halo], axis=0)

    def doubled(self, low, here, high):
        above = jnp.where(self.last_lane, 0.0, roll(here, -1, 1))
        below = jnp.where(self.lane == 0, 0.0, roll(here, 1, 1))
        right = roll(here, -1, 0)
        ends = high if low is None else low + high
        return 6.0 * here + ends + (right + roll(here, 1, 0)) + (above + below), right, above

    def gain_of(self, doubled, valid=None):
        ok = self.col_ok & (doubled > 0.0)
        if valid is not None:
            ok = ok & valid
        return jnp.where(ok, (2.0 * OMEGA) / doubled, 0.0)

    def weights(self, q, gain, src, first, diag, wx, wy, wz, x, valid=None):
        here = q[x]
        doubled, right, above = self.doubled(q[x - 1], here, q[x + 1])
        gain_here = self.gain_of(doubled, valid)
        gain[x] = gain_here
        first[x] = gain_here * src[x]
        if diag is not None:
            diag[x] = 0.5 * doubled
        if wx is not None:
            wx[x] = 0.5 * (here + q[x + 1])
        if wy is not None:
            self.plane_weights(wy, wz, x, here, right, above)

    def plane_weights(self, wy, wz, x, here, right, above):
        wy[x] = 0.5 * (here + right)
        wz[x] = jnp.where(self.last_lane, 0.0, 0.5 * (here + above))


def residual(frame, src, diag, pres, wx, wy, wz, x):
    spread = gather(pres[x], pres[x - 1], pres[x + 1], wx[x - 1], wx[x], wy[x], wz[x])
    return (src[x] - diag[x] * pres[x] + spread)[frame.own]


def spans(rows):
    early = dict(
        q=(0, rows + DEPTH), src=(0, rows + DEPTH - 1), gain=(1, rows + DEPTH - 1),
        first=(1, rows + DEPTH - 1), diag=(1, rows), wx=(0, rows + 1), wy=(0, rows + 1),
        wz=(0, rows + 1), pres=(2, rows + 1),
    )
    late = dict(
        q=(-DEPTH, 0), src=(1 - DEPTH, 0), gain=(1 - DEPTH, 1), first=(1 - DEPTH, 1), diag=(0, 1),
        wx=(1 - DEPTH, 0), wy=(-1, 0), wz=(-1, 0), pres=(-1, 2),
    )
    return early, late


EARLY = ("q", "src", "gain", "first", "diag", "wx", "wy", "wz", "pres")
LATE_KEPT = ("src", "gain", "wx", "wy", "wz", "pres")
LATE_SCRATCH = ("q", "first", "diag")


def span_shape(span, wide, layers):
    return (span[1] - span[0], wide, layers)


def joined(rows, name, early_ref, late_ref):
    early, late = (d[name] for d in spans(rows))
    return Rows((early_ref, early[0], early[1] - early[0]), (late_ref, late[0], late[1] - late[0]))


def coarse_rows(pair, couples, tile_w):
    t = pair.reshape(couples, 2, tile_w, pair.shape[1])
    return pack_pairs(t[:, 0], t[:, 1], 2)


def tile_kernel(tiles, conduct, route, coef, touched):
    rows, cols, layers = conduct.shape
    tile_w = cols // tiles
    couples = tiles // 2
    even_lane = iota((tile_w, layers), 1) % 2 == 0
    for t in range(couples):
        numbers = [jnp.broadcast_to(route[0:1, i : i + 1], (tile_w, layers)) for i in (2 * t, 2 * t + 1)]
        touched[t] = jnp.where(jnp.where(even_lane, *numbers) >= 0, 1.0, 0.0)

    packs = rows // 4
    by_row = [
        coarse_rows(0.125 * (conduct[2 * k] + conduct[2 * k + 1]), couples, tile_w)
        for k in range(rows // 2)
    ]
    con = [pack_pairs(by_row[k], by_row[k + packs], 1) for k in range(packs)]
    shape = (couples, tile_w, layers)
    tile_col, tile_lane = iota(shape, 1), iota(shape, 2)
    even_col = tile_col % 2 == 0
    y_end, y_start = tile_col >= tile_w - 2, tile_col < 2
    z_end, z_start = tile_lane >= layers - 2, tile_lane < 2
    for k in range(packs - 1):
        coef[3 * packs + 2 + k] = 2.0 * (con[k] + con[k + 1])
    middle = 2.0 * (con[packs - 1] + roll(con[0], -1, 1))
    coef[3 * packs] = jnp.where(even_col, middle, 0.0)
    coef[3 * packs + 1] = jnp.where(even_col, 0.0, roll(middle, 1, 1))
    for k in range(packs):
        c = con[k]
        y_high = jnp.where(y_end, 0.0, roll(c, -2, 1))
        z_high = jnp.where(z_end, 0.0, roll(c, -2, 2))
        y_low = jnp.where(y_start, 0.0, roll(c, 2, 1))
        z_low = jnp.where(z_start, 0.0, roll(c, 2, 2))
        total = 6.0 * c + (y_high + y_low) + (z_high + z_low)
        if k > 0:
            total = total + con[k - 1]
        else:
            total = total + jnp.where(even_col, 0.0, roll(con[packs - 1], 1, 1))
        if k < packs - 1:
            total = total + con[k + 1]
        else:
            total = total + jnp.where(even_col, roll(con[0], -1, 1), 0.0)
        total = 2.0 * total
        coef[k] = OMEGA / jnp.where(total > 0.0, total, 1.0)
        coef[packs + k] = jnp.where(y_end, 0.0, 2.0 * (c + y_high))
        coef[2 * packs + k] = jnp.where(z_end, 0.0, 2.0 * (c + z_high))


def early_kernel(nd, nc, tiles, rhs, conduct, even, *refs):
    rows, cols, layers = conduct.shape
    tile_w = cols // tiles
    couples = tiles // 2
    n_cross = len(pairings(nc))
    strips = refs[:n_cross]
    *arrays, res_coarse, res_row, part, sums = refs[n_cross:]
    early, _ = spans(rows)
    at = {n: Rows((r, early[n][0], r.shape[0])) for n, r in zip(EARLY, arrays)}
    q, src, gain, first, diag, wx, wy, wz, pres = (at[n] for n in EARLY)
    frame = Frame(nd, nc, cols, layers)
    own, halo = frame.own, frame.halo

    for x in range(rows):
        q[x] = frame.row(conduct[x], frame.merged(strips, unpack_row, 0, x))
        edge = frame.merged(strips, unpack_source, rows // 2, rows, x)
        src[x] = frame.row(rhs[counted(x, rows)], edge)
    _, valid = facing(lax.axis_index("down"), nd, False)
    for i in range(DEPTH):
        corner = frame.merged(strips, unpack_corner, rows - 1, i)
        q[rows + i] = jnp.where(valid, frame.row(even[i], corner), 0.0)
    for i in range(DEPTH - 1):
        corner = frame.merged(strips, unpack_corner, rows - 1, DEPTH + i)
        src[rows + i] = jnp.where(valid, frame.row(even[DEPTH + i], corner), 0.0)

    here = q[0]
    above = jnp.where(frame.last_lane, 0.0, roll(here, -1, 1))
    frame.plane_weights(wy, wz, 0, here, roll(here, -1, 0), above)
    wx[0] = 0.5 * (here + q[1])
    part[0] = frame.doubled(None, here, q[1])[0]
    for x in range(*early["gain"]):
        frame.weights(
            q, gain, src, first,
            diag if x < rows else None,
            wx if x < early["wx"][1] else None,
            wy if x < early["wy"][1] else None,
            wz, x, valid if x >= rows else None,
        )
    for x in range(*early["pres"]):
        pres[x] = smooth(first, gain, src, wx, wy, wz, x)

    spread = gather(first[1], None, first[2], None, wx[1], wy[1], wz[1])
    part[1] = KEEP * first[1] + gain[1] * (src[1] + spread)
    part[2] = gain[1] * wx[0]
    spread = gather(pres[2], None, pres[3], None, wx[2], wy[2], wz[2])
    part[3] = src[2] - diag[2] * pres[2] + spread

    res = {x: residual(frame, src, diag, pres, wx, wy, wz, x) for x in range(3, rows)}
    res_row[...] = res[3]
    for k in range(2, rows // 2):
        res_coarse[k - 2] = coarse_rows(res[2 * k] + res[2 * k + 1], couples, tile_w)

    strip_col = iota((STRIP, layers), 0)
    plane = sum(q[x][own] for x in range(rows))
    beyond = sum(q[x][halo] for x in range(rows))
    own_lane = iota((cols, layers), 1)
    low, high = strip_col < 2, strip_col >= STRIP - 2
    sums[0:1] = fold(sum(res.values()))
    sums[1:2] = fold(sum(q[x][own] for x in range(rows - 2, rows + 2)))
    sums[2:3] = fold(jnp.where(high, plane[cols - STRIP :], 0.0) + jnp.where(low, beyond, 0.0))
    sums[3:4] = fold(jnp.where(low, plane[:STRIP], 0.0) + jnp.where(high, beyond, 0.0))
    sums[4:5] = fold(jnp.where((own_lane < 2) | (own_lane >= layers - 2), plane, 0.0))


def late_kernel(nd, nc, tiles, rows, odd, *refs):
    n_cross = len(pairings(nc)) if len(pairings(nd)) > 1 else 0
    corners = refs[:n_cross]
    n_in = n_cross + len(EARLY) + 6
    early_refs = dict(zip(EARLY, refs[n_cross:]))
    res_coarse, res_row, part, sums, coef, touched = refs[n_in - 6 : n_in]
    names = LATE_KEPT + ("fix", "near", "far", "chunks_hbm") + LATE_SCRATCH + ("chunks", "sem")
    n_side = len(pairings(nc))
    sides = refs[n_in : n_in + n_side]
    late_refs = dict(zip(names, refs[n_in + n_side :]))
    fix_out, near_out, far_out = (late_refs[n] for n in ("fix", "near", "far"))
    chunks_hbm, chunks, sem = (late_refs[n] for n in ("chunks_hbm", "chunks", "sem"))
    wide, layers = early_refs["q"].shape[1:]
    cols = wide - STRIP
    tile_w = cols // tiles
    couples = tiles // 2
    down = lax.axis_index("down")
    even = down % 2 == 0
    q, src, gain, first, diag, wx, wy, wz, pres = (
        joined(rows, n, early_refs[n], late_refs[n]) for n in EARLY
    )
    frame = Frame(nd, nc, cols, layers)
    _, late = spans(rows)

    valid = beside(down, nd, jnp.where(even, -1, 1))
    for i in range(DEPTH):
        corner = frame.merged(corners, unpack_corner, 0, i)
        q[-1 - i] = jnp.where(valid, frame.row(odd[i], corner), 0.0)
    for i in range(DEPTH - 1):
        corner = frame.merged(corners, unpack_corner, 0, DEPTH + i)
        src[-1 - i] = jnp.where(valid, frame.row(odd[DEPTH + i], corner), 0.0)
    for x in range(*late["wx"]):
        frame.weights(
            q, gain, src, first, None, wx, wy if x == -1 else None, wz, x, valid
        )
    doubled = part[0] + q[-1]
    gain[0] = frame.gain_of(doubled)
    first[0] = gain[0] * src[0]
    diag[0] = 0.5 * doubled
    for x in (-1, 0):
        pres[x] = smooth(first, gain, src, wx, wy, wz, x)
    pres[1] = part[1] + part[2] * first[0]
    res = [residual(frame, src, diag, pres, wx, wy, wz, x) for x in (0, 1)]
    res.append((part[3] + wx[1] * pres[1])[frame.own])
    res.append(res_row[...])

    res_total = sums[0:1] + fold(res[0] + res[1] + res[2])
    link_odd = fold(sum(q[x][frame.own] for x in range(-2, 2)))
    link_even, link_cross, link_back, ends = (sums[i : i + 1] for i in range(1, 5))
    outflow = link_even + link_odd + link_cross + link_back + ends
    link_down = jnp.where(even, link_even, link_odd)
    lines = jnp.concatenate([res_total, 0.25 * link_down, 0.25 * link_cross, 0.25 * outflow])
    lines = jnp.sum(lines, axis=1, keepdims=True)
    line = iota((1, layers), 1)
    summary = jnp.zeros((1, layers), FLOAT)
    for i in range(4):
        summary = jnp.where(line == 2 * i + 1, lines[i : i + 1], summary)

    packs = rows // 4
    by_row = [coarse_rows(res[2 * k] + res[2 * k + 1], couples, tile_w) for k in range(2)]
    by_row += [res_coarse[k] for k in range(rows // 2 - 2)]
    r = [pack_pairs(by_row[k], by_row[k + packs], 1) for k in range(packs)]
    middle_low, middle_high = coef[3 * packs], coef[3 * packs + 1]
    fix = [coef[k] * r[k] for k in range(packs)]
    for _ in range(BLOCK_SWEEPS - 1):
        updated = []
        for k in range(packs):
            value, link_y, link_z = fix[k], coef[packs + k], coef[2 * packs + k]
            acc = r[k] + link_y * roll(value, -2, 1) + roll(link_y * value, 2, 1)
            acc = acc + link_z * roll(value, -2, 2) + roll(link_z * value, 2, 2)
            if k > 0:
                acc = acc + coef[3 * packs + 1 + k] * fix[k - 1]
            else:
                acc = acc + middle_high * roll(fix[packs - 1], 1, 1)
            if k < packs - 1:
                acc = acc + coef[3 * packs + 2 + k] * fix[k + 1]
            else:
                acc = acc + middle_low * roll(fix[0], -1, 1)
            updated.append(KEEP * value + coef[k] * acc)
        fix = updated
    fix = [jnp.where(touched[...] > 0.0, f, 0.0) for f in fix]
    for k in range(packs):
        fix_out[k] = fix[k]

    parts = [unpack_pairs(fix[k % packs], 1)[k // packs] for k in range(rows // 2)]
    count = nd * nc
    for i in range(CHUNK):
        part = summary[:, i * LANES : (i + 1) * LANES]
        chunks[pl.ds(i, count, stride=CHUNK), :] = jnp.broadcast_to(part, (count, LANES))
    cross = lax.axis_index("cross")
    odd_step = jnp.where(even, -1, 1)
    edges = {}
    for dy in (-1, 1):
        at_couple, at_col = (0, 0) if dy < 0 else (couples - 1, tile_w - 1)
        edge = jnp.concatenate([p[at_couple][at_col : at_col + 1] for p in parts])
        edges[dy] = edge = unpack_pairs(edge, 1)[0 if dy < 0 else 1]
        for k, step in ((0, odd_step), (rows // 2 - 1, -odd_step)):

            @pl.when(beside(cross, nc, dy) & beside(down, nd, step))
            def _(k=k, step=step, dy=dy, edge=edge):
                both = jnp.where(line % 2 == 0, edge[k : k + 1], summary)
                at = ((cross + dy) * nd + down + step) * CHUNK
                for i in range(CHUNK):
                    chunks[pl.ds(at + i, 1), :] = both[:, i * LANES : (i + 1) * LANES]

    copy = pltpu.make_async_copy(chunks, chunks_hbm, sem)
    copy.start()

    sub = iota((tile_w, layers), 0) % couples
    for out, k, x in ((far_out, 0, 1), (near_out, rows // 2 - 1, rows - 2)):
        packed = parts[k][0]
        for t in range(1, couples):
            packed = jnp.where(sub == t, parts[k][t], packed)
        out[cols:] = packed
        fine = jnp.stack(unpack_pairs(parts[k], 2), axis=1).reshape(cols, layers)
        out[:cols] = pres[x][frame.own] + fine
    for cross_kind, out in zip(pairings(nc), sides):
        right, _ = facing(cross, nc, cross_kind)
        out[: rows // 2] = jnp.where(right, edges[1], edges[-1])
    copy.wait()


def coarse_solve(totals, outflow, link_down, link_up, link_cross):
    nc = len(totals)

    def operate(v):
        out = []
        for c in range(nc):
            image = outflow[c] * v[c] - link_down[c] * roll(v[c], -1, 0) - link_up[c] * roll(v[c], 1, 0)
            if c < nc - 1:
                image = image - link_cross[c] * v[c + 1]
            if c > 0:
                image = image - link_cross[c - 1] * v[c - 1]
            out.append(image)
        return out

    def dot(a, b):
        return jnp.sum(sum(x * y for x, y in zip(a, b)), axis=0, keepdims=True)

    answer = [jnp.zeros_like(t) for t in totals]
    resid = search = totals
    image = operate(resid)
    norm, bend = dot(resid, resid), dot(resid, image)
    alpha = norm / bend
    for step in range(COARSE_ITERS):
        answer = [a + alpha * s for a, s in zip(answer, search)]
        if step == COARSE_ITERS - 1:
            break
        scale = 1.0 / norm
        resid = [r - alpha * m for r, m in zip(resid, image)]
        moved = operate(resid)
        norm, bend = dot(resid, resid), dot(resid, moved)
        beta = norm * scale
        alpha = norm / (bend - beta * norm / alpha)
        search = [r + beta * s for r, s in zip(resid, search)]
        image = [m + beta * i for m, i in zip(moved, image)]
    return answer


KEPT = ("src", "gain", "wx", "wy", "wz")


def around(nd, nc, step, dy):
    row = jnp.clip(lax.axis_index("down") + step, 0, nd - 1)
    return row, jnp.clip(lax.axis_index("cross") + dy, 0, nc - 1)


def fine_row(packed, couples):
    sub = iota(packed.shape, 0) % couples
    parts = []
    for t in range(couples):
        tall = jnp.where(sub == t, packed, 0.0)
        for s in range(couples):
            if s != t:
                tall = tall + jnp.where(sub == s, roll(packed, s - t, 0), 0.0)
        parts += unpack_pairs(tall, 1)
    return jnp.concatenate(parts, axis=0)


def strip_mask(nc, layers):
    cross, half = lax.axis_index("cross"), STRIP // 2
    col = iota((STRIP, layers), 0)
    there = (col < jnp.where(cross < nc - 1, half, 0)) | (col >= jnp.where(cross > 0, half, STRIP))
    return there, col < half


def sides_of(nd):
    down = lax.axis_index("down")
    step = jnp.where(down % 2 == 0, -1, 1)
    return step, beside(down, nd, step), beside(down, nd, -step)


def base_kernel(nd, nc, tiles, near, far, fix, pres_early, pres_late, *refs):
    n_side = len(pairings(nc))
    sides = refs[:n_side]
    early = dict(zip(KEPT, refs[n_side:]))
    late = dict(zip(KEPT, refs[n_side + len(KEPT) :]))
    out, pres_ref, third_ref = refs[n_side + 2 * len(KEPT) :]
    packs, couples, tile_w, layers = fix.shape
    rows, cols = 4 * packs, tiles * tile_w
    src, gain, wx, wy, wz = (joined(rows, n, early[n], late[n]) for n in KEPT)
    start = joined(rows, "pres", pres_early, pres_late)
    own, halo = slice(0, cols), slice(cols, cols + STRIP)
    frame = Frame(nd, nc, cols, layers)
    pres = Rows((pres_ref, -2, rows + 4))
    third = Rows((third_ref, -1, rows + 2))
    for k in range(packs):
        for j, part in enumerate(unpack_pairs(fix[k], 1)):
            both = unpack_pairs(part, 2)
            fine = jnp.stack(both, axis=1).reshape(cols, layers)
            row = k + j * packs
            edge = jnp.zeros((STRIP, layers), FLOAT)
            for place, side in zip(frame.sides, sides):
                edge = jnp.where(place, side[row : row + 1], edge)
            for x in (2 * row, 2 * row + 1):
                pres_ref[x + 2, own, :] = start[x][own] + fine
                pres_ref[x + 2, halo, :] = start[x][halo] + edge
    _, odd_there, even_there = sides_of(nd)
    for message, there, xs in ((near, even_there, (rows, rows + 1)), (far, odd_there, (-1, -2))):
        rim = jnp.where(there, fine_row(message[cols:], couples), 0.0)
        pres_ref[xs[0] + 2, own, :] = start[xs[0]][own] + rim
        pres_ref[xs[0] + 2, halo, :] = start[xs[0]][halo]
        pres_ref[xs[1] + 2, own, :] = jnp.where(there, message[:cols], 0.0)
        pres_ref[xs[1] + 2, halo, :] = jnp.zeros((STRIP, layers), FLOAT)
    for x in range(-1, rows + 1):
        third[x] = smooth(pres, gain, src, wx, wy, wz, x)
    for x in range(rows):
        out[x] = smooth(third, gain, src, wx, wy, wz, x)[own]


def plain_sweep(field, gain, wx, wy, wz, x):
    total = 0.0
    if x in field:
        value = field[x]
        total = wy[x] * roll(value, -1, 0) + roll(wy[x] * value, 1, 0)
        total = total + wz[x] * roll(value, -1, 1) + roll(wz[x] * value, 1, 1)
    if x + 1 in field:
        total = total + wx[x] * field[x + 1]
    if x - 1 in field:
        total = total + wx[x - 1] * field[x - 1]
    total = gain[x] * total
    return KEEP * field[x] + total if x in field else total


def response_kernel(nd, nc, rows, *refs):
    early = dict(zip(KEPT, refs))
    late = dict(zip(KEPT, refs[len(KEPT) :]))
    every, by_odd, by_even, by_side, by_corner = refs[2 * len(KEPT) :]
    _, gain, wx, wy, wz = (joined(rows, n, early[n], late[n]) for n in KEPT)
    cols, layers = every.shape[1:]
    _, odd_there, even_there = sides_of(nd)
    there, _ = strip_mask(nc, layers)
    strip = jnp.where(there, 1.0, 0.0)
    blank = jnp.zeros((cols, layers), FLOAT)
    ones = jnp.ones((cols, layers), FLOAT)
    row_all = jnp.concatenate([ones, strip])
    row_own = jnp.concatenate([ones, jnp.zeros((STRIP, layers), FLOAT)])
    row_strip = jnp.concatenate([blank, strip])

    def sweeps(field, first, second):
        once = {x: plain_sweep(field, gain, wx, wy, wz, x) for x in first}
        return [plain_sweep(once, gain, wx, wy, wz, x)[:cols] for x in second]

    def ends(value):
        return value[:STRIP], value[cols - STRIP :]

    def put(ref, x, value):
        ref[x, :STRIP, :], ref[x, STRIP:, :] = ends(value)

    odd_row, even_row = (jnp.where(t, row_own, 0.0) for t in (odd_there, even_there))
    field = {x: row_all for x in range(rows)}
    field |= {-2: odd_row, rows + 1: even_row}
    field |= {-1: jnp.where(odd_there, row_all, 0.0), rows: jnp.where(even_there, row_all, 0.0)}
    for x, value in enumerate(sweeps(field, range(-1, rows + 1), range(rows))):
        every[x] = value
    for x, value in enumerate(sweeps({-2: odd_row, -1: odd_row}, (-1, 0), (0, 1))):
        by_odd[x] = value
    field = {rows: even_row, rows + 1: even_row}
    for x, value in enumerate(sweeps(field, (rows - 1, rows), (rows - 2, rows - 1))):
        by_even[x] = value
    field = {x: row_strip for x in range(rows)}
    for x, value in enumerate(sweeps(field, range(-1, rows + 1), range(rows))):
        put(by_side, x, value)
    for i, (at, x, t) in enumerate(((-1, 0, odd_there), (rows, rows - 1, even_there))):
        field = {at: jnp.where(t, row_strip, 0.0)}
        put(by_corner, i, sweeps(field, (at, x), (x,))[0])


def last_kernel(nd, nc, got, base, every, by_odd, by_even, by_side, by_corner, *refs):
    out, new, bricks, sems = refs
    rows, cols, layers = out.shape
    down, cross = lax.axis_index("down"), lax.axis_index("cross")
    even = down % 2 == 0

    tables = [got[pl.ds(c * nd * CHUNK, nd, stride=CHUNK), :] for c in range(nc)]

    def spread_lane(table, at):
        return jnp.broadcast_to(table[:, 2 * at + 1 : 2 * at + 2], (nd, LANES))

    last = iota((nd, LANES), 0) == nd - 1
    totals = [spread_lane(t, 0) for t in tables]
    link_down = [jnp.where(last, 0.0, spread_lane(t, 1)) for t in tables]
    link_up = [roll(link, 1, 0) for link in link_down]
    link_cross = [spread_lane(t, 2) for t in tables]
    outflow = [spread_lane(t, 3) for t in tables]
    answer = coarse_solve(totals, outflow, link_down, link_up, link_cross)
    for c in range(nc):
        bricks[c] = answer[c]

    def brick(step, dy):
        row, col = around(nd, nc, step, dy)
        return jnp.concatenate([bricks[col, pl.ds(row, 1), :]] * (layers // LANES), axis=1)

    def corner(step, dy):
        row, col = around(nd, nc, step, dy)
        at = (col * nd + row) * CHUNK
        both = jnp.concatenate([got[pl.ds(at + i, 1), :] for i in range(CHUNK)], axis=1)
        return unpack_pairs(both, 1)[0] + brick(step, dy) - mine

    odd_step, _, _ = sides_of(nd)
    mine = brick(0, 0)
    more_odd, more_even = brick(odd_step, 0) - mine, brick(-odd_step, 0) - mine
    more_side = brick(0, -1) - mine, brick(0, 1) - mine
    more_corner = [[corner(step, dy) for dy in (-1, 1)] for step in (odd_step, -odd_step)]
    halves = slice(0, STRIP), slice(STRIP, 2 * STRIP)
    ends = slice(0, STRIP), slice(cols - STRIP, cols)
    copies = []
    for x in reversed(range(rows)):
        at = counted(x, rows)
        value = base[x] + mine * every[x]
        if x < 2:
            value = value + more_odd * by_odd[x]
        if x >= rows - 2:
            value = value + more_even * by_even[x - (rows - 2)]
        new[at] = value
        for end, half, side, odd_corner, even_corner in zip(ends, halves, more_side, *more_corner):
            part = value[end] + side * by_side[x, half, :]
            if x == 0:
                part = part + odd_corner * by_corner[0, half, :]
            if x == rows - 1:
                part = part + even_corner * by_corner[1, half, :]
            new[at, end, :] = part
        if x % 2 == 0:
            span = pl.ds(jnp.where(even, x, rows - 2 - x), 2)
            copies.append(pltpu.make_async_copy(new.at[span], out.at[span], sems.at[len(copies)]))
            copies[-1].start()
    for copy in copies:
        copy.wait()


def whole(*shape):
    return jax.ShapeDtypeStruct(shape, FLOAT)


def call(kernel, out_shape, spaces, scratch=(), vmem_bytes=VMEM_BYTES, out_spaces=None):
    return pl.pallas_call(
        kernel,
        out_shape=out_shape,
        in_specs=[pl.BlockSpec(memory_space=s) for s in spaces],
        out_specs=jax.tree.map(
            lambda _, s: pl.BlockSpec(memory_space=s),
            out_shape,
            out_spaces or jax.tree.map(lambda _: pltpu.VMEM, out_shape),
        ),
        scratch_shapes=list(scratch),
        compiler_params=pltpu.CompilerParams(vmem_limit_bytes=vmem_bytes),
    )


def body(nd, nc, right_side, kappa, band_mask, tile_route):
    rows, cols, layers = right_side.shape
    tiles = tile_route.shape[1]
    axes = ("down", "cross")
    wide = cols + STRIP
    block = whole(rows, cols, layers)
    vmem = pltpu.VMEM
    early, late = spans(rows)

    shapes, perms = [], []
    for kind in pairings(nd):
        shapes.append(whole(2 * DEPTH - 1, cols, layers))
        perms.append(pairs_of(nd, nc, kind, None))
        if kind:
            for cross_kind in pairings(nc):
                shapes.append(whole(CORNER, STRIP, layers))
                perms.append(pairs_of(nd, nc, kind, cross_kind))
    strips = [whole(rows - 1, STRIP, layers) for _ in pairings(nc)]
    packs, couples, tile_w = rows // 4, tiles // 2, cols // tiles
    tile_shape = (couples, tile_w, layers)
    conduct, *messages = call(
        functools.partial(pack_kernel, nd, nc),
        [block] + shapes + strips,
        [pltpu.HBM] * 3,
        scratch=[
            pltpu.VMEM((rows, cols, layers), FLOAT),
            pltpu.VMEM((rows, cols, layers), FLOAT),
            pltpu.VMEM((rows, cols, layers), band_mask.dtype),
            pltpu.SemaphoreType.DMA((3,)),
        ],
        vmem_bytes=54400 * 1024,
    )(right_side, kappa, band_mask)

    received = [lax.ppermute(m, axes, p) for m, p in zip(messages, perms)]
    even, odd = received[0], received[1:]
    if strips:
        strips = call(
            functools.partial(strip_kernel, nd, nc),
            [whole(rows - 1 + CORNER, STRIP, layers) for _ in strips],
            [vmem] * (1 + len(strips)),
        )(even, *messages[len(perms) :])
        strips = [
            lax.ppermute(m, axes, pairs_of(nd, nc, None, cross_kind))
            for m, cross_kind in zip(strips, pairings(nc))
        ]
    if not odd:
        odd = [jnp.zeros((2 * DEPTH - 1, cols, layers), FLOAT)]

    first_part = call(
        functools.partial(early_kernel, nd, nc, tiles),
        [whole(*span_shape(early[n], wide, layers)) for n in EARLY]
        + [
            whole(rows // 2 - 2, *tile_shape),
            whole(cols, layers),
            whole(4, wide, layers),
            whole(5, LANES),
        ],
        [vmem] * (3 + len(strips)),
    )(right_side, conduct, even, *strips)
    first_part += call(
        functools.partial(tile_kernel, tiles),
        [whole(4 * packs + 1, *tile_shape), whole(*tile_shape)],
        [vmem] * 2,
    )(conduct, tile_route)
    late_arrays = call(
        functools.partial(late_kernel, nd, nc, tiles, rows),
        [whole(STRIP, layers) for _ in pairings(nc)]
        + [whole(*span_shape(late[n], wide, layers)) for n in LATE_KEPT]
        + [
            whole(packs, *tile_shape),
            whole(cols + tile_w, layers),
            whole(cols + tile_w, layers),
            whole(nd * nc * CHUNK, LANES),
        ],
        [vmem] * (len(odd) + len(first_part)),
        scratch=[pltpu.VMEM(span_shape(late[n], wide, layers), FLOAT) for n in LATE_SCRATCH]
        + [pltpu.VMEM((nd * nc * CHUNK, LANES), FLOAT), pltpu.SemaphoreType.DMA],
        out_spaces=[vmem] * (len(pairings(nc)) + len(LATE_KEPT) + 3) + [pltpu.HBM],
    )(*odd, *first_part)
    n_side = len(pairings(nc))
    sides, late_arrays = late_arrays[:n_side], late_arrays[n_side:]
    *late_arrays, fix, near, far, chunks = late_arrays
    early_arrays = dict(zip(EARLY, first_part))
    late_arrays = dict(zip(LATE_KEPT, late_arrays))
    kept = [d[n] for d in (early_arrays, late_arrays) for n in KEPT]

    chunks = chunks.reshape(nd * nc, CHUNK, 1, LANES)
    arrived = lax.all_to_all(chunks, ("cross", "down"), 0, 0, tiled=True).reshape(nd * nc * CHUNK, LANES)
    far = lax.ppermute(far, axes, pairs_of(nd, nc, True, None))
    near = lax.ppermute(near, axes, pairs_of(nd, nc, False, None))
    sides = [
        lax.ppermute(m, axes, pairs_of(nd, nc, None, cross_kind))
        for m, cross_kind in zip(sides, pairings(nc))
    ]
    base = call(
        functools.partial(base_kernel, nd, nc, tiles),
        block,
        [vmem] * (5 + n_side + len(kept)),
        scratch=[
            pltpu.VMEM((rows + 4, wide, layers), FLOAT),
            pltpu.VMEM((rows + 2, wide, layers), FLOAT),
        ],
    )(near, far, fix, early_arrays["pres"], late_arrays["pres"], *sides, *kept)
    responses = call(
        functools.partial(response_kernel, nd, nc, rows),
        [
            block,
            whole(2, cols, layers),
            whole(2, cols, layers),
            whole(rows, 2 * STRIP, layers),
            whole(2, 2 * STRIP, layers),
        ],
        [vmem] * len(kept),
    )(*kept)
    return call(
        functools.partial(last_kernel, nd, nc),
        block,
        [vmem] * (2 + len(responses)),
        scratch=[
            pltpu.VMEM((rows, cols, layers), FLOAT),
            pltpu.VMEM((nc, nd, LANES), FLOAT),
            pltpu.SemaphoreType.DMA((rows // 2,)),
        ],
        out_spaces=pltpu.HBM,
    )(arrived, base, *responses)


def solution(mesh):
    return jax.shard_map(
        functools.partial(body, mesh.shape["down"], mesh.shape["cross"]),
        mesh=mesh,
        in_specs=(
            P("down", "cross", None),
            P("down", "cross", None),
            P("down", "cross", None),
            P("down", "cross"),
        ),
        out_specs=P("down", "cross", None),
        check_vma=False,
    )
```

```python
import functools

import jax
import jax.numpy as jnp
from jax import lax
from jax.experimental import pallas as pl
from jax.experimental.pallas import tpu as pltpu
from jax.sharding import PartitionSpec as P

BLOCK_SWEEPS = 4
COARSE_ITERS = 12
OMEGA = 0.8
KEEP = 1.0 - OMEGA
SNOW_FACTOR = 3.0

DEPTH = 3
CORNER = 2
STRIP = 8
LANES = 128
CHUNK = 2
FLOAT = jnp.float32
VMEM_BYTES = 24 * 1024 * 1024


def partners(count, odd):
    found = []
    for i in range(count):
        j = ((i + 1) ^ 1) - 1 if odd else i ^ 1
        found.append(j if 0 <= j < count else i)
    return found


def pairings(count):
    return [k for k in (False, True) if any(j != i for i, j in enumerate(partners(count, k)))]


def pairs_of(count_down, count_cross, down_kind, cross_kind):
    rows = list(range(count_down)) if down_kind is None else partners(count_down, down_kind)
    cols = list(range(count_cross)) if cross_kind is None else partners(count_cross, cross_kind)
    return [
        (i * count_cross + j, rows[i] * count_cross + cols[j])
        for i in range(count_down)
        for j in range(count_cross)
    ]


def facing(index, count, kind):
    ahead = (index % 2 == 0) != kind
    return ahead, jnp.where(ahead, index < count - 1, index > 0)


def beside(index, count, step):
    return (index + step >= 0) & (index + step < count)


def roll(x, amount, axis):
    return pltpu.roll(x, amount % x.shape[axis], axis)


def iota(shape, axis):
    return lax.broadcasted_iota(jnp.int32, shape, axis)


def gather(value, low, high, wx_low, wx_high, wy, wz):
    total = wx_high * high
    if low is not None:
        total = total + wx_low * low
    total = total + wy * roll(value, -1, 0) + roll(wy * value, 1, 0)
    return total + wz * roll(value, -1, 1) + roll(wz * value, 1, 1)


class Rows:
    def __init__(self, *parts):
        self.parts = parts

    def place(self, x):
        for ref, first, count in self.parts:
            if first <= x < first + count:
                return ref, x - first
        raise IndexError(x)

    def __getitem__(self, x):
        ref, i = self.place(x)
        return ref[i]

    def __setitem__(self, x, value):
        ref, i = self.place(x)
        ref[i] = value


def smooth(field, gain, src, wx, wy, wz, x):
    spread = gather(field[x], field[x - 1], field[x + 1], wx[x - 1], wx[x], wy[x], wz[x])
    return KEEP * field[x] + gain[x] * (src[x] + spread)


def counted(x, rows):
    return jnp.where(lax.axis_index("down") % 2 == 0, x, rows - 1 - x)


def edge_strip(right, cols):
    return pl.ds(pl.multiple_of(jnp.where(right, cols - STRIP, 0), STRIP), STRIP)


def strip_tiles(rows):
    return rows // 2 - 1 + rows // 4


def upper_half(tile, right):
    return jnp.where(right, roll(tile, STRIP // 2, 0), tile)


def lower_half(tile, right):
    return jnp.where(right, tile, roll(tile, STRIP // 2, 0))


def pack_rows(tiles, right):
    upper = iota(tiles[0].shape, 0) < STRIP // 2
    return [
        jnp.where(upper, upper_half(a, right), lower_half(b, right)) for a, b in zip(tiles[::2], tiles[1::2])
    ]


def pack_pair_columns(tiles, right):
    packed = []
    for i in range(0, len(tiles), 4):
        out = jnp.zeros(tiles[0].shape, FLOAT)
        for j, tile in enumerate(tiles[i : i + 4]):
            half = upper_half(tile, right)
            moved = jnp.where(right, roll(half, 2 * j - 2, 0), roll(half, 2 * j, 0))
            out = jnp.where(iota(out.shape, 0) // 2 == j, moved, out)
        packed.append(out)
    return packed


def unpack_pair_columns(message, start, i, right):
    tile = message[start + i // 4]
    col, j = iota(tile.shape, 0), i % 4
    from_right = jnp.where(col < 2, roll(tile, -2 * j, 0), 0.0)
    from_left = jnp.where(col >= STRIP - 2, roll(tile, STRIP - 2 - 2 * j, 0), 0.0)
    return jnp.where(right, from_right, from_left)


def pack_three(tiles, right):
    *packed, last = pack_rows(tiles, right)
    col = iota(last.shape, 0) % (STRIP // 2)
    free = col == jnp.where(right, 0, 3)
    for m in range(3):
        packed[m] = jnp.where(free, jnp.where(right, roll(last, -1 - m, 0), roll(last, 3 - m, 0)), packed[m])
    return packed


def pack_corner(tiles, right):
    near, far = pack_rows(tiles[:4], right)
    last = upper_half(tiles[4], right)
    free = iota(last.shape, 0) == jnp.where(right, 0, 3)
    return [near, jnp.where(free, jnp.where(right, roll(last, -3, 0), roll(last, 3, 0)), far)]


def unpack_row(message, start, i, right):
    tile = message[start + i // 2]
    return jnp.where(right == (i % 2 == 0), tile, roll(tile, STRIP // 2, 0))


def unpack_three(message, start, rows, i, right):
    if i < rows - 2:
        return unpack_row(message, start, i, right)
    tiles = [message[start + m] for m in range(3)]
    col = iota(tiles[0].shape, 0) % (STRIP // 2)
    last = jnp.zeros(tiles[0].shape, FLOAT)
    for m, tile in enumerate(tiles):
        from_right = jnp.where(col == m, roll(tile, m - 3, 0), last)
        last = jnp.where(right, from_right, jnp.where(col == m + 1, roll(tile, m + 1, 0), last))
    return jnp.where(right == (i % 2 == 0), last, roll(last, STRIP // 2, 0))


def unpack_corner(message, start, i, right):
    if i < 2 or i == 3:
        return unpack_row(message, start, i, right)
    tile = message[start + 1]
    col = iota(tile.shape, 0)
    if i == 2:
        tile = jnp.where(col == jnp.where(right, 3, 0), 0.0, tile)
    else:
        place = col == jnp.where(right, 0, 3)
        tile = jnp.where(place, jnp.where(right, roll(tile, -3, 0), roll(tile, 3, 0)), 0.0)
    return jnp.where(right, tile, roll(tile, STRIP // 2, 0))


def put_tiles(out, start, tiles):
    for i, tile in enumerate(tiles):
        out[start + i] = tile


def pack_kernel(nd, nc, rhs_hbm, kappa_hbm, mask_hbm, conduct, *refs):
    *messages, rhs, kappa, mask, sems = refs
    rows, cols, _ = rhs.shape
    messages = iter(messages)
    cross = lax.axis_index("cross")
    copies = [
        pltpu.make_async_copy(src, dst, sems.at[i])
        for i, (src, dst) in enumerate(((kappa_hbm, kappa), (mask_hbm, mask), (rhs_hbm, rhs)))
    ]
    for copy in copies:
        copy.start()
    copies[0].wait()
    copies[1].wait()
    for x in range(rows):
        at = counted(x, rows)
        conduct[x] = kappa[at] / (1.0 + SNOW_FACTOR * mask[at].astype(FLOAT))
    copies[2].wait()
    for kind in pairings(nd):
        near = [i if kind else rows - 1 - i for i in range(DEPTH)]
        out = next(messages)
        for i, x in enumerate(near):
            out[i] = conduct[x]
        for i, x in enumerate(near[:-1]):
            out[DEPTH + i] = rhs[counted(x, rows)]
        if kind:
            for cross_kind in pairings(nc):
                right, _ = facing(cross, nc, cross_kind)
                strip = edge_strip(right, cols)
                tiles = [conduct[x, strip, :] for x in near]
                tiles += [rhs[counted(x, rows), strip, :] for x in near[:-1]]
                put_tiles(next(messages), 0, pack_corner(tiles, right))
    for cross_kind in pairings(nc):
        right, _ = facing(cross, nc, cross_kind)
        strip = edge_strip(right, cols)
        tiles = pack_three([conduct[x, strip, :] for x in range(rows)], right)
        tiles += pack_pair_columns([rhs[counted(x, rows), strip, :] for x in range(rows)], right)
        put_tiles(next(messages), 0, tiles)


def strip_kernel(nd, nc, even, *refs):
    cols = even.shape[1]
    count = len(pairings(nc))
    for cross_kind, own, out in zip(pairings(nc), refs[:count], refs[count:]):
        right, _ = facing(lax.axis_index("cross"), nc, cross_kind)
        strip = edge_strip(right, cols)
        count = own.shape[0]
        out[:count] = own[...]
        put_tiles(out, count, pack_corner([even[i, strip, :] for i in range(2 * DEPTH - 1)], right))


def fold(x):
    x = sum(x[:, i : i + LANES] for i in range(0, x.shape[1], LANES))
    return jnp.sum(x, axis=0, keepdims=True)


def swap_pairs(x, axis):
    return jnp.where(iota(x.shape, axis) % 2 == 0, roll(x, -1, axis), roll(x, 1, axis))


def pack_pairs(a, b, axis):
    even = iota(a.shape, axis) % 2 == 0
    return jnp.where(even, a, b) + swap_pairs(jnp.where(even, b, a), axis)


def unpack_pairs(x, axis):
    even = iota(x.shape, axis) % 2 == 0
    return jnp.where(even, x, roll(x, 1, axis)), jnp.where(even, roll(x, -1, axis), x)


class Frame:
    def __init__(self, nd, nc, cols, layers):
        self.cols, self.layers, self.wide = cols, layers, cols + STRIP
        self.own, self.halo = slice(0, cols), slice(cols, cols + STRIP)
        cross = lax.axis_index("cross")
        half = STRIP // 2
        self.lane = iota((self.wide, layers), 1)
        self.last_lane = self.lane == layers - 1
        col = iota((self.wide, layers), 0)
        self.col_ok = (col < jnp.where(cross < nc - 1, cols + half, cols)) | (
            col >= jnp.where(cross > 0, cols + half, self.wide)
        )
        halo_col = iota((STRIP, layers), 0)
        self.sides, self.rights = [], []
        for cross_kind in pairings(nc):
            right, valid = facing(cross, nc, cross_kind)
            start = jnp.where(right, 0, half)
            stop = jnp.where(valid, start + half, 0)
            self.sides.append((halo_col >= start) & (halo_col < stop))
            self.rights.append(right)

    def merged(self, messages, unpack, *place):
        total = jnp.zeros((STRIP, self.layers), FLOAT)
        for side, right, message in zip(self.sides, self.rights, messages):
            total = jnp.where(side, unpack(message, *place, right), total)
        return total

    def row(self, own, halo):
        return jnp.concatenate([own, halo], axis=0)

    def doubled(self, low, here, high):
        above = jnp.where(self.last_lane, 0.0, roll(here, -1, 1))
        below = jnp.where(self.lane == 0, 0.0, roll(here, 1, 1))
        right = roll(here, -1, 0)
        ends = high if low is None else low + high
        return 6.0 * here + ends + (right + roll(here, 1, 0)) + (above + below), right, above

    def gain_of(self, doubled, valid=None):
        ok = self.col_ok & (doubled > 0.0)
        if valid is not None:
            ok = ok & valid
        return jnp.where(ok, (2.0 * OMEGA) / doubled, 0.0)

    def weights(self, q, gain, src, first, diag, wx, wy, wz, x, valid=None):
        here = q[x]
        doubled, right, above = self.doubled(q[x - 1], here, q[x + 1])
        gain_here = self.gain_of(doubled, valid)
        gain[x] = gain_here
        first[x] = gain_here * src[x]
        if diag is not None:
            diag[x] = 0.5 * doubled
        if wx is not None:
            wx[x] = 0.5 * (here + q[x + 1])
        if wy is not None:
            self.plane_weights(wy, wz, x, here, right, above)

    def plane_weights(self, wy, wz, x, here, right, above):
        wy[x] = 0.5 * (here + right)
        wz[x] = jnp.where(self.last_lane, 0.0, 0.5 * (here + above))


def residual(frame, src, diag, pres, wx, wy, wz, x):
    spread = gather(pres[x], pres[x - 1], pres[x + 1], wx[x - 1], wx[x], wy[x], wz[x])
    return (src[x] - diag[x] * pres[x] + spread)[frame.own]


def spans(rows):
    early = dict(
        q=(0, rows + DEPTH), src=(0, rows + DEPTH - 1), gain=(1, rows + DEPTH - 1),
        first=(1, rows + DEPTH - 1), diag=(1, rows), wx=(0, rows + 1), wy=(0, rows + 1),
        wz=(0, rows + 1), pres=(2, rows + 1),
    )
    late = dict(
        q=(-DEPTH, 0), src=(1 - DEPTH, 0), gain=(1 - DEPTH, 1), first=(1 - DEPTH, 1), diag=(0, 1),
        wx=(1 - DEPTH, 0), wy=(-1, 0), wz=(-1, 0), pres=(-1, 2),
    )
    return early, late


EARLY = ("q", "src", "gain", "first", "diag", "wx", "wy", "wz", "pres")
LATE_KEPT = ("src", "gain", "wx", "wy", "wz", "pres")
LATE_SCRATCH = ("q", "first", "diag")


def span_shape(span, wide, layers):
    return (span[1] - span[0], wide, layers)


def joined(rows, name, early_ref, late_ref):
    early, late = (d[name] for d in spans(rows))
    return Rows((early_ref, early[0], early[1] - early[0]), (late_ref, late[0], late[1] - late[0]))


def coarse_rows(pair, couples, tile_w):
    t = pair.reshape(couples, 2, tile_w, pair.shape[1])
    return pack_pairs(t[:, 0], t[:, 1], 2)


def tile_kernel(tiles, conduct, route, coef, touched):
    rows, cols, layers = conduct.shape
    tile_w = cols // tiles
    couples = tiles // 2
    even_lane = iota((tile_w, layers), 1) % 2 == 0
    for t in range(couples):
        numbers = [jnp.broadcast_to(route[0:1, i : i + 1], (tile_w, layers)) for i in (2 * t, 2 * t + 1)]
        touched[t] = jnp.where(jnp.where(even_lane, *numbers) >= 0, 1.0, 0.0)

    packs = rows // 4
    by_row = [
        coarse_rows(0.125 * (conduct[2 * k] + conduct[2 * k + 1]), couples, tile_w)
        for k in range(rows // 2)
    ]
    con = [pack_pairs(by_row[k], by_row[k + packs], 1) for k in range(packs)]
    shape = (couples, tile_w, layers)
    tile_col, tile_lane = iota(shape, 1), iota(shape, 2)
    even_col = tile_col % 2 == 0
    y_end, y_start = tile_col >= tile_w - 2, tile_col < 2
    z_end, z_start = tile_lane >= layers - 2, tile_lane < 2
    for k in range(packs - 1):
        coef[3 * packs + 2 + k] = 2.0 * (con[k] + con[k + 1])
    middle = 2.0 * (con[packs - 1] + roll(con[0], -1, 1))
    coef[3 * packs] = jnp.where(even_col, middle, 0.0)
    coef[3 * packs + 1] = jnp.where(even_col, 0.0, roll(middle, 1, 1))
    for k in range(packs):
        c = con[k]
        y_high = jnp.where(y_end, 0.0, roll(c, -2, 1))
        z_high = jnp.where(z_end, 0.0, roll(c, -2, 2))
        y_low = jnp.where(y_start, 0.0, roll(c, 2, 1))
        z_low = jnp.where(z_start, 0.0, roll(c, 2, 2))
        total = 6.0 * c + (y_high + y_low) + (z_high + z_low)
        if k > 0:
            total = total + con[k - 1]
        else:
            total = total + jnp.where(even_col, 0.0, roll(con[packs - 1], 1, 1))
        if k < packs - 1:
            total = total + con[k + 1]
        else:
            total = total + jnp.where(even_col, roll(con[0], -1, 1), 0.0)
        total = 2.0 * total
        coef[k] = OMEGA / jnp.where(total > 0.0, total, 1.0)
        coef[packs + k] = jnp.where(y_end, 0.0, 2.0 * (c + y_high))
        coef[2 * packs + k] = jnp.where(z_end, 0.0, 2.0 * (c + z_high))


def early_kernel(nd, nc, tiles, rhs, conduct, even, *refs):
    rows, cols, layers = conduct.shape
    tile_w = cols // tiles
    couples = tiles // 2
    n_cross = len(pairings(nc))
    strips = refs[:n_cross]
    *arrays, res_coarse, res_row, part, sums = refs[n_cross:]
    early, _ = spans(rows)
    at = {n: Rows((r, early[n][0], r.shape[0])) for n, r in zip(EARLY, arrays)}
    q, src, gain, first, diag, wx, wy, wz, pres = (at[n] for n in EARLY)
    frame = Frame(nd, nc, cols, layers)
    own, halo = frame.own, frame.halo

    for x in range(rows):
        q[x] = frame.row(conduct[x], frame.merged(strips, unpack_three, 0, rows, x))
        edge = frame.merged(strips, unpack_pair_columns, rows // 2 - 1, x)
        src[x] = frame.row(rhs[counted(x, rows)], edge)
    _, valid = facing(lax.axis_index("down"), nd, False)
    for i in range(DEPTH):
        corner = frame.merged(strips, unpack_corner, strip_tiles(rows), i)
        q[rows + i] = jnp.where(valid, frame.row(even[i], corner), 0.0)
    for i in range(DEPTH - 1):
        corner = frame.merged(strips, unpack_corner, strip_tiles(rows), DEPTH + i)
        src[rows + i] = jnp.where(valid, frame.row(even[DEPTH + i], corner), 0.0)

    here = q[0]
    above = jnp.where(frame.last_lane, 0.0, roll(here, -1, 1))
    frame.plane_weights(wy, wz, 0, here, roll(here, -1, 0), above)
    wx[0] = 0.5 * (here + q[1])
    part[0] = frame.doubled(None, here, q[1])[0]
    for x in range(*early["gain"]):
        frame.weights(
            q, gain, src, first,
            diag if x < rows else None,
            wx if x < early["wx"][1] else None,
            wy if x < early["wy"][1] else None,
            wz, x, valid if x >= rows else None,
        )
    for x in range(*early["pres"]):
        pres[x] = smooth(first, gain, src, wx, wy, wz, x)

    spread = gather(first[1], None, first[2], None, wx[1], wy[1], wz[1])
    part[1] = KEEP * first[1] + gain[1] * (src[1] + spread)
    part[2] = gain[1] * wx[0]
    spread = gather(pres[2], None, pres[3], None, wx[2], wy[2], wz[2])
    part[3] = src[2] - diag[2] * pres[2] + spread

    res = {x: residual(frame, src, diag, pres, wx, wy, wz, x) for x in range(3, rows)}
    res_row[...] = res[3]
    for k in range(2, rows // 2):
        res_coarse[k - 2] = coarse_rows(res[2 * k] + res[2 * k + 1], couples, tile_w)

    strip_col = iota((STRIP, layers), 0)
    plane = sum(q[x][own] for x in range(rows))
    beyond = sum(q[x][halo] for x in range(rows))
    own_lane = iota((cols, layers), 1)
    low, high = strip_col < 2, strip_col >= STRIP - 2
    sums[0:1] = fold(sum(res.values()))
    sums[1:2] = fold(sum(q[x][own] for x in range(rows - 2, rows + 2)))
    sums[2:3] = fold(jnp.where(high, plane[cols - STRIP :], 0.0) + jnp.where(low, beyond, 0.0))
    sums[3:4] = fold(jnp.where(low, plane[:STRIP], 0.0) + jnp.where(high, beyond, 0.0))
    sums[4:5] = fold(jnp.where((own_lane < 2) | (own_lane >= layers - 2), plane, 0.0))


def late_kernel(nd, nc, tiles, rows, odd, *refs):
    n_cross = len(pairings(nc)) if len(pairings(nd)) > 1 else 0
    corners = refs[:n_cross]
    n_in = n_cross + len(EARLY) + 6
    early_refs = dict(zip(EARLY, refs[n_cross:]))
    res_coarse, res_row, part, sums, coef, touched = refs[n_in - 6 : n_in]
    names = LATE_KEPT + ("fix", "near", "far", "chunks_hbm") + LATE_SCRATCH + ("chunks", "sem")
    n_side = len(pairings(nc))
    sides = refs[n_in : n_in + n_side]
    late_refs = dict(zip(names, refs[n_in + n_side :]))
    fix_out, near_out, far_out = (late_refs[n] for n in ("fix", "near", "far"))
    chunks_hbm, chunks, sem = (late_refs[n] for n in ("chunks_hbm", "chunks", "sem"))
    wide, layers = early_refs["q"].shape[1:]
    cols = wide - STRIP
    tile_w = cols // tiles
    couples = tiles // 2
    down = lax.axis_index("down")
    even = down % 2 == 0
    q, src, gain, first, diag, wx, wy, wz, pres = (
        joined(rows, n, early_refs[n], late_refs[n]) for n in EARLY
    )
    frame = Frame(nd, nc, cols, layers)
    _, late = spans(rows)

    valid = beside(down, nd, jnp.where(even, -1, 1))
    for i in range(DEPTH):
        corner = frame.merged(corners, unpack_corner, 0, i)
        q[-1 - i] = jnp.where(valid, frame.row(odd[i], corner), 0.0)
    for i in range(DEPTH - 1):
        corner = frame.merged(corners, unpack_corner, 0, DEPTH + i)
        src[-1 - i] = jnp.where(valid, frame.row(odd[DEPTH + i], corner), 0.0)
    for x in range(*late["wx"]):
        frame.weights(
            q, gain, src, first, None, wx, wy if x == -1 else None, wz, x, valid
        )
    doubled = part[0] + q[-1]
    gain[0] = frame.gain_of(doubled)
    first[0] = gain[0] * src[0]
    diag[0] = 0.5 * doubled
    for x in (-1, 0):
        pres[x] = smooth(first, gain, src, wx, wy, wz, x)
    pres[1] = part[1] + part[2] * first[0]
    res = [residual(frame, src, diag, pres, wx, wy, wz, x) for x in (0, 1)]
    res.append((part[3] + wx[1] * pres[1])[frame.own])
    res.append(res_row[...])

    res_total = sums[0:1] + fold(res[0] + res[1] + res[2])
    link_odd = fold(sum(q[x][frame.own] for x in range(-2, 2)))
    link_even, link_cross, link_back, ends = (sums[i : i + 1] for i in range(1, 5))
    outflow = link_even + link_odd + link_cross + link_back + ends
    link_down = jnp.where(even, link_even, link_odd)
    lines = jnp.concatenate([res_total, 0.25 * link_down, 0.25 * link_cross, 0.25 * outflow])
    lines = jnp.sum(lines, axis=1, keepdims=True)
    line = iota((1, layers), 1)
    summary = jnp.zeros((1, layers), FLOAT)
    for i in range(4):
        summary = jnp.where(line == 2 * i + 1, lines[i : i + 1], summary)

    packs = rows // 4
    by_row = [coarse_rows(res[2 * k] + res[2 * k + 1], couples, tile_w) for k in range(2)]
    by_row += [res_coarse[k] for k in range(rows // 2 - 2)]
    r = [pack_pairs(by_row[k], by_row[k + packs], 1) for k in range(packs)]
    middle_low, middle_high = coef[3 * packs], coef[3 * packs + 1]
    fix = [coef[k] * r[k] for k in range(packs)]
    for _ in range(BLOCK_SWEEPS - 1):
        updated = []
        for k in range(packs):
            value, link_y, link_z = fix[k], coef[packs + k], coef[2 * packs + k]
            acc = r[k] + link_y * roll(value, -2, 1) + roll(link_y * value, 2, 1)
            acc = acc + link_z * roll(value, -2, 2) + roll(link_z * value, 2, 2)
            if k > 0:
                acc = acc + coef[3 * packs + 1 + k] * fix[k - 1]
            else:
                acc = acc + middle_high * roll(fix[packs - 1], 1, 1)
            if k < packs - 1:
                acc = acc + coef[3 * packs + 2 + k] * fix[k + 1]
            else:
                acc = acc + middle_low * roll(fix[0], -1, 1)
            updated.append(KEEP * value + coef[k] * acc)
        fix = updated
    fix = [jnp.where(touched[...] > 0.0, f, 0.0) for f in fix]
    for k in range(packs):
        fix_out[k] = fix[k]

    parts = [unpack_pairs(fix[k % packs], 1)[k // packs] for k in range(rows // 2)]
    count = nd * nc
    for i in range(CHUNK):
        part = summary[:, i * LANES : (i + 1) * LANES]
        chunks[pl.ds(i, count, stride=CHUNK), :] = jnp.broadcast_to(part, (count, LANES))
    cross = lax.axis_index("cross")
    odd_step = jnp.where(even, -1, 1)
    edges = {}
    for dy in (-1, 1):
        at_couple, at_col = (0, 0) if dy < 0 else (couples - 1, tile_w - 1)
        edge = jnp.concatenate([p[at_couple][at_col : at_col + 1] for p in parts])
        edges[dy] = edge = unpack_pairs(edge, 1)[0 if dy < 0 else 1]
        for k, step in ((0, odd_step), (rows // 2 - 1, -odd_step)):

            @pl.when(beside(cross, nc, dy) & beside(down, nd, step))
            def _(k=k, step=step, dy=dy, edge=edge):
                both = jnp.where(line % 2 == 0, edge[k : k + 1], summary)
                at = ((cross + dy) * nd + down + step) * CHUNK
                for i in range(CHUNK):
                    chunks[pl.ds(at + i, 1), :] = both[:, i * LANES : (i + 1) * LANES]

    copy = pltpu.make_async_copy(chunks, chunks_hbm, sem)
    copy.start()

    sub = iota((tile_w, layers), 0) % couples
    for out, k, x in ((far_out, 0, 1), (near_out, rows // 2 - 1, rows - 2)):
        packed = parts[k][0]
        for t in range(1, couples):
            packed = jnp.where(sub == t, parts[k][t], packed)
        out[cols:] = packed
        fine = jnp.stack(unpack_pairs(parts[k], 2), axis=1).reshape(cols, layers)
        out[:cols] = pres[x][frame.own] + fine
    for cross_kind, out in zip(pairings(nc), sides):
        right, _ = facing(cross, nc, cross_kind)
        edge = jnp.where(right, edges[1], edges[-1])
        out[: rows // 2] = edge
        for x in range(rows):
            second = jnp.where(right, pres[x][cols - 2 : cols - 1], pres[x][1:2])
            out[STRIP + x : STRIP + x + 1] = second + edge[x // 2 : x // 2 + 1]
    copy.wait()


def coarse_solve(totals, outflow, link_down, link_up, link_cross):
    nc = len(totals)

    def operate(v):
        out = []
        for c in range(nc):
            image = outflow[c] * v[c] - link_down[c] * roll(v[c], -1, 0) - link_up[c] * roll(v[c], 1, 0)
            if c < nc - 1:
                image = image - link_cross[c] * v[c + 1]
            if c > 0:
                image = image - link_cross[c - 1] * v[c - 1]
            out.append(image)
        return out

    def dot(a, b):
        return jnp.sum(sum(x * y for x, y in zip(a, b)), axis=0, keepdims=True)

    answer = [jnp.zeros_like(t) for t in totals]
    resid = search = totals
    image = operate(resid)
    norm, bend = dot(resid, resid), dot(resid, image)
    alpha = norm / bend
    for step in range(COARSE_ITERS):
        answer = [a + alpha * s for a, s in zip(answer, search)]
        if step == COARSE_ITERS - 1:
            break
        scale = 1.0 / norm
        resid = [r - alpha * m for r, m in zip(resid, image)]
        moved = operate(resid)
        norm, bend = dot(resid, resid), dot(resid, moved)
        beta = norm * scale
        alpha = norm / (bend - beta * norm / alpha)
        search = [r + beta * s for r, s in zip(resid, search)]
        image = [m + beta * i for m, i in zip(moved, image)]
    return answer


KEPT = ("src", "gain", "wx", "wy", "wz")


def around(nd, nc, step, dy):
    row = jnp.clip(lax.axis_index("down") + step, 0, nd - 1)
    return row, jnp.clip(lax.axis_index("cross") + dy, 0, nc - 1)


def fine_row(packed, couples):
    sub = iota(packed.shape, 0) % couples
    parts = []
    for t in range(couples):
        tall = jnp.where(sub == t, packed, 0.0)
        for s in range(couples):
            if s != t:
                tall = tall + jnp.where(sub == s, roll(packed, s - t, 0), 0.0)
        parts += unpack_pairs(tall, 1)
    return jnp.concatenate(parts, axis=0)


def strip_mask(nc, layers):
    cross, half = lax.axis_index("cross"), STRIP // 2
    col = iota((STRIP, layers), 0)
    there = (col < jnp.where(cross < nc - 1, half, 0)) | (col >= jnp.where(cross > 0, half, STRIP))
    return there, col < half


def sides_of(nd):
    down = lax.axis_index("down")
    step = jnp.where(down % 2 == 0, -1, 1)
    return step, beside(down, nd, step), beside(down, nd, -step)


def base_kernel(nd, nc, tiles, near, far, fix, pres_early, pres_late, *refs):
    n_side = len(pairings(nc))
    sides = refs[:n_side]
    early = dict(zip(KEPT, refs[n_side:]))
    late = dict(zip(KEPT, refs[n_side + len(KEPT) :]))
    out, pres_ref, third_ref = refs[n_side + 2 * len(KEPT) :]
    packs, couples, tile_w, layers = fix.shape
    rows, cols = 4 * packs, tiles * tile_w
    src, gain, wx, wy, wz = (joined(rows, n, early[n], late[n]) for n in KEPT)
    start = joined(rows, "pres", pres_early, pres_late)
    own, halo = slice(0, cols), slice(cols, cols + STRIP)
    frame = Frame(nd, nc, cols, layers)
    pres = Rows((pres_ref, -2, rows + 4))
    third = Rows((third_ref, -1, rows + 2))
    halo_col = iota((STRIP, layers), 0)
    for k in range(packs):
        for j, part in enumerate(unpack_pairs(fix[k], 1)):
            both = unpack_pairs(part, 2)
            fine = jnp.stack(both, axis=1).reshape(cols, layers)
            row = k + j * packs
            edge = jnp.zeros((STRIP, layers), FLOAT)
            for place, side in zip(frame.sides, sides):
                edge = jnp.where(place, side[row : row + 1], edge)
            for x in (2 * row, 2 * row + 1):
                pres_ref[x + 2, own, :] = start[x][own] + fine
                strip = start[x][halo] + edge
                for place, right, side in zip(frame.sides, frame.rights, sides):
                    second = place & (halo_col == jnp.where(right, 1, STRIP - 2))
                    strip = jnp.where(second, side[STRIP + x : STRIP + x + 1], strip)
                pres_ref[x + 2, halo, :] = strip
    _, odd_there, even_there = sides_of(nd)
    for message, there, xs in ((near, even_there, (rows, rows + 1)), (far, odd_there, (-1, -2))):
        rim = jnp.where(there, fine_row(message[cols:], couples), 0.0)
        pres_ref[xs[0] + 2, own, :] = start[xs[0]][own] + rim
        pres_ref[xs[0] + 2, halo, :] = start[xs[0]][halo]
        pres_ref[xs[1] + 2, own, :] = jnp.where(there, message[:cols], 0.0)
        pres_ref[xs[1] + 2, halo, :] = jnp.zeros((STRIP, layers), FLOAT)
    for x in range(-1, rows + 1):
        third[x] = smooth(pres, gain, src, wx, wy, wz, x)
    for x in range(rows):
        out[x] = smooth(third, gain, src, wx, wy, wz, x)[own]


def plain_sweep(field, gain, wx, wy, wz, x):
    total = 0.0
    if x in field:
        value = field[x]
        total = wy[x] * roll(value, -1, 0) + roll(wy[x] * value, 1, 0)
        total = total + wz[x] * roll(value, -1, 1) + roll(wz[x] * value, 1, 1)
    if x + 1 in field:
        total = total + wx[x] * field[x + 1]
    if x - 1 in field:
        total = total + wx[x - 1] * field[x - 1]
    total = gain[x] * total
    return KEEP * field[x] + total if x in field else total


def response_kernel(nd, nc, rows, *refs):
    early = dict(zip(KEPT, refs))
    late = dict(zip(KEPT, refs[len(KEPT) :]))
    every, by_odd, by_even, by_side, by_corner = refs[2 * len(KEPT) :]
    _, gain, wx, wy, wz = (joined(rows, n, early[n], late[n]) for n in KEPT)
    cols, layers = every.shape[1:]
    _, odd_there, even_there = sides_of(nd)
    there, _ = strip_mask(nc, layers)
    strip = jnp.where(there, 1.0, 0.0)
    blank = jnp.zeros((cols, layers), FLOAT)
    ones = jnp.ones((cols, layers), FLOAT)
    row_all = jnp.concatenate([ones, strip])
    row_own = jnp.concatenate([ones, jnp.zeros((STRIP, layers), FLOAT)])
    row_strip = jnp.concatenate([blank, strip])

    def sweeps(field, first, second):
        once = {x: plain_sweep(field, gain, wx, wy, wz, x) for x in first}
        return [plain_sweep(once, gain, wx, wy, wz, x)[:cols] for x in second]

    def ends(value):
        return value[:STRIP], value[cols - STRIP :]

    def put(ref, x, value):
        ref[x, :STRIP, :], ref[x, STRIP:, :] = ends(value)

    odd_row, even_row = (jnp.where(t, row_own, 0.0) for t in (odd_there, even_there))
    field = {x: row_all for x in range(rows)}
    field |= {-2: odd_row, rows + 1: even_row}
    field |= {-1: jnp.where(odd_there, row_all, 0.0), rows: jnp.where(even_there, row_all, 0.0)}
    for x, value in enumerate(sweeps(field, range(-1, rows + 1), range(rows))):
        every[x] = value
    for x, value in enumerate(sweeps({-2: odd_row, -1: odd_row}, (-1, 0), (0, 1))):
        by_odd[x] = value
    field = {rows: even_row, rows + 1: even_row}
    for x, value in enumerate(sweeps(field, (rows - 1, rows), (rows - 2, rows - 1))):
        by_even[x] = value
    field = {x: row_strip for x in range(rows)}
    for x, value in enumerate(sweeps(field, range(-1, rows + 1), range(rows))):
        put(by_side, x, value)
    for i, (at, x, t) in enumerate(((-1, 0, odd_there), (rows, rows - 1, even_there))):
        field = {at: jnp.where(t, row_strip, 0.0)}
        put(by_corner, i, sweeps(field, (at, x), (x,))[0])


def last_kernel(nd, nc, got, base, every, by_odd, by_even, by_side, by_corner, *refs):
    out, new, bricks, sems = refs
    rows, cols, layers = out.shape
    down, cross = lax.axis_index("down"), lax.axis_index("cross")
    even = down % 2 == 0

    tables = [got[pl.ds(c * nd * CHUNK, nd, stride=CHUNK), :] for c in range(nc)]

    def spread_lane(table, at):
        return jnp.broadcast_to(table[:, 2 * at + 1 : 2 * at + 2], (nd, LANES))

    last = iota((nd, LANES), 0) == nd - 1
    totals = [spread_lane(t, 0) for t in tables]
    link_down = [jnp.where(last, 0.0, spread_lane(t, 1)) for t in tables]
    link_up = [roll(link, 1, 0) for link in link_down]
    link_cross = [spread_lane(t, 2) for t in tables]
    outflow = [spread_lane(t, 3) for t in tables]
    answer = coarse_solve(totals, outflow, link_down, link_up, link_cross)
    for c in range(nc):
        bricks[c] = answer[c]

    def brick(step, dy):
        row, col = around(nd, nc, step, dy)
        return jnp.concatenate([bricks[col, pl.ds(row, 1), :]] * (layers // LANES), axis=1)

    def corner(step, dy):
        row, col = around(nd, nc, step, dy)
        at = (col * nd + row) * CHUNK
        both = jnp.concatenate([got[pl.ds(at + i, 1), :] for i in range(CHUNK)], axis=1)
        return unpack_pairs(both, 1)[0] + brick(step, dy) - mine

    odd_step, _, _ = sides_of(nd)
    mine = brick(0, 0)
    more_odd, more_even = brick(odd_step, 0) - mine, brick(-odd_step, 0) - mine
    more_side = brick(0, -1) - mine, brick(0, 1) - mine
    more_corner = [[corner(step, dy) for dy in (-1, 1)] for step in (odd_step, -odd_step)]
    halves = slice(0, STRIP), slice(STRIP, 2 * STRIP)
    ends = slice(0, STRIP), slice(cols - STRIP, cols)
    copies = []
    for x in reversed(range(rows)):
        at = counted(x, rows)
        value = base[x] + mine * every[x]
        if x < 2:
            value = value + more_odd * by_odd[x]
        if x >= rows - 2:
            value = value + more_even * by_even[x - (rows - 2)]
        new[at] = value
        for end, half, side, odd_corner, even_corner in zip(ends, halves, more_side, *more_corner):
            part = value[end] + side * by_side[x, half, :]
            if x == 0:
                part = part + odd_corner * by_corner[0, half, :]
            if x == rows - 1:
                part = part + even_corner * by_corner[1, half, :]
            new[at, end, :] = part
        if x % 2 == 0:
            span = pl.ds(jnp.where(even, x, rows - 2 - x), 2)
            copies.append(pltpu.make_async_copy(new.at[span], out.at[span], sems.at[len(copies)]))
            copies[-1].start()
    for copy in copies:
        copy.wait()


def whole(*shape):
    return jax.ShapeDtypeStruct(shape, FLOAT)


def call(kernel, out_shape, spaces, scratch=(), vmem_bytes=VMEM_BYTES, out_spaces=None):
    return pl.pallas_call(
        kernel,
        out_shape=out_shape,
        in_specs=[pl.BlockSpec(memory_space=s) for s in spaces],
        out_specs=jax.tree.map(
            lambda _, s: pl.BlockSpec(memory_space=s),
            out_shape,
            out_spaces or jax.tree.map(lambda _: pltpu.VMEM, out_shape),
        ),
        scratch_shapes=list(scratch),
        compiler_params=pltpu.CompilerParams(vmem_limit_bytes=vmem_bytes),
    )


def body(nd, nc, right_side, kappa, band_mask, tile_route):
    rows, cols, layers = right_side.shape
    tiles = tile_route.shape[1]
    axes = ("down", "cross")
    wide = cols + STRIP
    block = whole(rows, cols, layers)
    vmem = pltpu.VMEM
    early, late = spans(rows)

    shapes, perms = [], []
    for kind in pairings(nd):
        shapes.append(whole(2 * DEPTH - 1, cols, layers))
        perms.append(pairs_of(nd, nc, kind, None))
        if kind:
            for cross_kind in pairings(nc):
                shapes.append(whole(CORNER, STRIP, layers))
                perms.append(pairs_of(nd, nc, kind, cross_kind))
    strips = [whole(strip_tiles(rows), STRIP, layers) for _ in pairings(nc)]
    packs, couples, tile_w = rows // 4, tiles // 2, cols // tiles
    tile_shape = (couples, tile_w, layers)
    conduct, *messages = call(
        functools.partial(pack_kernel, nd, nc),
        [block] + shapes + strips,
        [pltpu.HBM] * 3,
        scratch=[
            pltpu.VMEM((rows, cols, layers), FLOAT),
            pltpu.VMEM((rows, cols, layers), FLOAT),
            pltpu.VMEM((rows, cols, layers), band_mask.dtype),
            pltpu.SemaphoreType.DMA((3,)),
        ],
        vmem_bytes=54400 * 1024,
    )(right_side, kappa, band_mask)

    received = [lax.ppermute(m, axes, p) for m, p in zip(messages, perms)]
    even, odd = received[0], received[1:]
    if strips:
        strips = call(
            functools.partial(strip_kernel, nd, nc),
            [whole(strip_tiles(rows) + CORNER, STRIP, layers) for _ in strips],
            [vmem] * (1 + len(strips)),
        )(even, *messages[len(perms) :])
        strips = [
            lax.ppermute(m, axes, pairs_of(nd, nc, None, cross_kind))
            for m, cross_kind in zip(strips, pairings(nc))
        ]
    if not odd:
        odd = [jnp.zeros((2 * DEPTH - 1, cols, layers), FLOAT)]

    first_part = call(
        functools.partial(early_kernel, nd, nc, tiles),
        [whole(*span_shape(early[n], wide, layers)) for n in EARLY]
        + [
            whole(rows // 2 - 2, *tile_shape),
            whole(cols, layers),
            whole(4, wide, layers),
            whole(5, LANES),
        ],
        [vmem] * (3 + len(strips)),
    )(right_side, conduct, even, *strips)
    first_part += call(
        functools.partial(tile_kernel, tiles),
        [whole(4 * packs + 1, *tile_shape), whole(*tile_shape)],
        [vmem] * 2,
    )(conduct, tile_route)
    late_arrays = call(
        functools.partial(late_kernel, nd, nc, tiles, rows),
        [whole(STRIP + rows, layers) for _ in pairings(nc)]
        + [whole(*span_shape(late[n], wide, layers)) for n in LATE_KEPT]
        + [
            whole(packs, *tile_shape),
            whole(cols + tile_w, layers),
            whole(cols + tile_w, layers),
            whole(nd * nc * CHUNK, LANES),
        ],
        [vmem] * (len(odd) + len(first_part)),
        scratch=[pltpu.VMEM(span_shape(late[n], wide, layers), FLOAT) for n in LATE_SCRATCH]
        + [pltpu.VMEM((nd * nc * CHUNK, LANES), FLOAT), pltpu.SemaphoreType.DMA],
        out_spaces=[vmem] * (len(pairings(nc)) + len(LATE_KEPT) + 3) + [pltpu.HBM],
    )(*odd, *first_part)
    n_side = len(pairings(nc))
    sides, late_arrays = late_arrays[:n_side], late_arrays[n_side:]
    *late_arrays, fix, near, far, chunks = late_arrays
    early_arrays = dict(zip(EARLY, first_part))
    late_arrays = dict(zip(LATE_KEPT, late_arrays))
    kept = [d[n] for d in (early_arrays, late_arrays) for n in KEPT]

    chunks = chunks.reshape(nd * nc, CHUNK, 1, LANES)
    arrived = lax.all_to_all(chunks, ("cross", "down"), 0, 0, tiled=True).reshape(nd * nc * CHUNK, LANES)
    far = lax.ppermute(far, axes, pairs_of(nd, nc, True, None))
    near = lax.ppermute(near, axes, pairs_of(nd, nc, False, None))
    sides = [
        lax.ppermute(m, axes, pairs_of(nd, nc, None, cross_kind))
        for m, cross_kind in zip(sides, pairings(nc))
    ]
    base = call(
        functools.partial(base_kernel, nd, nc, tiles),
        block,
        [vmem] * (5 + n_side + len(kept)),
        scratch=[
            pltpu.VMEM((rows + 4, wide, layers), FLOAT),
            pltpu.VMEM((rows + 2, wide, layers), FLOAT),
        ],
    )(near, far, fix, early_arrays["pres"], late_arrays["pres"], *sides, *kept)
    responses = call(
        functools.partial(response_kernel, nd, nc, rows),
        [
            block,
            whole(2, cols, layers),
            whole(2, cols, layers),
            whole(rows, 2 * STRIP, layers),
            whole(2, 2 * STRIP, layers),
        ],
        [vmem] * len(kept),
    )(*kept)
    return call(
        functools.partial(last_kernel, nd, nc),
        block,
        [vmem] * (2 + len(responses)),
        scratch=[
            pltpu.VMEM((rows, cols, layers), FLOAT),
            pltpu.VMEM((nc, nd, LANES), FLOAT),
            pltpu.SemaphoreType.DMA((rows // 2,)),
        ],
        out_spaces=pltpu.HBM,
    )(arrived, base, *responses)


def solution(mesh):
    return jax.shard_map(
        functools.partial(body, mesh.shape["down"], mesh.shape["cross"]),
        mesh=mesh,
        in_specs=(
            P("down", "cross", None),
            P("down", "cross", None),
            P("down", "cross", None),
            P("down", "cross"),
        ),
        out_specs=P("down", "cross", None),
        check_vma=False,
    )
```

```python
import functools

import jax
import jax.numpy as jnp
from jax import lax
from jax.experimental import pallas as pl
from jax.experimental.pallas import tpu as pltpu
from jax.sharding import PartitionSpec as P

BLOCK_SWEEPS = 4
COARSE_ITERS = 12
OMEGA = 0.8
KEEP = 1.0 - OMEGA
SNOW_FACTOR = 3.0

DEPTH = 3
CORNER = 2
STRIP = 8
LANES = 128
CHUNK = 2
FLOAT = jnp.float32
VMEM_BYTES = 24 * 1024 * 1024


def partners(count, odd):
    found = []
    for i in range(count):
        j = ((i + 1) ^ 1) - 1 if odd else i ^ 1
        found.append(j if 0 <= j < count else i)
    return found


def pairings(count):
    return [k for k in (False, True) if any(j != i for i, j in enumerate(partners(count, k)))]


def pairs_of(count_down, count_cross, down_kind, cross_kind):
    rows = list(range(count_down)) if down_kind is None else partners(count_down, down_kind)
    cols = list(range(count_cross)) if cross_kind is None else partners(count_cross, cross_kind)
    return [
        (i * count_cross + j, rows[i] * count_cross + cols[j])
        for i in range(count_down)
        for j in range(count_cross)
    ]


def facing(index, count, kind):
    ahead = (index % 2 == 0) != kind
    return ahead, jnp.where(ahead, index < count - 1, index > 0)


def beside(index, count, step):
    return (index + step >= 0) & (index + step < count)


def roll(x, amount, axis):
    return pltpu.roll(x, amount % x.shape[axis], axis)


def iota(shape, axis):
    return lax.broadcasted_iota(jnp.int32, shape, axis)


def gather(value, low, high, wx_low, wx_high, wy, wz):
    total = wx_high * high
    if low is not None:
        total = total + wx_low * low
    total = total + wy * roll(value, -1, 0) + roll(wy * value, 1, 0)
    return total + wz * roll(value, -1, 1) + roll(wz * value, 1, 1)


class Rows:
    def __init__(self, *parts):
        self.parts = parts

    def place(self, x):
        for ref, first, count in self.parts:
            if first <= x < first + count:
                return ref, x - first
        raise IndexError(x)

    def __getitem__(self, x):
        ref, i = self.place(x)
        return ref[i]

    def __setitem__(self, x, value):
        ref, i = self.place(x)
        ref[i] = value


def smooth(field, gain, src, wx, wy, wz, x):
    spread = gather(field[x], field[x - 1], field[x + 1], wx[x - 1], wx[x], wy[x], wz[x])
    return KEEP * field[x] + gain[x] * (src[x] + spread)


def counted(x, rows):
    return jnp.where(lax.axis_index("down") % 2 == 0, x, rows - 1 - x)


def edge_strip(right, cols):
    return pl.ds(pl.multiple_of(jnp.where(right, cols - STRIP, 0), STRIP), STRIP)


def upper_half(tile, right):
    return jnp.where(right, roll(tile, STRIP // 2, 0), tile)


def lower_half(tile, right):
    return jnp.where(right, tile, roll(tile, STRIP // 2, 0))


def pack_rows(tiles, right):
    upper = iota(tiles[0].shape, 0) < STRIP // 2
    return [
        jnp.where(upper, upper_half(a, right), lower_half(b, right)) for a, b in zip(tiles[::2], tiles[1::2])
    ]


def pack_source(tiles, right):
    *packed, last = pack_rows(tiles, right)
    col = iota(last.shape, 0) % (STRIP // 2)
    free = col == jnp.where(right, 0, 3)
    for m in range(3):
        packed[m] = jnp.where(free, jnp.where(right, roll(last, -1 - m, 0), roll(last, 3 - m, 0)), packed[m])
    return packed


def pack_corner(tiles, right):
    near, far = pack_rows(tiles[:4], right)
    last = upper_half(tiles[4], right)
    free = iota(last.shape, 0) == jnp.where(right, 0, 3)
    return [near, jnp.where(free, jnp.where(right, roll(last, -3, 0), roll(last, 3, 0)), far)]


def unpack_row(message, start, i, right):
    tile = message[start + i // 2]
    return jnp.where(right == (i % 2 == 0), tile, roll(tile, STRIP // 2, 0))


def unpack_source(message, start, rows, i, right):
    if i < rows - 2:
        return unpack_row(message, start, i, right)
    tiles = [message[start + m] for m in range(3)]
    col = iota(tiles[0].shape, 0) % (STRIP // 2)
    last = jnp.zeros(tiles[0].shape, FLOAT)
    for m, tile in enumerate(tiles):
        from_right = jnp.where(col == m, roll(tile, m - 3, 0), last)
        last = jnp.where(right, from_right, jnp.where(col == m + 1, roll(tile, m + 1, 0), last))
    return jnp.where(right == (i % 2 == 0), last, roll(last, STRIP // 2, 0))


def unpack_corner(message, start, i, right):
    if i < 2 or i == 3:
        return unpack_row(message, start, i, right)
    tile = message[start + 1]
    col = iota(tile.shape, 0)
    if i == 2:
        tile = jnp.where(col == jnp.where(right, 3, 0), 0.0, tile)
    else:
        place = col == jnp.where(right, 0, 3)
        tile = jnp.where(place, jnp.where(right, roll(tile, -3, 0), roll(tile, 3, 0)), 0.0)
    return jnp.where(right, tile, roll(tile, STRIP // 2, 0))


def put_tiles(out, start, tiles):
    for i, tile in enumerate(tiles):
        out[start + i] = tile


def pack_kernel(nd, nc, rhs_hbm, kappa_hbm, mask_hbm, conduct, *refs):
    *messages, rhs, kappa, mask, sems = refs
    rows, cols, _ = rhs.shape
    messages = iter(messages)
    cross = lax.axis_index("cross")
    copies = [
        pltpu.make_async_copy(src, dst, sems.at[i])
        for i, (src, dst) in enumerate(((kappa_hbm, kappa), (mask_hbm, mask), (rhs_hbm, rhs)))
    ]
    for copy in copies:
        copy.start()
    copies[0].wait()
    copies[1].wait()
    for x in range(rows):
        at = counted(x, rows)
        conduct[x] = kappa[at] / (1.0 + SNOW_FACTOR * mask[at].astype(FLOAT))
    copies[2].wait()
    for kind in pairings(nd):
        near = [i if kind else rows - 1 - i for i in range(DEPTH)]
        out = next(messages)
        for i, x in enumerate(near):
            out[i] = conduct[x]
        for i, x in enumerate(near[:-1]):
            out[DEPTH + i] = rhs[counted(x, rows)]
        if kind:
            for cross_kind in pairings(nc):
                right, _ = facing(cross, nc, cross_kind)
                strip = edge_strip(right, cols)
                tiles = [conduct[x, strip, :] for x in near]
                tiles += [rhs[counted(x, rows), strip, :] for x in near[:-1]]
                put_tiles(next(messages), 0, pack_corner(tiles, right))
    for cross_kind in pairings(nc):
        right, _ = facing(cross, nc, cross_kind)
        strip = edge_strip(right, cols)
        tiles = pack_rows([conduct[x, strip, :] for x in range(rows)], right)
        tiles += pack_source([rhs[counted(x, rows), strip, :] for x in range(rows)], right)
        put_tiles(next(messages), 0, tiles)


def strip_kernel(nd, nc, even, *refs):
    cols = even.shape[1]
    count = len(pairings(nc))
    for cross_kind, own, out in zip(pairings(nc), refs[:count], refs[count:]):
        right, _ = facing(lax.axis_index("cross"), nc, cross_kind)
        strip = edge_strip(right, cols)
        count = own.shape[0]
        out[:count] = own[...]
        put_tiles(out, count, pack_corner([even[i, strip, :] for i in range(2 * DEPTH - 1)], right))


def fold(x):
    x = sum(x[:, i : i + LANES] for i in range(0, x.shape[1], LANES))
    return jnp.sum(x, axis=0, keepdims=True)


def swap_pairs(x, axis):
    return jnp.where(iota(x.shape, axis) % 2 == 0, roll(x, -1, axis), roll(x, 1, axis))


def pack_pairs(a, b, axis):
    even = iota(a.shape, axis) % 2 == 0
    return jnp.where(even, a, b) + swap_pairs(jnp.where(even, b, a), axis)


def unpack_pairs(x, axis):
    even = iota(x.shape, axis) % 2 == 0
    return jnp.where(even, x, roll(x, 1, axis)), jnp.where(even, roll(x, -1, axis), x)


class Frame:
    def __init__(self, nd, nc, cols, layers):
        self.cols, self.layers, self.wide = cols, layers, cols + STRIP
        self.own, self.halo = slice(0, cols), slice(cols, cols + STRIP)
        cross = lax.axis_index("cross")
        half = STRIP // 2
        self.lane = iota((self.wide, layers), 1)
        self.last_lane = self.lane == layers - 1
        col = iota((self.wide, layers), 0)
        self.col_ok = (col < jnp.where(cross < nc - 1, cols + half, cols)) | (
            col >= jnp.where(cross > 0, cols + half, self.wide)
        )
        halo_col = iota((STRIP, layers), 0)
        self.sides, self.rights = [], []
        for cross_kind in pairings(nc):
            right, valid = facing(cross, nc, cross_kind)
            start = jnp.where(right, 0, half)
            stop = jnp.where(valid, start + half, 0)
            self.sides.append((halo_col >= start) & (halo_col < stop))
            self.rights.append(right)

    def merged(self, messages, unpack, *place):
        total = jnp.zeros((STRIP, self.layers), FLOAT)
        for side, right, message in zip(self.sides, self.rights, messages):
            total = jnp.where(side, unpack(message, *place, right), total)
        return total

    def row(self, own, halo):
        return jnp.concatenate([own, halo], axis=0)

    def doubled(self, low, here, high):
        above = jnp.where(self.last_lane, 0.0, roll(here, -1, 1))
        below = jnp.where(self.lane == 0, 0.0, roll(here, 1, 1))
        right = roll(here, -1, 0)
        ends = high if low is None else low + high
        return 6.0 * here + ends + (right + roll(here, 1, 0)) + (above + below), right, above

    def gain_of(self, doubled, valid=None):
        ok = self.col_ok & (doubled > 0.0)
        if valid is not None:
            ok = ok & valid
        return jnp.where(ok, (2.0 * OMEGA) / doubled, 0.0)

    def weights(self, q, gain, src, first, diag, wx, wy, wz, x, valid=None):
        here = q[x]
        doubled, right, above = self.doubled(q[x - 1], here, q[x + 1])
        gain_here = self.gain_of(doubled, valid)
        gain[x] = gain_here
        first[x] = gain_here * src[x]
        if diag is not None:
            diag[x] = 0.5 * doubled
        if wx is not None:
            wx[x] = 0.5 * (here + q[x + 1])
        if wy is not None:
            self.plane_weights(wy, wz, x, here, right, above)

    def plane_weights(self, wy, wz, x, here, right, above):
        wy[x] = 0.5 * (here + right)
        wz[x] = jnp.where(self.last_lane, 0.0, 0.5 * (here + above))


def residual(frame, src, diag, pres, wx, wy, wz, x):
    spread = gather(pres[x], pres[x - 1], pres[x + 1], wx[x - 1], wx[x], wy[x], wz[x])
    return (src[x] - diag[x] * pres[x] + spread)[frame.own]


def spans(rows):
    early = dict(
        q=(0, rows + DEPTH), src=(0, rows + DEPTH - 1), gain=(1, rows + DEPTH - 1),
        first=(1, rows + DEPTH - 1), diag=(1, rows), wx=(0, rows + 1), wy=(0, rows + 1),
        wz=(0, rows + 1), pres=(2, rows + 1),
    )
    late = dict(
        q=(-DEPTH, 0), src=(1 - DEPTH, 0), gain=(1 - DEPTH, 1), first=(1 - DEPTH, 1), diag=(0, 1),
        wx=(1 - DEPTH, 0), wy=(-1, 0), wz=(-1, 0), pres=(-1, 2),
    )
    return early, late


EARLY = ("q", "src", "gain", "first", "diag", "wx", "wy", "wz", "pres")
LATE_KEPT = ("src", "gain", "wx", "wy", "wz", "pres")
LATE_SCRATCH = ("q", "first", "diag")


def span_shape(span, wide, layers):
    return (span[1] - span[0], wide, layers)


def joined(rows, name, early_ref, late_ref):
    early, late = (d[name] for d in spans(rows))
    return Rows((early_ref, early[0], early[1] - early[0]), (late_ref, late[0], late[1] - late[0]))


def coarse_rows(pair, couples, tile_w):
    t = pair.reshape(couples, 2, tile_w, pair.shape[1])
    return pack_pairs(t[:, 0], t[:, 1], 2)


def tile_kernel(tiles, conduct, route, coef, touched):
    rows, cols, layers = conduct.shape
    tile_w = cols // tiles
    couples = tiles // 2
    even_lane = iota((tile_w, layers), 1) % 2 == 0
    for t in range(couples):
        numbers = [jnp.broadcast_to(route[0:1, i : i + 1], (tile_w, layers)) for i in (2 * t, 2 * t + 1)]
        touched[t] = jnp.where(jnp.where(even_lane, *numbers) >= 0, 1.0, 0.0)

    packs = rows // 4
    by_row = [
        coarse_rows(0.125 * (conduct[2 * k] + conduct[2 * k + 1]), couples, tile_w)
        for k in range(rows // 2)
    ]
    con = [pack_pairs(by_row[k], by_row[k + packs], 1) for k in range(packs)]
    shape = (couples, tile_w, layers)
    tile_col, tile_lane = iota(shape, 1), iota(shape, 2)
    even_col = tile_col % 2 == 0
    y_end, y_start = tile_col >= tile_w - 2, tile_col < 2
    z_end, z_start = tile_lane >= layers - 2, tile_lane < 2
    for k in range(packs - 1):
        coef[3 * packs + 2 + k] = 2.0 * (con[k] + con[k + 1])
    middle = 2.0 * (con[packs - 1] + roll(con[0], -1, 1))
    coef[3 * packs] = jnp.where(even_col, middle, 0.0)
    coef[3 * packs + 1] = jnp.where(even_col, 0.0, roll(middle, 1, 1))
    for k in range(packs):
        c = con[k]
        y_high = jnp.where(y_end, 0.0, roll(c, -2, 1))
        z_high = jnp.where(z_end, 0.0, roll(c, -2, 2))
        y_low = jnp.where(y_start, 0.0, roll(c, 2, 1))
        z_low = jnp.where(z_start, 0.0, roll(c, 2, 2))
        total = 6.0 * c + (y_high + y_low) + (z_high + z_low)
        if k > 0:
            total = total + con[k - 1]
        else:
            total = total + jnp.where(even_col, 0.0, roll(con[packs - 1], 1, 1))
        if k < packs - 1:
            total = total + con[k + 1]
        else:
            total = total + jnp.where(even_col, roll(con[0], -1, 1), 0.0)
        total = 2.0 * total
        coef[k] = OMEGA / jnp.where(total > 0.0, total, 1.0)
        coef[packs + k] = jnp.where(y_end, 0.0, 2.0 * (c + y_high))
        coef[2 * packs + k] = jnp.where(z_end, 0.0, 2.0 * (c + z_high))


def early_kernel(nd, nc, tiles, rhs, conduct, even, *refs):
    rows, cols, layers = conduct.shape
    tile_w = cols // tiles
    couples = tiles // 2
    n_cross = len(pairings(nc))
    strips = refs[:n_cross]
    *arrays, res_coarse, res_row, part, sums = refs[n_cross:]
    early, _ = spans(rows)
    at = {n: Rows((r, early[n][0], r.shape[0])) for n, r in zip(EARLY, arrays)}
    q, src, gain, first, diag, wx, wy, wz, pres = (at[n] for n in EARLY)
    frame = Frame(nd, nc, cols, layers)
    own, halo = frame.own, frame.halo

    for x in range(rows):
        q[x] = frame.row(conduct[x], frame.merged(strips, unpack_row, 0, x))
        edge = frame.merged(strips, unpack_source, rows // 2, rows, x)
        src[x] = frame.row(rhs[counted(x, rows)], edge)
    _, valid = facing(lax.axis_index("down"), nd, False)
    for i in range(DEPTH):
        corner = frame.merged(strips, unpack_corner, rows - 1, i)
        q[rows + i] = jnp.where(valid, frame.row(even[i], corner), 0.0)
    for i in range(DEPTH - 1):
        corner = frame.merged(strips, unpack_corner, rows - 1, DEPTH + i)
        src[rows + i] = jnp.where(valid, frame.row(even[DEPTH + i], corner), 0.0)

    here = q[0]
    above = jnp.where(frame.last_lane, 0.0, roll(here, -1, 1))
    frame.plane_weights(wy, wz, 0, here, roll(here, -1, 0), above)
    wx[0] = 0.5 * (here + q[1])
    part[0] = frame.doubled(None, here, q[1])[0]
    for x in range(*early["gain"]):
        frame.weights(
            q, gain, src, first,
            diag if x < rows else None,
            wx if x < early["wx"][1] else None,
            wy if x < early["wy"][1] else None,
            wz, x, valid if x >= rows else None,
        )
    for x in range(*early["pres"]):
        pres[x] = smooth(first, gain, src, wx, wy, wz, x)

    spread = gather(first[1], None, first[2], None, wx[1], wy[1], wz[1])
    part[1] = KEEP * first[1] + gain[1] * (src[1] + spread)
    part[2] = gain[1] * wx[0]
    spread = gather(pres[2], None, pres[3], None, wx[2], wy[2], wz[2])
    part[3] = src[2] - diag[2] * pres[2] + spread

    res = {x: residual(frame, src, diag, pres, wx, wy, wz, x) for x in range(3, rows)}
    res_row[...] = res[3]
    for k in range(2, rows // 2):
        res_coarse[k - 2] = coarse_rows(res[2 * k] + res[2 * k + 1], couples, tile_w)

    strip_col = iota((STRIP, layers), 0)
    plane = sum(q[x][own] for x in range(rows))
    beyond = sum(q[x][halo] for x in range(rows))
    own_lane = iota((cols, layers), 1)
    low, high = strip_col < 2, strip_col >= STRIP - 2
    sums[0:1] = fold(sum(res.values()))
    sums[1:2] = fold(sum(q[x][own] for x in range(rows - 2, rows + 2)))
    sums[2:3] = fold(jnp.where(high, plane[cols - STRIP :], 0.0) + jnp.where(low, beyond, 0.0))
    sums[3:4] = fold(jnp.where(low, plane[:STRIP], 0.0) + jnp.where(high, beyond, 0.0))
    sums[4:5] = fold(jnp.where((own_lane < 2) | (own_lane >= layers - 2), plane, 0.0))


def late_kernel(nd, nc, tiles, rows, odd, *refs):
    n_cross = len(pairings(nc)) if len(pairings(nd)) > 1 else 0
    corners = refs[:n_cross]
    n_in = n_cross + len(EARLY) + 6
    early_refs = dict(zip(EARLY, refs[n_cross:]))
    res_coarse, res_row, part, sums, coef, touched = refs[n_in - 6 : n_in]
    names = LATE_KEPT + ("fix", "near", "far", "chunks_hbm") + LATE_SCRATCH + ("chunks", "sem")
    n_side = len(pairings(nc))
    sides = refs[n_in : n_in + n_side]
    late_refs = dict(zip(names, refs[n_in + n_side :]))
    fix_out, near_out, far_out = (late_refs[n] for n in ("fix", "near", "far"))
    chunks_hbm, chunks, sem = (late_refs[n] for n in ("chunks_hbm", "chunks", "sem"))
    wide, layers = early_refs["q"].shape[1:]
    cols = wide - STRIP
    tile_w = cols // tiles
    couples = tiles // 2
    down = lax.axis_index("down")
    even = down % 2 == 0
    q, src, gain, first, diag, wx, wy, wz, pres = (
        joined(rows, n, early_refs[n], late_refs[n]) for n in EARLY
    )
    frame = Frame(nd, nc, cols, layers)
    _, late = spans(rows)

    valid = beside(down, nd, jnp.where(even, -1, 1))
    for i in range(DEPTH):
        corner = frame.merged(corners, unpack_corner, 0, i)
        q[-1 - i] = jnp.where(valid, frame.row(odd[i], corner), 0.0)
    for i in range(DEPTH - 1):
        corner = frame.merged(corners, unpack_corner, 0, DEPTH + i)
        src[-1 - i] = jnp.where(valid, frame.row(odd[DEPTH + i], corner), 0.0)
    for x in range(*late["wx"]):
        frame.weights(
            q, gain, src, first, None, wx, wy if x == -1 else None, wz, x, valid
        )
    doubled = part[0] + q[-1]
    gain[0] = frame.gain_of(doubled)
    first[0] = gain[0] * src[0]
    diag[0] = 0.5 * doubled
    for x in (-1, 0):
        pres[x] = smooth(first, gain, src, wx, wy, wz, x)
    pres[1] = part[1] + part[2] * first[0]
    res = [residual(frame, src, diag, pres, wx, wy, wz, x) for x in (0, 1)]
    res.append((part[3] + wx[1] * pres[1])[frame.own])
    res.append(res_row[...])

    res_total = sums[0:1] + fold(res[0] + res[1] + res[2])
    link_odd = fold(sum(q[x][frame.own] for x in range(-2, 2)))
    link_even, link_cross, link_back, ends = (sums[i : i + 1] for i in range(1, 5))
    outflow = link_even + link_odd + link_cross + link_back + ends
    link_down = jnp.where(even, link_even, link_odd)
    lines = jnp.concatenate([res_total, 0.25 * link_down, 0.25 * link_cross, 0.25 * outflow])
    lines = jnp.sum(lines, axis=1, keepdims=True)
    line = iota((1, layers), 1)
    summary = jnp.zeros((1, layers), FLOAT)
    for i in range(4):
        summary = jnp.where(line == 2 * i + 1, lines[i : i + 1], summary)

    packs = rows // 4
    by_row = [coarse_rows(res[2 * k] + res[2 * k + 1], couples, tile_w) for k in range(2)]
    by_row += [res_coarse[k] for k in range(rows // 2 - 2)]
    r = [pack_pairs(by_row[k], by_row[k + packs], 1) for k in range(packs)]
    middle_low, middle_high = coef[3 * packs], coef[3 * packs + 1]
    fix = [coef[k] * r[k] for k in range(packs)]
    for _ in range(BLOCK_SWEEPS - 1):
        updated = []
        for k in range(packs):
            value, link_y, link_z = fix[k], coef[packs + k], coef[2 * packs + k]
            acc = r[k] + link_y * roll(value, -2, 1) + roll(link_y * value, 2, 1)
            acc = acc + link_z * roll(value, -2, 2) + roll(link_z * value, 2, 2)
            if k > 0:
                acc = acc + coef[3 * packs + 1 + k] * fix[k - 1]
            else:
                acc = acc + middle_high * roll(fix[packs - 1], 1, 1)
            if k < packs - 1:
                acc = acc + coef[3 * packs + 2 + k] * fix[k + 1]
            else:
                acc = acc + middle_low * roll(fix[0], -1, 1)
            updated.append(KEEP * value + coef[k] * acc)
        fix = updated
    fix = [jnp.where(touched[...] > 0.0, f, 0.0) for f in fix]
    for k in range(packs):
        fix_out[k] = fix[k]

    parts = [unpack_pairs(fix[k % packs], 1)[k // packs] for k in range(rows // 2)]
    count = nd * nc
    for i in range(CHUNK):
        part = summary[:, i * LANES : (i + 1) * LANES]
        chunks[pl.ds(i, count, stride=CHUNK), :] = jnp.broadcast_to(part, (count, LANES))
    cross = lax.axis_index("cross")
    odd_step = jnp.where(even, -1, 1)
    edges = {}
    for dy in (-1, 1):
        at_couple, at_col = (0, 0) if dy < 0 else (couples - 1, tile_w - 1)
        edge = jnp.concatenate([p[at_couple][at_col : at_col + 1] for p in parts])
        edges[dy] = edge = unpack_pairs(edge, 1)[0 if dy < 0 else 1]
    for cross_kind in pairings(nc):
        right, side_there = facing(cross, nc, cross_kind)
        edge = jnp.where(right, edges[1], edges[-1])
        other = cross + jnp.where(right, 1, -1)
        for k, step in ((0, odd_step), (rows // 2 - 1, -odd_step)):
            there = side_there & beside(down, nd, step)
            both = jnp.where(line % 2 == 0, edge[k : k + 1], summary)
            at = jnp.where(there, other * nd + down + step, cross * nd + down) * CHUNK
            for i in range(CHUNK):
                chunks[pl.ds(at + i, 1), :] = both[:, i * LANES : (i + 1) * LANES]

    copy = pltpu.make_async_copy(chunks, chunks_hbm, sem)
    copy.start()

    sub = iota((tile_w, layers), 0) % couples
    for out, k, x in ((far_out, 0, 1), (near_out, rows // 2 - 1, rows - 2)):
        packed = parts[k][0]
        for t in range(1, couples):
            packed = jnp.where(sub == t, parts[k][t], packed)
        out[cols:] = packed
        fine = jnp.stack(unpack_pairs(parts[k], 2), axis=1).reshape(cols, layers)
        out[:cols] = pres[x][frame.own] + fine
    for cross_kind, out in zip(pairings(nc), sides):
        right, _ = facing(cross, nc, cross_kind)
        out[: rows // 2] = jnp.where(right, edges[1], edges[-1])
    copy.wait()


def coarse_solve(totals, outflow, link_down, link_up, link_cross):
    nc = len(totals)

    def operate(v):
        out = []
        for c in range(nc):
            image = outflow[c] * v[c] - link_down[c] * roll(v[c], -1, 0) - link_up[c] * roll(v[c], 1, 0)
            if c < nc - 1:
                image = image - link_cross[c] * v[c + 1]
            if c > 0:
                image = image - link_cross[c - 1] * v[c - 1]
            out.append(image)
        return out

    def dot(a, b):
        return jnp.sum(sum(x * y for x, y in zip(a, b)), axis=0, keepdims=True)

    answer = [jnp.zeros_like(t) for t in totals]
    resid = search = totals
    image = operate(resid)
    norm, bend = dot(resid, resid), dot(resid, image)
    alpha = norm / bend
    for step in range(COARSE_ITERS):
        answer = [a + alpha * s for a, s in zip(answer, search)]
        if step == COARSE_ITERS - 1:
            break
        scale = 1.0 / norm
        resid = [r - alpha * m for r, m in zip(resid, image)]
        moved = operate(resid)
        norm, bend = dot(resid, resid), dot(resid, moved)
        beta = norm * scale
        alpha = norm / (bend - beta * norm / alpha)
        search = [r + beta * s for r, s in zip(resid, search)]
        image = [m + beta * i for m, i in zip(moved, image)]
    return answer


KEPT = ("src", "gain", "wx", "wy", "wz")


def around(nd, nc, step, dy):
    row = jnp.clip(lax.axis_index("down") + step, 0, nd - 1)
    return row, jnp.clip(lax.axis_index("cross") + dy, 0, nc - 1)


def fine_row(packed, couples):
    sub = iota(packed.shape, 0) % couples
    parts = []
    for t in range(couples):
        tall = jnp.where(sub == t, packed, 0.0)
        for s in range(couples):
            if s != t:
                tall = tall + jnp.where(sub == s, roll(packed, s - t, 0), 0.0)
        parts += unpack_pairs(tall, 1)
    return jnp.concatenate(parts, axis=0)


def strip_mask(nc, layers):
    cross, half = lax.axis_index("cross"), STRIP // 2
    col = iota((STRIP, layers), 0)
    there = (col < jnp.where(cross < nc - 1, half, 0)) | (col >= jnp.where(cross > 0, half, STRIP))
    return there, col < half


def sides_of(nd):
    down = lax.axis_index("down")
    step = jnp.where(down % 2 == 0, -1, 1)
    return step, beside(down, nd, step), beside(down, nd, -step)


def base_kernel(nd, nc, tiles, near, far, fix, pres_early, pres_late, *refs):
    n_side = len(pairings(nc))
    sides = refs[:n_side]
    early = dict(zip(KEPT, refs[n_side:]))
    late = dict(zip(KEPT, refs[n_side + len(KEPT) :]))
    out, pres_ref, third_ref = refs[n_side + 2 * len(KEPT) :]
    packs, couples, tile_w, layers = fix.shape
    rows, cols = 4 * packs, tiles * tile_w
    src, gain, wx, wy, wz = (joined(rows, n, early[n], late[n]) for n in KEPT)
    start = joined(rows, "pres", pres_early, pres_late)
    own, halo = slice(0, cols), slice(cols, cols + STRIP)
    frame = Frame(nd, nc, cols, layers)
    pres = Rows((pres_ref, -2, rows + 4))
    third = Rows((third_ref, -1, rows + 2))
    for k in range(packs):
        for j, part in enumerate(unpack_pairs(fix[k], 1)):
            both = unpack_pairs(part, 2)
            fine = jnp.stack(both, axis=1).reshape(cols, layers)
            row = k + j * packs
            edge = jnp.zeros((STRIP, layers), FLOAT)
            for place, side in zip(frame.sides, sides):
                edge = jnp.where(place, side[row : row + 1], edge)
            for x in (2 * row, 2 * row + 1):
                pres_ref[x + 2, own, :] = start[x][own] + fine
                pres_ref[x + 2, halo, :] = start[x][halo] + edge
    _, odd_there, even_there = sides_of(nd)
    for message, there, xs in ((near, even_there, (rows, rows + 1)), (far, odd_there, (-1, -2))):
        rim = jnp.where(there, fine_row(message[cols:], couples), 0.0)
        pres_ref[xs[0] + 2, own, :] = start[xs[0]][own] + rim
        pres_ref[xs[0] + 2, halo, :] = start[xs[0]][halo]
        pres_ref[xs[1] + 2, own, :] = jnp.where(there, message[:cols], 0.0)
        pres_ref[xs[1] + 2, halo, :] = jnp.zeros((STRIP, layers), FLOAT)
    for x in range(-1, rows + 1):
        third[x] = smooth(pres, gain, src, wx, wy, wz, x)
    for x in range(rows):
        out[x] = smooth(third, gain, src, wx, wy, wz, x)[own]


def plain_sweep(field, gain, wx, wy, wz, x):
    total = 0.0
    if x in field:
        value = field[x]
        total = wy[x] * roll(value, -1, 0) + roll(wy[x] * value, 1, 0)
        total = total + wz[x] * roll(value, -1, 1) + roll(wz[x] * value, 1, 1)
    if x + 1 in field:
        total = total + wx[x] * field[x + 1]
    if x - 1 in field:
        total = total + wx[x - 1] * field[x - 1]
    total = gain[x] * total
    return KEEP * field[x] + total if x in field else total


def response_kernel(nd, nc, rows, *refs):
    early = dict(zip(KEPT, refs))
    late = dict(zip(KEPT, refs[len(KEPT) :]))
    every, by_odd, by_even, by_side, by_corner = refs[2 * len(KEPT) :]
    _, gain, wx, wy, wz = (joined(rows, n, early[n], late[n]) for n in KEPT)
    cols, layers = every.shape[1:]
    _, odd_there, even_there = sides_of(nd)
    there, _ = strip_mask(nc, layers)
    strip = jnp.where(there, 1.0, 0.0)
    blank = jnp.zeros((cols, layers), FLOAT)
    ones = jnp.ones((cols, layers), FLOAT)
    row_all = jnp.concatenate([ones, strip])
    row_own = jnp.concatenate([ones, jnp.zeros((STRIP, layers), FLOAT)])
    row_strip = jnp.concatenate([blank, strip])

    def sweeps(field, first, second):
        once = {x: plain_sweep(field, gain, wx, wy, wz, x) for x in first}
        return [plain_sweep(once, gain, wx, wy, wz, x)[:cols] for x in second]

    def ends(value):
        return value[:STRIP], value[cols - STRIP :]

    def put(ref, x, value):
        ref[x, :STRIP, :], ref[x, STRIP:, :] = ends(value)

    odd_row, even_row = (jnp.where(t, row_own, 0.0) for t in (odd_there, even_there))
    field = {x: row_all for x in range(rows)}
    field |= {-2: odd_row, rows + 1: even_row}
    field |= {-1: jnp.where(odd_there, row_all, 0.0), rows: jnp.where(even_there, row_all, 0.0)}
    for x, value in enumerate(sweeps(field, range(-1, rows + 1), range(rows))):
        every[x] = value
    for x, value in enumerate(sweeps({-2: odd_row, -1: odd_row}, (-1, 0), (0, 1))):
        by_odd[x] = value
    field = {rows: even_row, rows + 1: even_row}
    for x, value in enumerate(sweeps(field, (rows - 1, rows), (rows - 2, rows - 1))):
        by_even[x] = value
    field = {x: row_strip for x in range(rows)}
    for x, value in enumerate(sweeps(field, range(-1, rows + 1), range(rows))):
        put(by_side, x, value)
    for i, (at, x, t) in enumerate(((-1, 0, odd_there), (rows, rows - 1, even_there))):
        field = {at: jnp.where(t, row_strip, 0.0)}
        put(by_corner, i, sweeps(field, (at, x), (x,))[0])


def last_kernel(nd, nc, got, base, every, by_odd, by_even, by_side, by_corner, *refs):
    out, new, bricks, sems = refs
    rows, cols, layers = out.shape
    down, cross = lax.axis_index("down"), lax.axis_index("cross")
    even = down % 2 == 0

    tables = [got[pl.ds(c * nd * CHUNK, nd, stride=CHUNK), :] for c in range(nc)]

    def spread_lane(table, at):
        return jnp.broadcast_to(table[:, 2 * at + 1 : 2 * at + 2], (nd, LANES))

    last = iota((nd, LANES), 0) == nd - 1
    totals = [spread_lane(t, 0) for t in tables]
    link_down = [jnp.where(last, 0.0, spread_lane(t, 1)) for t in tables]
    link_up = [roll(link, 1, 0) for link in link_down]
    link_cross = [spread_lane(t, 2) for t in tables]
    outflow = [spread_lane(t, 3) for t in tables]
    answer = coarse_solve(totals, outflow, link_down, link_up, link_cross)
    for c in range(nc):
        bricks[c] = answer[c]

    def brick(step, dy):
        row, col = around(nd, nc, step, dy)
        return jnp.concatenate([bricks[col, pl.ds(row, 1), :]] * (layers // LANES), axis=1)

    def corner(step, dy):
        row, col = around(nd, nc, step, dy)
        at = (col * nd + row) * CHUNK
        both = jnp.concatenate([got[pl.ds(at + i, 1), :] for i in range(CHUNK)], axis=1)
        return unpack_pairs(both, 1)[0] + brick(step, dy) - mine

    odd_step, _, _ = sides_of(nd)
    mine = brick(0, 0)
    more_odd, more_even = brick(odd_step, 0) - mine, brick(-odd_step, 0) - mine
    more_side = brick(0, -1) - mine, brick(0, 1) - mine
    more_corner = [[corner(step, dy) for dy in (-1, 1)] for step in (odd_step, -odd_step)]
    halves = slice(0, STRIP), slice(STRIP, 2 * STRIP)
    ends = slice(0, STRIP), slice(cols - STRIP, cols)
    copies = []
    for x in reversed(range(rows)):
        at = counted(x, rows)
        value = base[x] + mine * every[x]
        if x < 2:
            value = value + more_odd * by_odd[x]
        if x >= rows - 2:
            value = value + more_even * by_even[x - (rows - 2)]
        new[at] = value
        for end, half, side, odd_corner, even_corner in zip(ends, halves, more_side, *more_corner):
            part = value[end] + side * by_side[x, half, :]
            if x == 0:
                part = part + odd_corner * by_corner[0, half, :]
            if x == rows - 1:
                part = part + even_corner * by_corner[1, half, :]
            new[at, end, :] = part
        if x % 2 == 0:
            span = pl.ds(jnp.where(even, x, rows - 2 - x), 2)
            copies.append(pltpu.make_async_copy(new.at[span], out.at[span], sems.at[len(copies)]))
            copies[-1].start()
    for copy in copies:
        copy.wait()


def whole(*shape):
    return jax.ShapeDtypeStruct(shape, FLOAT)


def call(kernel, out_shape, spaces, scratch=(), vmem_bytes=VMEM_BYTES, out_spaces=None):
    return pl.pallas_call(
        kernel,
        out_shape=out_shape,
        in_specs=[pl.BlockSpec(memory_space=s) for s in spaces],
        out_specs=jax.tree.map(
            lambda _, s: pl.BlockSpec(memory_space=s),
            out_shape,
            out_spaces or jax.tree.map(lambda _: pltpu.VMEM, out_shape),
        ),
        scratch_shapes=list(scratch),
        compiler_params=pltpu.CompilerParams(vmem_limit_bytes=vmem_bytes),
    )


def body(nd, nc, right_side, kappa, band_mask, tile_route):
    rows, cols, layers = right_side.shape
    tiles = tile_route.shape[1]
    axes = ("down", "cross")
    wide = cols + STRIP
    block = whole(rows, cols, layers)
    vmem = pltpu.VMEM
    early, late = spans(rows)

    shapes, perms = [], []
    for kind in pairings(nd):
        shapes.append(whole(2 * DEPTH - 1, cols, layers))
        perms.append(pairs_of(nd, nc, kind, None))
        if kind:
            for cross_kind in pairings(nc):
                shapes.append(whole(CORNER, STRIP, layers))
                perms.append(pairs_of(nd, nc, kind, cross_kind))
    strips = [whole(rows - 1, STRIP, layers) for _ in pairings(nc)]
    packs, couples, tile_w = rows // 4, tiles // 2, cols // tiles
    tile_shape = (couples, tile_w, layers)
    conduct, *messages = call(
        functools.partial(pack_kernel, nd, nc),
        [block] + shapes + strips,
        [pltpu.HBM] * 3,
        scratch=[
            pltpu.VMEM((rows, cols, layers), FLOAT),
            pltpu.VMEM((rows, cols, layers), FLOAT),
            pltpu.VMEM((rows, cols, layers), band_mask.dtype),
            pltpu.SemaphoreType.DMA((3,)),
        ],
        vmem_bytes=54400 * 1024,
    )(right_side, kappa, band_mask)

    received = [lax.ppermute(m, axes, p) for m, p in zip(messages, perms)]
    even, odd = received[0], received[1:]
    if strips:
        strips = call(
            functools.partial(strip_kernel, nd, nc),
            [whole(rows - 1 + CORNER, STRIP, layers) for _ in strips],
            [vmem] * (1 + len(strips)),
        )(even, *messages[len(perms) :])
        strips = [
            lax.ppermute(m, axes, pairs_of(nd, nc, None, cross_kind))
            for m, cross_kind in zip(strips, pairings(nc))
        ]
    if not odd:
        odd = [jnp.zeros((2 * DEPTH - 1, cols, layers), FLOAT)]

    first_part = call(
        functools.partial(early_kernel, nd, nc, tiles),
        [whole(*span_shape(early[n], wide, layers)) for n in EARLY]
        + [
            whole(rows // 2 - 2, *tile_shape),
            whole(cols, layers),
            whole(4, wide, layers),
            whole(5, LANES),
        ],
        [vmem] * (3 + len(strips)),
    )(right_side, conduct, even, *strips)
    first_part += call(
        functools.partial(tile_kernel, tiles),
        [whole(4 * packs + 1, *tile_shape), whole(*tile_shape)],
        [vmem] * 2,
    )(conduct, tile_route)
    late_arrays = call(
        functools.partial(late_kernel, nd, nc, tiles, rows),
        [whole(STRIP, layers) for _ in pairings(nc)]
        + [whole(*span_shape(late[n], wide, layers)) for n in LATE_KEPT]
        + [
            whole(packs, *tile_shape),
            whole(cols + tile_w, layers),
            whole(cols + tile_w, layers),
            whole(nd * nc * CHUNK, LANES),
        ],
        [vmem] * (len(odd) + len(first_part)),
        scratch=[pltpu.VMEM(span_shape(late[n], wide, layers), FLOAT) for n in LATE_SCRATCH]
        + [pltpu.VMEM((nd * nc * CHUNK, LANES), FLOAT), pltpu.SemaphoreType.DMA],
        out_spaces=[vmem] * (len(pairings(nc)) + len(LATE_KEPT) + 3) + [pltpu.HBM],
    )(*odd, *first_part)
    n_side = len(pairings(nc))
    sides, late_arrays = late_arrays[:n_side], late_arrays[n_side:]
    *late_arrays, fix, near, far, chunks = late_arrays
    early_arrays = dict(zip(EARLY, first_part))
    late_arrays = dict(zip(LATE_KEPT, late_arrays))
    kept = [d[n] for d in (early_arrays, late_arrays) for n in KEPT]

    chunks = chunks.reshape(nd * nc, CHUNK, 1, LANES)
    arrived = lax.all_to_all(chunks, ("cross", "down"), 0, 0, tiled=True).reshape(nd * nc * CHUNK, LANES)
    far = lax.ppermute(far, axes, pairs_of(nd, nc, True, None))
    near = lax.ppermute(near, axes, pairs_of(nd, nc, False, None))
    sides = [
        lax.ppermute(m, axes, pairs_of(nd, nc, None, cross_kind))
        for m, cross_kind in zip(sides, pairings(nc))
    ]
    base = call(
        functools.partial(base_kernel, nd, nc, tiles),
        block,
        [vmem] * (5 + n_side + len(kept)),
        scratch=[
            pltpu.VMEM((rows + 4, wide, layers), FLOAT),
            pltpu.VMEM((rows + 2, wide, layers), FLOAT),
        ],
    )(near, far, fix, early_arrays["pres"], late_arrays["pres"], *sides, *kept)
    responses = call(
        functools.partial(response_kernel, nd, nc, rows),
        [
            block,
            whole(2, cols, layers),
            whole(2, cols, layers),
            whole(rows, 2 * STRIP, layers),
            whole(2, 2 * STRIP, layers),
        ],
        [vmem] * len(kept),
    )(*kept)
    return call(
        functools.partial(last_kernel, nd, nc),
        block,
        [vmem] * (2 + len(responses)),
        scratch=[
            pltpu.VMEM((rows, cols, layers), FLOAT),
            pltpu.VMEM((nc, nd, LANES), FLOAT),
            pltpu.SemaphoreType.DMA((rows // 2,)),
        ],
        out_spaces=pltpu.HBM,
    )(arrived, base, *responses)


def solution(mesh):
    return jax.shard_map(
        functools.partial(body, mesh.shape["down"], mesh.shape["cross"]),
        mesh=mesh,
        in_specs=(
            P("down", "cross", None),
            P("down", "cross", None),
            P("down", "cross", None),
            P("down", "cross"),
        ),
        out_specs=P("down", "cross", None),
        check_vma=False,
    )
```
